32 devices in a mesh: seq: 2 (over core), shard: 16 (over z, y, x).
Axes of the slice: x: 2, y: 2, z: 4, core: 2. Of those that a mesh axis runs over, the one named last changes fastest.
Arguments:
- tokens: bfloat16 [16, 8, 392, 512], P('shard', 'seq'), may hold values from -26 to 26
- norm1_gain: bfloat16 [512], P('shard'), may hold values from 0.099609375 to 1.8984375
- norm1_bias: bfloat16 [512], P('shard'), may hold values from -1.75 to 1.75
- qkv_weight: bfloat16 [512, 1536], P('shard'), may hold values from -0.25 to 0.25
- qv_bias: bfloat16 [1024], P('shard'), may hold values from -1.75 to 1.75
- position_table: bfloat16 [2535, 16], replicated, may hold values from -4 to 4
- proj_weight: bfloat16 [512, 512], P(None, 'shard'), may hold values from -1.5 to 1.5
- proj_bias: bfloat16 [512], P('shard'), may hold values from -1.75 to 1.75
- norm2_gain: bfloat16 [512], P('shard'), may hold values from 0.099609375 to 1.8984375
- norm2_bias: bfloat16 [512], P('shard'), may hold values from -1.75 to 1.75
- fc1_weight: bfloat16 [512, 2048], P('shard'), may hold values from -0.25 to 0.25
- fc1_bias: bfloat16 [2048], P('shard'), may hold values from -3 to 3
- fc2_weight: bfloat16 [2048, 512], P(None, 'shard'), may hold values from -0.125 to 0.125
- fc2_bias: bfloat16 [512], P('shard'), may hold values from -1.75 to 1.75
- rel_index: int32 [392, 392], replicated, may hold values from 0 to 2534, as said below
- region_ids: int32 [8, 392], P('seq'), may hold values from 0 to 26, as said below
- cotangent: bfloat16 [16, 8, 392, 512], P('shard', 'seq'), may hold values from -8 to 8
Outputs:
- block_out: bfloat16 [16, 8, 392, 512], P('shard', 'seq')
- input_grad: float32 [16, 8, 392, 512], P('shard', 'seq')
- norm1_gain_grad: float32 [512], P('shard')
- norm1_bias_grad: float32 [512], P('shard')
- qkv_weight_grad: float32 [512, 1536], P('shard')
- qv_bias_grad: float32 [1024], P('shard')
- position_table_grad: float32 [2535, 16], replicated
- proj_weight_grad: float32 [512, 512], P(None, 'shard')
- proj_bias_grad: float32 [512], P('shard')
- norm2_gain_grad: float32 [512], P('shard')
- norm2_bias_grad: float32 [512], P('shard')
- fc1_weight_grad: float32 [512, 2048], P('shard')
- fc1_bias_grad: float32 [2048], P('shard')
- fc2_weight_grad: float32 [2048, 512], P(None, 'shard')
- fc2_bias_grad: float32 [512], P('shard')
The draws below stay inside these ranges and needn't reach their ends.
Inputs may be any that keep to these rules, and one draw needn't show every extreme that they name: `rel_index`: each relative offset of the two positions of a pair has a row of its own, relabelled anew in each draw; every row is used. `region_ids`: 9 a + 3 b + c with labels a, b, c that never fall along time, height and width of the shifted grid, each of the labels 0, 1, 2 occurring along each.
All inputs are finite; a program needn't handle non-finite values.
Results may differ from the reference program's by a relative error of at most 0.02.
Values may be sent and summed in bfloat16 or wider, within the bound.
No kernel may reach another device: no remote copies, remote signals or barrier semaphores. Data moves between devices by JAX's collectives and lax.ppermute only.
A program may use at most 448 MiB of HBM per device.

```python
import jax
import jax.numpy as jnp
from jax import lax

HEADS = 16
HEAD_DIM = 32
D = 512
FF = 2048
WT = 8
WH = 7
WW = 7
WINDOWS = 8
SHIFT_T = 4
SHIFT_H = 3
SHIFT_W = 3
WIN_TOK = 392
TABLE_ROWS = 2535
CLIPS = 16


def draw_tokens(key, part):
    key = jax.random.fold_in(key, 3)
    column_key, row_key, base_key = jax.random.split(key, 3)
    full_shape = (CLIPS, WINDOWS, WIN_TOK, D)
    column_scale = jnp.exp(jax.random.uniform(column_key, (D,), jnp.float32, -1.15, 1.15))
    row_scale = jnp.exp(jax.random.uniform(row_key, (CLIPS, WINDOWS, WIN_TOK, 1), jnp.float32, -0.7, 0.7))
    base_values = jnp.clip(jax.random.normal(base_key, full_shape, jnp.float32), -4.0, 4.0)
    return (base_values * column_scale * row_scale).astype(jnp.bfloat16)


def draw_rel_index(key, part):
    key = jax.random.fold_in(key, 7)
    places = jnp.arange(WIN_TOK, dtype=jnp.int32)
    along_t = places // (WH * WW)
    along_h = places // WW % WH
    along_w = places % WW
    offset_t = along_t[:, None] - along_t[None, :] + WT - 1
    offset_h = along_h[:, None] - along_h[None, :] + WH - 1
    offset_w = along_w[:, None] - along_w[None, :] + WW - 1
    offsets = (offset_t * (2 * WH - 1) + offset_h) * (2 * WW - 1) + offset_w
    relabel = jax.random.permutation(key, TABLE_ROWS).astype(jnp.int32)
    return relabel[offsets]


def draw_region_ids(key, part):
    key = jax.random.fold_in(key, 5)
    cut_keys = jax.random.split(key, 6)
    labels = []
    for order, extent in enumerate((WT, WH, WW)):
        low_cut = jax.random.randint(cut_keys[2 * order], (), 1, extent + 1)
        high_cut = jax.random.randint(cut_keys[2 * order + 1], (), extent + 1, 2 * extent)
        places = jnp.arange(2 * extent, dtype=jnp.int32)
        labels.append((places >= low_cut).astype(jnp.int32) + (places >= high_cut).astype(jnp.int32))
    region_grid = 9 * labels[0][:, None, None] + 3 * labels[1][None, :, None] + labels[2][None, None, :]
    region_grid = region_grid.reshape(2, WT, 2, WH, 2, WW).transpose(0, 2, 4, 1, 3, 5)
    return region_grid.reshape(WINDOWS, WIN_TOK).astype(jnp.int32)


def strengthened(values, rng, source, target, shards_of, factor):
    owner, partner = [(jnp.arange(values.shape[axis_at]) // (values.shape[axis_at] // shards_of)).reshape([-1 if axis == axis_at else 1 for axis in range(values.ndim)]) for axis_at in (source, target)]
    chosen = jax.random.permutation(rng, shards_of)[partner]
    strong = (owner == chosen) | (owner == (partner + shards_of // 2) % shards_of)
    return jnp.where(strong, factor * values, values)


def shard_levels(key, shape, pieces, low, high):
    factor_of = 1.0
    for position, blocks in pieces:
        steps = jax.random.uniform(jax.random.fold_in(jax.random.fold_in(key, 6), position), (blocks,), jnp.float32, low / len(pieces), high / len(pieces))
        factor_of = factor_of * jnp.repeat(jnp.exp(steps), shape[position] // blocks).reshape((-1,) + (1,) * (len(shape) - 1 - position))
    return factor_of


def noise(rng, shape, scale, most, cuts=(), kind=jnp.bfloat16):
    level = shard_levels(rng, shape, cuts, -0.22, 0.18) if cuts else 1.0
    values = jax.random.normal(rng, shape, jnp.float32) * scale * level
    return jnp.minimum(jnp.maximum(values, -most), most).astype(kind)


def noise_with(stream_key, dims, scale, bound, shards, heavy, held_as=jnp.bfloat16):
    array = scale * jax.random.normal(stream_key, dims, jnp.float32)
    if shards:
        array = array * shard_levels(stream_key, dims, shards, -0.22, 0.18)
    return jnp.clip(strengthened(array, jax.random.fold_in(stream_key, 3), *heavy), -bound, bound).astype(held_as)


def setup_inputs(seed: int = 0) -> dict:
    streams_of = jax.random.split(jax.random.key(seed), 18)
    tokens = draw_tokens(jax.random.fold_in(streams_of[17], 71), 0)
    norm1_gain = jnp.clip(1.0 + 0.18 * jax.random.normal(streams_of[1], (D,), jnp.float32), 0.099609375, 1.8984375).astype(jnp.bfloat16)
    norm1_bias = noise(streams_of[2], (D,), 0.3, 1.75, ((0, 16),))
    qkv_weight = noise(streams_of[3], (D, 3 * D), D ** -0.5, 0.25, ((0, 16),))
    qv_bias = noise(streams_of[4], (2 * D,), 0.3, 1.75, ((0, 16),))
    position_table = noise(streams_of[5], (TABLE_ROWS, HEADS), 1.0, 4.0)
    proj_weight = noise(streams_of[6], (D, D), (D // 32) ** -0.5, 1.5, ((1, 16),))
    proj_bias = noise(streams_of[7], (D,), 0.3, 1.75, ((0, 16),))
    norm2_gain = jnp.clip(1.0 + 0.18 * jax.random.normal(streams_of[8], (D,), jnp.float32), 0.099609375, 1.8984375).astype(jnp.bfloat16)
    norm2_bias = noise(streams_of[9], (D,), 0.3, 1.75, ((0, 16),))
    fc1_weight = noise(streams_of[10], (D, FF), D ** -0.5, 0.25, ((0, 16),))
    fc1_bias = noise(streams_of[11], (FF,), 0.5, 3.0, ((0, 16),))
    fc2_weight = noise(streams_of[12], (FF, D), FF ** -0.5, 0.125, ((1, 16),))
    fc2_bias = noise(streams_of[13], (D,), 0.3, 1.75, ((0, 16),))
    rel_index = draw_rel_index(jax.random.fold_in(streams_of[17], 71), 0)
    region_ids = draw_region_ids(jax.random.fold_in(streams_of[17], 71), 0)
    cotangent = noise_with(streams_of[16], (CLIPS, WINDOWS, WIN_TOK, D), 1.0, 8.0, ((0, 16), (1, 2)), (0, 3, 16, 2.0))
    return {"tokens": tokens, "norm1_gain": norm1_gain, "norm1_bias": norm1_bias, "qkv_weight": qkv_weight, "qv_bias": qv_bias, "position_table": position_table, "proj_weight": proj_weight, "proj_bias": proj_bias, "norm2_gain": norm2_gain, "norm2_bias": norm2_bias, "fc1_weight": fc1_weight, "fc1_bias": fc1_bias, "fc2_weight": fc2_weight, "fc2_bias": fc2_bias, "rel_index": rel_index, "region_ids": region_ids, "cotangent": cotangent}


EPS = 1e-05
HIGH = lax.Precision.HIGHEST

@jax.custom_vjp
def low(v):
    return lax.optimization_barrier(v.astype(jnp.bfloat16)).astype(jnp.float32)

@jax.custom_vjp
def low_back(v):
    return v

def low_keep(v):
    return (low(v), None)

def low_pass(kept, grad):
    return (grad,)

def back_keep(v):
    return (v, None)

def back_low(kept, grad):
    return (low(grad),)
low.defvjp(low_keep, low_pass)
low_back.defvjp(back_keep, back_low)

def layer_norm(values, gain, offset):
    mean = lax.optimization_barrier(jnp.mean(values, axis=-1, keepdims=True))
    centred = values - mean
    variance = lax.optimization_barrier(jnp.mean(centred * centred, axis=-1, keepdims=True))
    return centred * lax.rsqrt(variance + EPS) * gain + offset

def gelu_exact(values):
    return 0.5 * values * (1.0 + lax.erf(values * 0.7071067811865476))

def to_grid(windows):
    chans = windows.shape[-1]
    parted = windows.reshape(2, 2, 2, WT, WH, WW, chans)
    return parted.transpose(0, 3, 1, 4, 2, 5, 6).reshape(2 * WT, 2 * WH, 2 * WW, chans)

def to_windows(grid_field):
    chans = grid_field.shape[-1]
    parted = grid_field.reshape(2, WT, 2, WH, 2, WW, chans)
    return parted.transpose(0, 2, 4, 1, 3, 5, 6).reshape(WINDOWS, WIN_TOK, chans)

def roll_windows(windows, direction):
    rolled = jnp.roll(to_grid(windows), (direction * SHIFT_T, direction * SHIFT_H, direction * SHIFT_W), (0, 1, 2))
    return to_windows(rolled)

def forward(clip, params, rel_index, region_ids):
    norm1_gain, norm1_bias, qkv_weight, qv_bias, position_table, proj_weight, proj_bias, norm2_gain, norm2_bias, fc1_weight, fc1_bias, fc2_weight, fc2_bias = params
    first = low_back(low(layer_norm(clip, norm1_gain, norm1_bias)))
    shifted = roll_windows(first, -1)
    qkv = jnp.dot(shifted.reshape(-1, D), qkv_weight, precision=HIGH)
    qkv = qkv + jnp.concatenate([qv_bias[:D], jnp.zeros((D,), jnp.float32), qv_bias[D:]])
    qkv = qkv.reshape(WINDOWS, WIN_TOK, 3, HEADS, HEAD_DIM)
    queries = low_back(low(qkv[:, :, 0]))
    key_rows = low_back(low(qkv[:, :, 1]))
    value_rows = low_back(low(qkv[:, :, 2]))
    scale_factor = HEAD_DIM ** (-0.5)
    scores = jnp.einsum('wihd,wjhd->whij', queries, key_rows, precision=HIGH) * scale_factor
    pos_bias = jnp.take(position_table, rel_index, axis=0).transpose(2, 0, 1)
    same_region = region_ids[:, :, None] == region_ids[:, None, :]
    scores = jnp.where(same_region[:, None], scores + pos_bias[None], -1000000000.0)
    scores = low_back(scores)
    attn = low(jax.nn.softmax(scores, axis=-1))
    context = jnp.einsum('whij,wjhd->wihd', attn, value_rows, precision=HIGH).reshape(WINDOWS, WIN_TOK, D)
    context = low_back(low(context))
    context_back = roll_windows(context, 1)
    branch = jnp.dot(context_back.reshape(-1, D), proj_weight, precision=HIGH) + proj_bias
    branch = low_back(branch).reshape(clip.shape)
    mid = clip + branch
    second = low(layer_norm(mid, norm2_gain, norm2_bias))
    hidden = low_back(jnp.dot(second.reshape(-1, D), fc1_weight, precision=HIGH) + fc1_bias)
    act = low(gelu_exact(hidden))
    mlp = low_back(jnp.dot(act, fc2_weight, precision=HIGH) + fc2_bias)
    return mid + mlp.reshape(clip.shape)

def reference(tokens, norm1_gain, norm1_bias, qkv_weight, qv_bias, position_table, proj_weight, proj_bias, norm2_gain, norm2_bias, fc1_weight, fc1_bias, fc2_weight, fc2_bias, rel_index, region_ids, cotangent):
    params = tuple((item.astype(jnp.float32) for item in (norm1_gain, norm1_bias, qkv_weight, qv_bias, position_table, proj_weight, proj_bias, norm2_gain, norm2_bias, fc1_weight, fc1_bias, fc2_weight, fc2_bias)))

    def one_clip(totals, inputs):
        clip, clip_grad = inputs

        def run(clip_in, *weights):
            return forward(clip_in, weights, rel_index, region_ids)
        result, pull = jax.vjp(run, clip.astype(jnp.float32), *params)
        grads = pull(clip_grad.astype(jnp.float32))
        totals = tuple((left + right for left, right in zip(totals, grads[1:])))
        return (totals, (result.astype(jnp.bfloat16), grads[0]))
    start = tuple((jnp.zeros_like(item) for item in params))
    totals, (block_out, input_grad) = lax.scan(one_clip, start, (tokens, cotangent))
    return (block_out, input_grad, totals[0], totals[1], totals[2], totals[3], totals[4], totals[5], totals[6], totals[7], totals[8], totals[9], totals[10], totals[11], totals[12])
```

```python
import jax
import jax.numpy as jnp
import numpy as np
from jax import lax
from jax.experimental import pallas as pl
from jax.experimental.pallas import tpu as pltpu
from jax.sharding import PartitionSpec as P

HEADS = 16
HEAD_DIM = 32
WT = 8
WH = 7
WW = 7
WIN_TOK = WT * WH * WW
EPS = 1e-05

BF=jnp.bfloat16; F32=jnp.float32
LOG2E=1.4426950408889634; LN2=0.6931471805599453
SCALE=HEAD_DIM**-0.5
BIG=-(2.0**30)
GROUP=4
VM=56*1024*1024

def nt(a,b): return lax.dot_general(a,b,(((1,),(1,)),((),())),preferred_element_type=F32)
def nn(a,b): return jnp.dot(a,b,preferred_element_type=F32)

def placed(block, at, rows):
    parts=[]
    if at: parts.append(jnp.zeros((at,block.shape[1]),block.dtype))
    parts.append(block)
    if rows-at-block.shape[0]: parts.append(jnp.zeros((rows-at-block.shape[0],block.shape[1]),block.dtype))
    return jnp.concatenate(parts,axis=0)

def attend_kernel(q_ref,k_ref,v_ref,bias_ref,mq_ref,mk_ref,ctx_ref,e_ref,r_ref):
    lhs=jnp.concatenate([k_ref[0],mk_ref[0]],axis=1)
    ones=jnp.ones((16,q_ref.shape[2]),BF)
    for h in range(GROUP):
        rows=slice(h*HEAD_DIM,(h+1)*HEAD_DIM)
        rhs=jnp.concatenate([placed(q_ref[0,rows,:],h*HEAD_DIM,GROUP*HEAD_DIM),placed(mq_ref[0],0,128)],axis=0)
        s=nn(lhs,rhs)+bias_ref[h]
        m=jnp.max(s,axis=0,keepdims=True)
        e=jnp.exp2(s-m).astype(BF)
        e_ref[0,h]=e
        c=nn(jnp.concatenate([v_ref[0,rows,:],ones],axis=0),e)
        r=1.0/c[HEAD_DIM:HEAD_DIM+1]
        ctx_ref[0,rows,:]=(c[:HEAD_DIM]*r).astype(BF)
        r_ref[0,0,h:h+1,:]=r

def attend(qT,k,vT,bias,mq,mk):
    nw,width,n=qT.shape
    ng=width//128
    return pl.pallas_call(
        attend_kernel,
        grid=(ng,nw),
        in_specs=[
            pl.BlockSpec((1,128,n),lambda g,w:(w,g,0)),
            pl.BlockSpec((1,n,128),lambda g,w:(w,0,g)),
            pl.BlockSpec((1,128,n),lambda g,w:(w,g,0)),
            pl.BlockSpec((GROUP,n,n),lambda g,w:(g,0,0)),
            pl.BlockSpec((1,32,n),lambda g,w:(w,0,0)),
            pl.BlockSpec((1,n,128),lambda g,w:(w,0,0)),
        ],
        out_specs=[
            pl.BlockSpec((1,128,n),lambda g,w:(w,g,0)),
            pl.BlockSpec((1,GROUP,n,n),lambda g,w:(w,g,0,0)),
            pl.BlockSpec((1,1,GROUP,n),lambda g,w:(w,g,0,0)),
        ],
        out_shape=[
            jax.ShapeDtypeStruct((nw,width,n),BF),
            jax.ShapeDtypeStruct((nw,ng*GROUP,n,n),BF),
            jax.ShapeDtypeStruct((nw,ng,GROUP,n),F32),
        ],
        compiler_params=pltpu.CompilerParams(vmem_limit_bytes=VM),
        name="attend",
    )(qT,k,vT,bias,mq,mk)

SPREAD=768
FLAT=1408
WIDE=2816

def spread_ones():
    n=WT*WH*WW
    tok=np.arange(n); c=tok//(WW*WT); e=tok//WT%WW; a=tok%WT
    out=np.zeros((n,SPREAD),np.float32); out[tok,c*104+e*8+a]=1
    return out

def lane16(mirror):
    out=np.zeros((128,256),np.float32)
    for u in range(16):
        for a in range(8):
            out[u*8+a,u*16+(7-a if mirror else a)]=1
    return out

def back_kernel(e_ref,k_ref,v_ref,q_ref,g_ref,ctx_ref,r_ref,sp_ref,l16_ref,dq_ref,dk_ref,dv_ref,tab_ref,tot,acc):
    w=pl.program_id(1); nw=pl.num_programs(1)
    n=q_ref.shape[2]
    dv=jnp.zeros((n,128),F32); dk=jnp.zeros((n,128),F32)
    @pl.when(w==0)
    def _():
        tot[...]=jnp.zeros_like(tot)
    for h in range(GROUP):
        rows=slice(h*HEAD_DIM,(h+1)*HEAD_DIM)
        go=g_ref[0,rows,:].astype(F32)*r_ref[0,0,h:h+1,:]
        inner=jnp.sum(go*ctx_ref[0,rows,:].astype(F32),axis=0,keepdims=True)
        rhs=placed(go.astype(BF),h*HEAD_DIM,128)
        e=e_ref[0,h]
        dp=nn(v_ref[0],rhs)
        ds=(e.astype(F32)*(dp-inner))
        dsl=ds.astype(BF)
        tot[h]+=ds
        dv+=nt(e,rhs)
        dk+=nt(dsl,placed(q_ref[0,rows,:],h*HEAD_DIM,128))
        dq_ref[0,rows,:]=(nn(k_ref[0,rows,:],dsl)*SCALE).astype(BF)
    dv_ref[0]=dv.astype(BF)
    dk_ref[0]=(dk*LN2).astype(BF)
    @pl.when(w==nw-1)
    def _():
        for h in range(GROUP):
            x=nn(tot[h].astype(BF),sp_ref[...])
            full=jnp.zeros((8,FLAT),F32)
            for d in range(WH):
                part=jnp.zeros((8,SPREAD),F32)
                for f in range(WW):
                    j=(d*WW+f)*8
                    part=part+pltpu.roll(x[j:j+8,:],8*(WW-1-f),1) if f<WW-1 else part+x[j:j+8,:]
                wide=jnp.concatenate([part,jnp.zeros((8,FLAT-SPREAD),F32)],axis=1)
                full=full+(pltpu.roll(wide,104*(WH-1-d),1) if d<WH-1 else wide)
            acc[h*8:(h+1)*8,:]=full
        a=acc[...]
        hi=a.astype(BF); lo=(a-hi.astype(F32)).astype(BF)
        wide=[]
        for t in range(FLAT//128):
            c=slice(t*128,(t+1)*128)
            wide.append(nn(hi[:,c],l16_ref[...])+nn(lo[:,c],l16_ref[...]))
        y=jnp.concatenate(wide,axis=1)
        for h in range(GROUP):
            z=pltpu.roll(y[h*8:(h+1)*8,:],0,1,stride=1,stride_axis=0)
            tab_ref[0,h:h+1,:]=jnp.sum(z,axis=0,keepdims=True)

def attend_back(e,kT,v,qT,gT,ctxT,r,sp,l16):
    nw,width,n=qT.shape
    ng=width//128
    feat=pl.BlockSpec((1,128,n),lambda g,w:(w,g,0))
    tok=pl.BlockSpec((1,n,128),lambda g,w:(w,0,g))
    return pl.pallas_call(
        back_kernel,
        grid=(ng,nw),
        in_specs=[
            pl.BlockSpec((1,GROUP,n,n),lambda g,w:(w,g,0,0)),
            feat,tok,feat,feat,feat,
            pl.BlockSpec((1,1,GROUP,n),lambda g,w:(w,g,0,0)),
            pl.BlockSpec(sp.shape,lambda g,w:(0,0)),
            pl.BlockSpec(l16.shape,lambda g,w:(0,0)),
        ],
        out_specs=[feat,tok,tok,pl.BlockSpec((1,GROUP,WIDE),lambda g,w:(g,0,0))],
        out_shape=[
            jax.ShapeDtypeStruct((nw,width,n),BF),
            jax.ShapeDtypeStruct((nw,n,width),BF),
            jax.ShapeDtypeStruct((nw,n,width),BF),
            jax.ShapeDtypeStruct((ng,GROUP,WIDE),F32),
        ],
        scratch_shapes=[pltpu.VMEM((GROUP,n,n),F32),pltpu.VMEM((GROUP*8,FLAT),F32)],
        compiler_params=pltpu.CompilerParams(vmem_limit_bytes=VM),
        name="attend_back",
    )(e,kT,v,qT,gT,ctxT,r,sp,l16)

def lane_maps(mirror):
    lane=np.arange(WIDE); pq=lane//16; o=lane%16
    p=pq//13; q=pq%13
    ok=(pq<169)&(o<15)
    if mirror: o=14-o
    A=o>=7; b=np.where(A,14-o,7-o); C=p>=6; d=np.where(C,12-p,6-p); E=q>=6; f=np.where(E,12-q,6-q)
    col=(b*WH+d)*WW+f
    corner=A*4+C*2+E*1
    return np.where(ok,col,-1).astype(np.int32), np.where(ok,corner,-1).astype(np.int32)

CORNER_ROWS=[(a*WH+c)*WW+e for a in (0,WT-1) for c in (0,WH-1) for e in (0,WW-1)]
TROWS=2560

def pick_kernel(rel_ref,maps_ref,table_ref,lab_ref,val_ref):
    rel=rel_ref[...]
    hi=(rel>>6).astype(F32).astype(BF); lo=(rel&63).astype(F32).astype(BF)
    both=jnp.concatenate([hi,lo],axis=0)
    n=rel.shape[1]
    corners=lax.broadcasted_iota(jnp.int32,(8,256),0)
    rows=lax.broadcasted_iota(jnp.int32,(n,256),0)
    trow=lax.broadcasted_iota(jnp.int32,(TROWS,256),0)
    for t in range(WIDE//256):
        c=slice(t*256,(t+1)*256)
        for version in range(2):
            col=maps_ref[2*version:2*version+1,c]; cor=maps_ref[2*version+1:2*version+2,c]
            m=jnp.where(rows==col,1.0,0.0).astype(BF)
            y=nn(both,m)
            full=y[:8]*64.0+y[8:]
            lab=jnp.sum(jnp.where(corners==cor,full,0.0),axis=0,keepdims=True)
            lab=jnp.where(cor>=0,lab,-1.0).astype(jnp.int32)
            lab_ref[version:version+1,c]=lab
            if version==0:
                hot=jnp.where(trow==lab,1.0,0.0).astype(BF)
                val_ref[:,c]=nn(table_ref[...],hot)

def pick(rel8,maps,tableT):
    return pl.pallas_call(
        pick_kernel,
        out_shape=[jax.ShapeDtypeStruct((2,WIDE),jnp.int32),jax.ShapeDtypeStruct((HEADS,WIDE),F32)],
        compiler_params=pltpu.CompilerParams(vmem_limit_bytes=VM),
        name="pick",
    )(rel8,maps,tableT)

def bias_kernel(val_ref,l8_ref,sp_ref,bias_ref,x_ref):
    base=jnp.broadcast_to(val_ref[0],(8,WIDE))
    z=pltpu.roll(base,WIDE-7,1,stride=1,stride_axis=0).astype(BF)
    narrow=jnp.concatenate([nn(z[:,t*256:(t+1)*256],l8_ref[...]) for t in range(FLAT//128)],axis=1)
    for d in range(WH):
        s=FLAT-104*(WH-1-d)
        wide=(pltpu.roll(narrow,s,1) if d<WH-1 else narrow)[:,:SPREAD]
        for f in range(WW):
            j=(d*WW+f)*8
            x_ref[j:j+8,:]=pltpu.roll(wide,SPREAD-8*(WW-1-f),1) if f<WW-1 else wide
    bias_ref[0]=nt(x_ref[...].astype(BF),sp_ref[...])*LOG2E

def bias_all(val,l8,sp):
    n=sp.shape[0]
    return pl.pallas_call(
        bias_kernel,
        grid=(HEADS,),
        in_specs=[pl.BlockSpec((1,1,WIDE),lambda h:(h,0,0)),pl.BlockSpec(l8.shape,lambda h:(0,0)),pl.BlockSpec(sp.shape,lambda h:(0,0))],
        out_specs=pl.BlockSpec((1,n,n),lambda h:(h,0,0)),
        out_shape=jax.ShapeDtypeStruct((HEADS,n,n),F32),
        scratch_shapes=[pltpu.VMEM((n,SPREAD),F32)],
        compiler_params=pltpu.CompilerParams(vmem_limit_bytes=VM),
        name="position_bias",
    )(val.reshape(HEADS,1,WIDE),l8,sp)

def spill_kernel(lab_ref,g_ref,out_ref):
    g=g_ref[...]
    hi=g.astype(BF); r1=g-hi.astype(F32); mid=r1.astype(BF); lo=(r1-mid.astype(F32)).astype(BF)
    three=jnp.concatenate([hi,mid,lo],axis=0)
    trow=lax.broadcasted_iota(jnp.int32,(TROWS,256),0)
    tot=jnp.zeros((48,TROWS),F32)
    for t in range(WIDE//256):
        c=slice(t*256,(t+1)*256)
        hot=jnp.where(trow==lab_ref[1:2,c],1.0,0.0).astype(BF)
        tot=tot+nt(three[:,c],hot)
    out_ref[...]=tot[:16]+tot[16:32]+tot[32:]

def spill(lab,g):
    return pl.pallas_call(
        spill_kernel,
        out_shape=jax.ShapeDtypeStruct((HEADS,TROWS),F32),
        compiler_params=pltpu.CompilerParams(vmem_limit_bytes=VM),
        name="table_rows",
    )(lab,g)


def from_partner(shard, axis, stride):
    return lax.ppermute(shard, axis, [(i, i ^ 1 << stride) for i in range(lax.axis_size(axis))])


def norm_forward(values, gain, offset):
    mean = jnp.mean(values, axis=-1, keepdims=True)
    centred = values - mean
    variance = jnp.mean(centred * centred, axis=-1, keepdims=True)
    inverse = lax.rsqrt(variance + EPS)
    normed = centred * inverse
    return (normed * gain + offset, normed, inverse)


def norm_backward(out_grad, normed, inverse, gain):
    scaled = out_grad * gain
    inner = jnp.mean(scaled, axis=-1, keepdims=True)
    along = jnp.mean(scaled * normed, axis=-1, keepdims=True)
    return inverse * (scaled - inner - normed * along)


def gelu_exact(values):
    return 0.5 * values * (1.0 + lax.erf(values * 0.7071067811865476))


def gelu_slope(values):
    density = jnp.exp(-0.5 * values * values) * 0.3989422804014327
    return 0.5 * (1.0 + lax.erf(values * 0.7071067811865476)) + values * density


def to_block(windows, local_count):
    clip_count, chans = (windows.shape[0], windows.shape[-1])
    parted = windows.reshape(
        clip_count, local_count[0], local_count[1], local_count[2], WT, WH, WW, chans
    )
    parted = parted.transpose(0, 1, 4, 2, 5, 3, 6, 7)
    return parted.reshape(
        clip_count, local_count[0] * WT, local_count[1] * WH, local_count[2] * WW, chans
    )


def from_block(block, local_count):
    clip_count, chans = (block.shape[0], block.shape[-1])
    parted = block.reshape(
        clip_count, local_count[0], WT, local_count[1], WH, local_count[2], WW, chans
    )
    parted = parted.transpose(0, 1, 3, 5, 2, 4, 6, 7)
    return parted.reshape(clip_count, -1, WT * WH * WW, chans)


def roll_ahead(windows, local_count, bit_list):
    block = to_block(windows, local_count)
    for grid_dim, amount, bit_pos in (
        (1, WT // 2, bit_list[0]),
        (2, WH // 2, bit_list[1]),
        (3, WW // 2, bit_list[2]),
    ):
        if bit_pos < 0:
            block = jnp.roll(block, -amount, axis=grid_dim)
        else:
            front = lax.slice_in_dim(block, 0, amount, axis=grid_dim)
            arrived = from_partner(front, "seq", bit_pos)
            rest = lax.slice_in_dim(block, amount, block.shape[grid_dim], axis=grid_dim)
            block = jnp.concatenate([rest, arrived], axis=grid_dim)
    return from_block(block, local_count)


def roll_behind(windows, local_count, bit_list):
    block = to_block(windows, local_count)
    for grid_dim, amount, bit_pos in (
        (1, WT // 2, bit_list[0]),
        (2, WH // 2, bit_list[1]),
        (3, WW // 2, bit_list[2]),
    ):
        if bit_pos < 0:
            block = jnp.roll(block, amount, axis=grid_dim)
        else:
            extent = block.shape[grid_dim]
            trailing = lax.slice_in_dim(block, extent - amount, extent, axis=grid_dim)
            arrived = from_partner(trailing, "seq", bit_pos)
            rest = lax.slice_in_dim(block, 0, extent - amount, axis=grid_dim)
            block = jnp.concatenate([arrived, rest], axis=grid_dim)
    return from_block(block, local_count)


HALF = 200


def hwt_order():
    place = np.arange(WIN_TOK)
    return (place % WT * WH + place // (WW * WT)) * WW + place // WT % WW


def roll_sources():
    own = np.full((4, WIN_TOK), -1)
    arrived = np.full((4, WIN_TOK), -1)
    for win in range(4):
        for place in range(WIN_TOK):
            t, h, w = place % WT, place // (WW * WT), place // WT % WW
            h = (win // 2 * WH + h + WH // 2) % (2 * WH)
            w = (win % 2 * WW + w + WW // 2) % (2 * WW)
            source = h // WH * 2 + w // WW
            inside = h % WH * WW + w % WW
            if t < WT // 2:
                own[win, place] = source * WIN_TOK + (t + WT // 2) * WH * WW + inside
            else:
                arrived[win, place] = source * HALF + (t - WT // 2) * WH * WW + inside
    return own.reshape(-1), arrived.reshape(-1)


def one_hot_rows(source, columns):
    return (jnp.asarray(source, jnp.int32)[:, None] == jnp.arange(columns, dtype=jnp.int32)[None, :]).astype(BF)


def swap_cores(part):
    return lax.ppermute(part, "seq", [(0, 1), (1, 0)])


def enter(windows, plan):
    clips, wins, toks, width = windows.shape
    if plan["levels"] == 1:
        arrived = swap_cores(windows[:, :, :HALF]).reshape(clips, wins * HALF, width)
        flat = windows.reshape(clips, wins * toks, width)
        own_hot, arrived_hot = plan["hots"]
        out = [
            jnp.dot(own_hot, flat[i], preferred_element_type=F32) + jnp.dot(arrived_hot, arrived[i], preferred_element_type=F32)
            for i in range(clips)
        ]
        return jnp.stack(out).astype(BF).reshape(clips * wins, toks, width)
    rolled = roll_ahead(windows, plan["local"], plan["bits"])
    rolled = rolled.reshape(clips * wins, WT, WH * WW, width).transpose(0, 2, 1, 3)
    return rolled.reshape(clips * wins, toks, width)


def leave(windows, plan, clips):
    count, toks, width = windows.shape
    wins = count // clips
    if plan["levels"] == 1:
        flat = windows.reshape(clips, wins * toks, width)
        own_hot, arrived_hot = plan["hots"]
        sent = jnp.stack([nt_first(arrived_hot, flat[i]) for i in range(clips)]).astype(BF)
        got = swap_cores(sent).reshape(clips, wins, HALF, width)
        kept = jnp.stack([nt_first(own_hot, flat[i]) for i in range(clips)]).astype(BF)
        kept = kept.reshape(clips, wins, toks, width)
        return kept + jnp.pad(got, ((0, 0), (0, 0), (0, toks - HALF), (0, 0)))
    rows = windows.reshape(count, WH * WW, WT, width).transpose(0, 2, 1, 3)
    return roll_behind(rows.reshape(clips, wins, toks, width), plan["local"], plan["bits"])


def nt_first(hot, rows):
    return lax.dot_general(hot, rows, (((0,), (0,)), ((), ())), preferred_element_type=F32)


def body(
    tokens, norm1_gain, norm1_bias, qkv_weight, qv_bias, position_table, proj_weight, proj_bias, norm2_gain,
    norm2_bias, fc1_weight, fc1_bias, fc2_weight, fc2_bias, rel_index, region_ids, cotangent,
):
    levels = lax.axis_size("seq").bit_length() - 1
    own_rows, arrived_rows = roll_sources()
    plan = {
        "levels": levels,
        "local": [1 if levels > level_pos else 2 for level_pos in range(3)],
        "bits": [levels - 1 - level_pos for level_pos in range(3)],
        "hots": (one_hot_rows(own_rows, 4 * WIN_TOK), one_hot_rows(arrived_rows, 4 * HALF)),
    }
    clips, wins, toks, width = tokens.shape
    gather = lambda part, axis: lax.all_gather(part, "shard", axis=axis, tiled=True)
    vectors = jnp.concatenate([norm1_gain, norm1_bias, qv_bias, proj_bias, norm2_gain, norm2_bias, fc1_bias, fc2_bias])
    vectors = lax.all_gather(vectors, "shard", axis=0, tiled=False).astype(F32)
    cuts = np.cumsum([part.shape[0] for part in (norm1_gain, norm1_bias, qv_bias, proj_bias, norm2_gain, norm2_bias, fc1_bias)])
    gain_one, bias_one, qv_full, b_proj, gain_two, bias_two, b_fc1, b_fc2 = [
        part.reshape(-1) for part in jnp.split(vectors, cuts, axis=1)
    ]
    w_qkv, w_proj, w_fc1, w_fc2 = gather(qkv_weight, 0), gather(proj_weight, 1), gather(fc1_weight, 0), gather(fc2_weight, 1)

    spread = jnp.asarray(spread_ones(), BF)
    wide8 = jnp.asarray(lane16(False).T, BF)
    wide16 = jnp.asarray(lane16(True), BF)
    maps = jnp.asarray(np.stack(lane_maps(False) + lane_maps(True)))
    rel8 = jnp.concatenate([rel_index[row : row + 1] for row in CORNER_ROWS], axis=0)
    table_rows = jnp.pad(position_table.T, ((0, 0), (0, TROWS - position_table.shape[0])))
    labels, values = pick(rel8, maps, table_rows)
    bias = bias_all(values, wide8, spread)

    region = region_ids[:, hwt_order()]
    region = jnp.broadcast_to(region[None], (clips, wins, toks)).reshape(-1, toks)
    mask_keys = (region[:, :, None] == jnp.arange(128)).astype(BF)
    mask_queries = jnp.where(region[:, None, :] == jnp.arange(32)[:, None], 0.0, BIG).astype(BF)

    rows_in = enter(tokens, plan).astype(F32)
    out_grad = enter(cotangent, plan)
    first, normed_one, inverse_one = norm_forward(rows_in, gain_one, bias_one)
    first = first.astype(BF)
    feature = jnp.einsum("de,wnd->wen", w_qkv, first, preferred_element_type=F32)
    q_t = ((feature[:, :width] + qv_full[:width, None]) * (SCALE * LOG2E)).astype(BF)
    k_t = feature[:, width : 2 * width].astype(BF)
    v_t = (feature[:, 2 * width :] + qv_full[width:, None]).astype(BF)
    token_k = jnp.einsum("wnd,de->wne", first, w_qkv[:, width : 2 * width], preferred_element_type=F32).astype(BF)
    token_v = jnp.einsum("wnd,de->wne", first, w_qkv[:, 2 * width :], preferred_element_type=F32)
    token_v = (token_v + qv_full[width:]).astype(BF)

    context_t, expo, inverse_sum = attend(q_t, token_k, v_t, bias, mask_queries, mask_keys)

    branch = jnp.einsum("wdn,de->wne", context_t, w_proj, preferred_element_type=F32) + b_proj
    mid = rows_in + branch
    second, normed_two, inverse_two = norm_forward(mid, gain_two, bias_two)
    second = second.astype(BF)
    hidden = jnp.einsum("wnd,df->wnf", second, w_fc1, preferred_element_type=F32) + b_fc1
    act = gelu_exact(hidden).astype(BF)
    mlp = jnp.einsum("wnf,fd->wnd", act, w_fc2, preferred_element_type=F32) + b_fc2
    block_out = leave((mid + mlp).astype(BF), plan, clips)

    fc2_grad = jnp.einsum("wnf,wnd->fd", act, out_grad, preferred_element_type=F32)
    fc2_bias_grad = jnp.sum(out_grad.astype(F32), axis=(0, 1))
    act_grad = jnp.einsum("wnd,fd->wnf", out_grad, w_fc2, preferred_element_type=F32)
    hidden_grad = (act_grad * gelu_slope(hidden)).astype(BF)
    fc1_grad = jnp.einsum("wnd,wnf->df", second, hidden_grad, preferred_element_type=F32)
    fc1_bias_grad = jnp.sum(hidden_grad.astype(F32), axis=(0, 1))
    second_grad = jnp.einsum("wnf,df->wnd", hidden_grad, w_fc1, preferred_element_type=F32)
    mid_grad = out_grad.astype(F32) + norm_backward(second_grad, normed_two, inverse_two, gain_two)
    norm2_gain_grad = jnp.sum(second_grad * normed_two, axis=(0, 1))
    norm2_bias_grad = jnp.sum(second_grad, axis=(0, 1))
    branch_grad = mid_grad.astype(BF)
    proj_grad = jnp.einsum("wdn,wne->de", context_t, branch_grad, preferred_element_type=F32)
    proj_bias_grad = jnp.sum(branch_grad.astype(F32), axis=(0, 1))
    context_grad_t = jnp.einsum("wne,de->wdn", branch_grad, w_proj, preferred_element_type=F32).astype(BF)

    dq_t, dk, dv, offsets = attend_back(expo, k_t, token_v, q_t, context_grad_t, context_t, inverse_sum, spread, wide16)

    wgrad_q = jnp.einsum("wnd,wen->de", first, dq_t, preferred_element_type=F32)
    wgrad_k = jnp.einsum("wnd,wne->de", first, dk, preferred_element_type=F32)
    wgrad_v = jnp.einsum("wnd,wne->de", first, dv, preferred_element_type=F32)
    qkv_wgrad = jnp.concatenate([wgrad_q, wgrad_k, wgrad_v], axis=1)
    qv_grad = jnp.concatenate([jnp.sum(dq_t.astype(F32), axis=(0, 2)), jnp.sum(dv.astype(F32), axis=(0, 1))])
    first_grad = (
        jnp.einsum("wen,de->wnd", dq_t, w_qkv[:, :width], preferred_element_type=F32)
        + jnp.einsum("wne,de->wnd", dk, w_qkv[:, width : 2 * width], preferred_element_type=F32)
        + jnp.einsum("wne,de->wnd", dv, w_qkv[:, 2 * width :], preferred_element_type=F32)
    )
    norm1_gain_grad = jnp.sum(first_grad * normed_one, axis=(0, 1))
    norm1_bias_grad = jnp.sum(first_grad, axis=(0, 1))
    input_grad = mid_grad + norm_backward(first_grad, normed_one, inverse_one, gain_one)
    input_grad = leave(input_grad.astype(BF), plan, clips).astype(F32)

    table_grad = spill(labels, lax.psum(offsets.reshape(HEADS, WIDE), ("seq", "shard")))
    table_grad = table_grad[:, : position_table.shape[0]].T

    def owned(grad, axis):
        total = lax.psum(grad.astype(BF), "seq")
        return lax.psum_scatter(total, "shard", scatter_dimension=axis, tiled=True).astype(F32)

    shards = lax.axis_size("shard")
    small = [norm1_gain_grad, norm1_bias_grad, qv_grad, proj_bias_grad, norm2_gain_grad, norm2_bias_grad, fc1_bias_grad, fc2_bias_grad]
    small = jnp.concatenate([part.reshape(shards, -1) for part in small], axis=1)
    small = lax.psum(small, ("seq", "shard"))
    small = lax.dynamic_index_in_dim(small, lax.axis_index("shard"), 0, keepdims=False)
    own_g1, own_b1, own_qv, own_pb, own_g2, own_b2, own_f1b, own_f2b = jnp.split(small, cuts)
    return (
        block_out, input_grad, own_g1, own_b1, owned(qkv_wgrad, 0), own_qv, table_grad, owned(proj_grad, 1), own_pb,
        own_g2, own_b2, owned(fc1_grad, 0), own_f1b, owned(fc2_grad, 1), own_f2b,
    )


def solution(mesh):
    return jax.shard_map(
        body,
        mesh=mesh,
        in_specs=(
            P("shard", "seq", None, None),
            P("shard"),
            P("shard"),
            P("shard", None),
            P("shard"),
            P(),
            P(None, "shard"),
            P("shard"),
            P("shard"),
            P("shard"),
            P("shard", None),
            P("shard"),
            P(None, "shard"),
            P("shard"),
            P(),
            P("seq", None),
            P("shard", "seq", None, None),
        ),
        out_specs=(
            P("shard", "seq", None, None),
            P("shard", "seq", None, None),
            P("shard"),
            P("shard"),
            P("shard", None),
            P("shard"),
            P(),
            P(None, "shard"),
            P("shard"),
            P("shard"),
            P("shard"),
            P("shard", None),
            P("shard"),
            P(None, "shard"),
            P("shard"),
        ),
        check_vma=False,
    )
```

```python
import jax
import jax.numpy as jnp
import numpy as np
from jax import lax
from jax.experimental import pallas as pl
from jax.experimental.pallas import tpu as pltpu
from jax.sharding import PartitionSpec as P

HEADS = 16
HEAD_DIM = 32
WT = 8
WH = 7
WW = 7
WIN_TOK = WT * WH * WW
EPS = 1e-05

BF=jnp.bfloat16; F32=jnp.float32
LOG2E=1.4426950408889634; LN2=0.6931471805599453
SCALE=HEAD_DIM**-0.5
BIG=-(2.0**30)
GROUP=4
VM=56*1024*1024

def nt(a,b): return lax.dot_general(a,b,(((1,),(1,)),((),())),preferred_element_type=F32)
def nn(a,b): return jnp.dot(a,b,preferred_element_type=F32)

def placed(block, at, rows):
    parts=[]
    if at: parts.append(jnp.zeros((at,block.shape[1]),block.dtype))
    parts.append(block)
    if rows-at-block.shape[0]: parts.append(jnp.zeros((rows-at-block.shape[0],block.shape[1]),block.dtype))
    return jnp.concatenate(parts,axis=0)

def attend_kernel(q_ref,k_ref,v_ref,bias_ref,mq_ref,mk_ref,ctx_ref,e_ref,r_ref):
    lhs=jnp.concatenate([k_ref[0],mk_ref[0]],axis=1)
    ones=jnp.ones((16,q_ref.shape[2]),BF)
    for h in range(GROUP):
        rows=slice(h*HEAD_DIM,(h+1)*HEAD_DIM)
        rhs=jnp.concatenate([placed(q_ref[0,rows,:],h*HEAD_DIM,GROUP*HEAD_DIM),placed(mq_ref[0],0,128)],axis=0)
        s=nn(lhs,rhs)+bias_ref[h]
        m=jnp.max(s,axis=0,keepdims=True)
        e=jnp.exp2(s-m).astype(BF)
        e_ref[0,h]=e
        c=nn(jnp.concatenate([v_ref[0,rows,:],ones],axis=0),e)
        r=1.0/c[HEAD_DIM:HEAD_DIM+1]
        ctx_ref[0,rows,:]=(c[:HEAD_DIM]*r).astype(BF)
        r_ref[0,0,h:h+1,:]=r

def attend(qT,k,vT,bias,mq,mk):
    nw,width,n=qT.shape
    ng=width//128
    return pl.pallas_call(
        attend_kernel,
        grid=(ng,nw),
        in_specs=[
            pl.BlockSpec((1,128,n),lambda g,w:(w,g,0)),
            pl.BlockSpec((1,n,128),lambda g,w:(w,0,g)),
            pl.BlockSpec((1,128,n),lambda g,w:(w,g,0)),
            pl.BlockSpec((GROUP,n,n),lambda g,w:(g,0,0)),
            pl.BlockSpec((1,32,n),lambda g,w:(w,0,0)),
            pl.BlockSpec((1,n,128),lambda g,w:(w,0,0)),
        ],
        out_specs=[
            pl.BlockSpec((1,128,n),lambda g,w:(w,g,0)),
            pl.BlockSpec((1,GROUP,n,n),lambda g,w:(w,g,0,0)),
            pl.BlockSpec((1,1,GROUP,n),lambda g,w:(w,g,0,0)),
        ],
        out_shape=[
            jax.ShapeDtypeStruct((nw,width,n),BF),
            jax.ShapeDtypeStruct((nw,ng*GROUP,n,n),BF),
            jax.ShapeDtypeStruct((nw,ng,GROUP,n),F32),
        ],
        compiler_params=pltpu.CompilerParams(vmem_limit_bytes=VM),
        name="attend",
    )(qT,k,vT,bias,mq,mk)

SPREAD=768
FLAT=1408
WIDE=2816

def spread_ones():
    n=WT*WH*WW
    tok=np.arange(n); c=tok//(WW*WT); e=tok//WT%WW; a=tok%WT
    out=np.zeros((n,SPREAD),np.float32); out[tok,c*104+e*8+a]=1
    return out

def lane16(mirror):
    out=np.zeros((128,256),np.float32)
    for u in range(16):
        for a in range(8):
            out[u*8+a,u*16+(7-a if mirror else a)]=1
    return out

def back_kernel(e_ref,k_ref,v_ref,q_ref,g_ref,ctx_ref,r_ref,sp_ref,l16_ref,dq_ref,dk_ref,dv_ref,tab_ref,tot,acc):
    w=pl.program_id(1); nw=pl.num_programs(1)
    n=q_ref.shape[2]
    dv=jnp.zeros((n,128),F32); dk=jnp.zeros((n,128),F32)
    @pl.when(w==0)
    def _():
        tot[...]=jnp.zeros_like(tot)
    for h in range(GROUP):
        rows=slice(h*HEAD_DIM,(h+1)*HEAD_DIM)
        go=g_ref[0,rows,:].astype(F32)*r_ref[0,0,h:h+1,:]
        inner=jnp.sum(go*ctx_ref[0,rows,:].astype(F32),axis=0,keepdims=True)
        rhs=placed(go.astype(BF),h*HEAD_DIM,128)
        e=e_ref[0,h]
        dp=nn(v_ref[0],rhs)
        ds=(e.astype(F32)*(dp-inner))
        dsl=ds.astype(BF)
        tot[h]+=ds
        dv+=nt(e,rhs)
        dk+=nt(dsl,placed(q_ref[0,rows,:],h*HEAD_DIM,128))
        dq_ref[0,rows,:]=(nn(k_ref[0,rows,:],dsl)*SCALE).astype(BF)
    dv_ref[0]=dv.astype(BF)
    dk_ref[0]=(dk*LN2).astype(BF)
    @pl.when(w==nw-1)
    def _():
        for h in range(GROUP):
            x=nn(tot[h].astype(BF),sp_ref[...])
            full=jnp.zeros((8,FLAT),F32)
            for d in range(WH):
                part=jnp.zeros((8,SPREAD),F32)
                for f in range(WW):
                    j=(d*WW+f)*8
                    part=part+pltpu.roll(x[j:j+8,:],8*(WW-1-f),1) if f<WW-1 else part+x[j:j+8,:]
                wide=jnp.concatenate([part,jnp.zeros((8,FLAT-SPREAD),F32)],axis=1)
                full=full+(pltpu.roll(wide,104*(WH-1-d),1) if d<WH-1 else wide)
            acc[h*8:(h+1)*8,:]=full
        a=acc[...]
        hi=a.astype(BF); lo=(a-hi.astype(F32)).astype(BF)
        wide=[]
        for t in range(FLAT//128):
            c=slice(t*128,(t+1)*128)
            wide.append(nn(hi[:,c],l16_ref[...])+nn(lo[:,c],l16_ref[...]))
        y=jnp.concatenate(wide,axis=1)
        for h in range(GROUP):
            z=pltpu.roll(y[h*8:(h+1)*8,:],0,1,stride=1,stride_axis=0)
            tab_ref[0,h:h+1,:]=jnp.sum(z,axis=0,keepdims=True)

def attend_back(e,kT,v,qT,gT,ctxT,r,sp,l16):
    nw,width,n=qT.shape
    ng=width//128
    feat=pl.BlockSpec((1,128,n),lambda g,w:(w,g,0))
    tok=pl.BlockSpec((1,n,128),lambda g,w:(w,0,g))
    return pl.pallas_call(
        back_kernel,
        grid=(ng,nw),
        in_specs=[
            pl.BlockSpec((1,GROUP,n,n),lambda g,w:(w,g,0,0)),
            feat,tok,feat,feat,feat,
            pl.BlockSpec((1,1,GROUP,n),lambda g,w:(w,g,0,0)),
            pl.BlockSpec(sp.shape,lambda g,w:(0,0)),
            pl.BlockSpec(l16.shape,lambda g,w:(0,0)),
        ],
        out_specs=[feat,tok,tok,pl.BlockSpec((1,GROUP,WIDE),lambda g,w:(g,0,0))],
        out_shape=[
            jax.ShapeDtypeStruct((nw,width,n),BF),
            jax.ShapeDtypeStruct((nw,n,width),BF),
            jax.ShapeDtypeStruct((nw,n,width),BF),
            jax.ShapeDtypeStruct((ng,GROUP,WIDE),F32),
        ],
        scratch_shapes=[pltpu.VMEM((GROUP,n,n),F32),pltpu.VMEM((GROUP*8,FLAT),F32)],
        compiler_params=pltpu.CompilerParams(vmem_limit_bytes=VM),
        name="attend_back",
    )(e,kT,v,qT,gT,ctxT,r,sp,l16)

def lane_maps(mirror):
    lane=np.arange(WIDE); pq=lane//16; o=lane%16
    p=pq//13; q=pq%13
    ok=(pq<169)&(o<15)
    if mirror: o=14-o
    A=o>=7; b=np.where(A,14-o,7-o); C=p>=6; d=np.where(C,12-p,6-p); E=q>=6; f=np.where(E,12-q,6-q)
    col=(b*WH+d)*WW+f
    corner=A*4+C*2+E*1
    return np.where(ok,col,-1).astype(np.int32), np.where(ok,corner,-1).astype(np.int32)

CORNER_ROWS=[(a*WH+c)*WW+e for a in (0,WT-1) for c in (0,WH-1) for e in (0,WW-1)]
TROWS=2560

def pick_kernel(rel_ref,maps_ref,table_ref,lab_ref,val_ref):
    rel=rel_ref[...]
    hi=(rel>>6).astype(F32).astype(BF); lo=(rel&63).astype(F32).astype(BF)
    both=jnp.concatenate([hi,lo],axis=0)
    n=rel.shape[1]
    corners=lax.broadcasted_iota(jnp.int32,(8,256),0)
    rows=lax.broadcasted_iota(jnp.int32,(n,256),0)
    trow=lax.broadcasted_iota(jnp.int32,(TROWS,256),0)
    for t in range(WIDE//256):
        c=slice(t*256,(t+1)*256)
        for version in range(2):
            col=maps_ref[2*version:2*version+1,c]; cor=maps_ref[2*version+1:2*version+2,c]
            m=jnp.where(rows==col,1.0,0.0).astype(BF)
            y=nn(both,m)
            full=y[:8]*64.0+y[8:]
            lab=jnp.sum(jnp.where(corners==cor,full,0.0),axis=0,keepdims=True)
            lab=jnp.where(cor>=0,lab,-1.0).astype(jnp.int32)
            lab_ref[version:version+1,c]=lab
            if version==0:
                hot=jnp.where(trow==lab,1.0,0.0).astype(BF)
                val_ref[:,c]=nn(table_ref[...],hot)

def pick(rel8,maps,tableT):
    return pl.pallas_call(
        pick_kernel,
        out_shape=[jax.ShapeDtypeStruct((2,WIDE),jnp.int32),jax.ShapeDtypeStruct((HEADS,WIDE),F32)],
        compiler_params=pltpu.CompilerParams(vmem_limit_bytes=VM),
        name="pick",
    )(rel8,maps,tableT)

def bias_kernel(val_ref,l8_ref,sp_ref,bias_ref,x_ref):
    base=jnp.broadcast_to(val_ref[0],(8,WIDE))
    z=pltpu.roll(base,WIDE-7,1,stride=1,stride_axis=0).astype(BF)
    narrow=jnp.concatenate([nn(z[:,t*256:(t+1)*256],l8_ref[...]) for t in range(FLAT//128)],axis=1)
    for d in range(WH):
        s=FLAT-104*(WH-1-d)
        wide=(pltpu.roll(narrow,s,1) if d<WH-1 else narrow)[:,:SPREAD]
        for f in range(WW):
            j=(d*WW+f)*8
            x_ref[j:j+8,:]=pltpu.roll(wide,SPREAD-8*(WW-1-f),1) if f<WW-1 else wide
    bias_ref[0]=nt(x_ref[...].astype(BF),sp_ref[...])*LOG2E

def bias_all(val,l8,sp):
    n=sp.shape[0]
    return pl.pallas_call(
        bias_kernel,
        grid=(HEADS,),
        in_specs=[pl.BlockSpec((1,1,WIDE),lambda h:(h,0,0)),pl.BlockSpec(l8.shape,lambda h:(0,0)),pl.BlockSpec(sp.shape,lambda h:(0,0))],
        out_specs=pl.BlockSpec((1,n,n),lambda h:(h,0,0)),
        out_shape=jax.ShapeDtypeStruct((HEADS,n,n),F32),
        scratch_shapes=[pltpu.VMEM((n,SPREAD),F32)],
        compiler_params=pltpu.CompilerParams(vmem_limit_bytes=VM),
        name="position_bias",
    )(val.reshape(HEADS,1,WIDE),l8,sp)

def spill_kernel(lab_ref,g_ref,out_ref):
    g=g_ref[...]
    hi=g.astype(BF); r1=g-hi.astype(F32); mid=r1.astype(BF); lo=(r1-mid.astype(F32)).astype(BF)
    three=jnp.concatenate([hi,mid,lo],axis=0)
    trow=lax.broadcasted_iota(jnp.int32,(TROWS,256),0)
    tot=jnp.zeros((48,TROWS),F32)
    for t in range(WIDE//256):
        c=slice(t*256,(t+1)*256)
        hot=jnp.where(trow==lab_ref[1:2,c],1.0,0.0).astype(BF)
        tot=tot+nt(three[:,c],hot)
    out_ref[...]=tot[:16]+tot[16:32]+tot[32:]

def spill(lab,g):
    return pl.pallas_call(
        spill_kernel,
        out_shape=jax.ShapeDtypeStruct((HEADS,TROWS),F32),
        compiler_params=pltpu.CompilerParams(vmem_limit_bytes=VM),
        name="table_rows",
    )(lab,g)


def from_partner(shard, axis, stride):
    return lax.ppermute(shard, axis, [(i, i ^ 1 << stride) for i in range(lax.axis_size(axis))])


def norm_forward(values, gain, offset):
    mean = jnp.mean(values, axis=-1, keepdims=True)
    centred = values - mean
    variance = jnp.mean(centred * centred, axis=-1, keepdims=True)
    inverse = lax.rsqrt(variance + EPS)
    normed = centred * inverse
    return (normed * gain + offset, normed, inverse)


def norm_backward(out_grad, normed, inverse, gain):
    scaled = out_grad * gain
    inner = jnp.mean(scaled, axis=-1, keepdims=True)
    along = jnp.mean(scaled * normed, axis=-1, keepdims=True)
    return inverse * (scaled - inner - normed * along)


def gelu_exact(values):
    return 0.5 * values * (1.0 + lax.erf(values * 0.7071067811865476))


def gelu_slope(values):
    density = jnp.exp(-0.5 * values * values) * 0.3989422804014327
    return 0.5 * (1.0 + lax.erf(values * 0.7071067811865476)) + values * density


def to_block(windows, local_count):
    clip_count, chans = (windows.shape[0], windows.shape[-1])
    parted = windows.reshape(
        clip_count, local_count[0], local_count[1], local_count[2], WT, WH, WW, chans
    )
    parted = parted.transpose(0, 1, 4, 2, 5, 3, 6, 7)
    return parted.reshape(
        clip_count, local_count[0] * WT, local_count[1] * WH, local_count[2] * WW, chans
    )


def from_block(block, local_count):
    clip_count, chans = (block.shape[0], block.shape[-1])
    parted = block.reshape(
        clip_count, local_count[0], WT, local_count[1], WH, local_count[2], WW, chans
    )
    parted = parted.transpose(0, 1, 3, 5, 2, 4, 6, 7)
    return parted.reshape(clip_count, -1, WT * WH * WW, chans)


def roll_ahead(windows, local_count, bit_list):
    block = to_block(windows, local_count)
    for grid_dim, amount, bit_pos in (
        (1, WT // 2, bit_list[0]),
        (2, WH // 2, bit_list[1]),
        (3, WW // 2, bit_list[2]),
    ):
        if bit_pos < 0:
            block = jnp.roll(block, -amount, axis=grid_dim)
        else:
            front = lax.slice_in_dim(block, 0, amount, axis=grid_dim)
            arrived = from_partner(front, "seq", bit_pos)
            rest = lax.slice_in_dim(block, amount, block.shape[grid_dim], axis=grid_dim)
            block = jnp.concatenate([rest, arrived], axis=grid_dim)
    return from_block(block, local_count)


def roll_behind(windows, local_count, bit_list):
    block = to_block(windows, local_count)
    for grid_dim, amount, bit_pos in (
        (1, WT // 2, bit_list[0]),
        (2, WH // 2, bit_list[1]),
        (3, WW // 2, bit_list[2]),
    ):
        if bit_pos < 0:
            block = jnp.roll(block, amount, axis=grid_dim)
        else:
            extent = block.shape[grid_dim]
            trailing = lax.slice_in_dim(block, extent - amount, extent, axis=grid_dim)
            arrived = from_partner(trailing, "seq", bit_pos)
            rest = lax.slice_in_dim(block, 0, extent - amount, axis=grid_dim)
            block = jnp.concatenate([arrived, rest], axis=grid_dim)
    return from_block(block, local_count)


HALF = 200


def hwt_order():
    place = np.arange(WIN_TOK)
    return (place % WT * WH + place // (WW * WT)) * WW + place // WT % WW


def roll_sources():
    own = np.full((4, WIN_TOK), -1)
    arrived = np.full((4, WIN_TOK), -1)
    for win in range(4):
        for place in range(WIN_TOK):
            t, h, w = place % WT, place // (WW * WT), place // WT % WW
            h = (win // 2 * WH + h + WH // 2) % (2 * WH)
            w = (win % 2 * WW + w + WW // 2) % (2 * WW)
            source = h // WH * 2 + w // WW
            inside = h % WH * WW + w % WW
            if t < WT // 2:
                own[win, place] = source * WIN_TOK + (t + WT // 2) * WH * WW + inside
            else:
                arrived[win, place] = source * HALF + (t - WT // 2) * WH * WW + inside
    return own.reshape(-1), arrived.reshape(-1)


def one_hot_rows(source, columns):
    return (jnp.asarray(source, jnp.int32)[:, None] == jnp.arange(columns, dtype=jnp.int32)[None, :]).astype(BF)


def swap_cores(part):
    return lax.ppermute(part, "seq", [(0, 1), (1, 0)])


def enter(windows, plan):
    clips, wins, toks, width = windows.shape
    if plan["levels"] == 1:
        arrived = swap_cores(windows[:, :, :HALF]).reshape(clips, wins * HALF, width)
        flat = windows.reshape(clips, wins * toks, width)
        own_hot, arrived_hot = plan["hots"]
        out = [
            jnp.dot(own_hot, flat[i], preferred_element_type=F32) + jnp.dot(arrived_hot, arrived[i], preferred_element_type=F32)
            for i in range(clips)
        ]
        return jnp.stack(out).astype(BF).reshape(clips * wins, toks, width)
    rolled = roll_ahead(windows, plan["local"], plan["bits"])
    rolled = rolled.reshape(clips * wins, WT, WH * WW, width).transpose(0, 2, 1, 3)
    return rolled.reshape(clips * wins, toks, width)


def leave(windows, plan, clips):
    count, toks, width = windows.shape
    wins = count // clips
    if plan["levels"] == 1:
        flat = windows.reshape(clips, wins * toks, width)
        own_hot, arrived_hot = plan["hots"]
        sent = jnp.stack([nt_first(arrived_hot, flat[i]) for i in range(clips)]).astype(BF)
        got = swap_cores(sent).reshape(clips, wins, HALF, width)
        kept = jnp.stack([nt_first(own_hot, flat[i]) for i in range(clips)]).astype(BF)
        kept = kept.reshape(clips, wins, toks, width)
        return kept + jnp.pad(got, ((0, 0), (0, 0), (0, toks - HALF), (0, 0)))
    rows = windows.reshape(count, WH * WW, WT, width).transpose(0, 2, 1, 3)
    return roll_behind(rows.reshape(clips, wins, toks, width), plan["local"], plan["bits"])


def nt_first(hot, rows):
    return lax.dot_general(hot, rows, (((0,), (0,)), ((), ())), preferred_element_type=F32)


def hop(part, flips):
    pairs = [(16 * c + s, 16 * c + (s ^ flips[c])) for c in range(2) for s in range(16)]
    return lax.ppermute(part, ("seq", "shard"), pairs)


def tree_places():
    me = lax.axis_index("shard")
    core = lax.axis_index("seq")
    entry = jnp.arange(16, dtype=jnp.int32)
    v, u, z = entry // 8, entry // 4 % 2, entry % 4
    straight = me ^ (4 * z + 2 * u + v)
    crossed = me ^ (4 * z + 2 * v + u)
    rel = me ^ entry
    z, y, x = rel // 4, rel // 2 % 2, rel % 2
    place_straight = x * 8 + y * 4 + z
    place_crossed = y * 8 + x * 4 + z
    mine = jnp.where(core == 0, straight, crossed)
    place_mine = jnp.where(core == 0, place_straight, place_crossed)
    place_other = jnp.where(core == 0, place_crossed, place_straight)
    return mine, place_mine, place_other, core


def tree_gather(part):
    stack = jnp.stack([part] + [hop(part, (4 * k, 4 * k)) for k in range(1, 4)])
    stack = jnp.concatenate([stack, hop(stack, (2, 1))])
    return jnp.concatenate([stack, hop(stack, (1, 2))])


def join_kernel(places_ref, own_ref, other_ref, out_ref):
    half = own_ref.shape[2]
    first = places_ref[32] == 0

    @pl.when(first)
    def _():
        out_ref[:, :half] = own_ref[0]
        out_ref[:, half:] = other_ref[0]

    @pl.when(jnp.logical_not(first))
    def _():
        out_ref[:, :half] = other_ref[0]
        out_ref[:, half:] = own_ref[0]


def join(own, other, places):
    _, rows, half = own.shape
    return pl.pallas_call(
        join_kernel,
        grid_spec=pltpu.PrefetchScalarGridSpec(
            num_scalar_prefetch=1,
            grid=(16,),
            in_specs=[
                pl.BlockSpec((1, rows, half), lambda i, s: (s[i], 0, 0)),
                pl.BlockSpec((1, rows, half), lambda i, s: (s[16 + i], 0, 0)),
            ],
            out_specs=pl.BlockSpec((rows, 2 * half), lambda i, s: (i, 0)),
        ),
        out_shape=jax.ShapeDtypeStruct((16 * rows, 2 * half), own.dtype),
        name="join",
    )(places, own, other)


def gather_weight(part, spots):
    half = part.shape[1] // 2
    own = tree_gather(lax.dynamic_slice_in_dim(part, spots[3] * half, half, 1))
    places = jnp.concatenate([spots[1], spots[2], jnp.broadcast_to(spots[3], (1,)).astype(jnp.int32)])
    return join(own, swap_cores(own), places)


def fold_kernel(places_ref, own_ref, got_ref, out_ref):
    out_ref[0] = (own_ref[...].astype(F32) + got_ref[...].astype(F32)).astype(BF)


def fold(grad, got, places):
    rows, half = grad.shape[0] // 16, grad.shape[1] // 2
    return pl.pallas_call(
        fold_kernel,
        grid_spec=pltpu.PrefetchScalarGridSpec(
            num_scalar_prefetch=1,
            grid=(16,),
            in_specs=[
                pl.BlockSpec((rows, half), lambda i, s: (s[i], s[16])),
                pl.BlockSpec((rows, half), lambda i, s: (s[i], 0)),
            ],
            out_specs=pl.BlockSpec((1, rows, half), lambda i, s: (i, 0, 0)),
        ),
        out_shape=jax.ShapeDtypeStruct((16, rows, half), BF),
        name="fold",
    )(places, grad, got)


def add_low(left, right):
    return (left.astype(F32) + right.astype(F32)).astype(BF)


def scatter_grad(grad, spots):
    half = grad.shape[1] // 2
    core = spots[3]
    got = swap_cores(lax.dynamic_slice_in_dim(grad, (1 - core) * half, half, 1))
    places = jnp.concatenate([spots[0], jnp.broadcast_to(core, (1,)).astype(jnp.int32)])
    stack = fold(grad, got, places)
    stack = add_low(stack[:8], hop(stack[8:], (1, 2)))
    stack = add_low(stack[:4], hop(stack[4:], (2, 1)))
    arrived = [hop(stack[k], (4 * k, 4 * k)).astype(F32) for k in range(1, 4)]
    total = (stack[0].astype(F32) + arrived[0]) + (arrived[1] + arrived[2])
    low = total.astype(BF)
    other = swap_cores(low).astype(F32)
    low = low.astype(F32)
    return jnp.where(core == 0, jnp.concatenate([low, other], axis=1), jnp.concatenate([other, low], axis=1))


def to_all(part):
    return lax.all_to_all(jnp.broadcast_to(part[None], (lax.axis_size("shard"),) + part.shape), "shard", 0, 0, tiled=True)


def body(
    tokens, norm1_gain, norm1_bias, qkv_weight, qv_bias, position_table, proj_weight, proj_bias, norm2_gain,
    norm2_bias, fc1_weight, fc1_bias, fc2_weight, fc2_bias, rel_index, region_ids, cotangent,
):
    levels = lax.axis_size("seq").bit_length() - 1
    own_rows, arrived_rows = roll_sources()
    plan = {
        "levels": levels,
        "local": [1 if levels > level_pos else 2 for level_pos in range(3)],
        "bits": [levels - 1 - level_pos for level_pos in range(3)],
        "hots": (one_hot_rows(own_rows, 4 * WIN_TOK), one_hot_rows(arrived_rows, 4 * HALF)),
    }
    clips, wins, toks, width = tokens.shape
    tree = lax.axis_size("shard") == 16 and lax.axis_size("seq") == 2
    vectors = jnp.concatenate([norm1_gain, norm1_bias, qv_bias, proj_bias, norm2_gain, norm2_bias, fc1_bias, fc2_bias])
    cuts = np.cumsum([part.shape[0] for part in (norm1_gain, norm1_bias, qv_bias, proj_bias, norm2_gain, norm2_bias, fc1_bias)])
    fc_part = jnp.concatenate([proj_weight.T, fc1_weight, fc2_weight.T], axis=1)
    if tree:
        spots = tree_places()
        vectors = to_all(vectors)
        w_qkv = gather_weight(qkv_weight, spots)
        fc_all = gather_weight(fc_part, spots)
    else:
        vectors = lax.all_gather(vectors, "shard", axis=0, tiled=False)
        w_qkv = lax.all_gather(qkv_weight, "shard", axis=0, tiled=True)
        fc_all = lax.all_gather(fc_part, "shard", axis=0, tiled=True)
    gain_one, bias_one, qv_full, b_proj, gain_two, bias_two, b_fc1, b_fc2 = [
        part.reshape(-1) for part in jnp.split(vectors.astype(F32), cuts, axis=1)
    ]
    hidden_width = fc1_weight.shape[1]
    w_proj_t, w_fc1, w_fc2_t = jnp.split(fc_all, (width, width + hidden_width), axis=1)

    spread = jnp.asarray(spread_ones(), BF)
    wide8 = jnp.asarray(lane16(False).T, BF)
    wide16 = jnp.asarray(lane16(True), BF)
    maps = jnp.asarray(np.stack(lane_maps(False) + lane_maps(True)))
    rel8 = jnp.concatenate([rel_index[row : row + 1] for row in CORNER_ROWS], axis=0)
    table_rows = jnp.pad(position_table.T, ((0, 0), (0, TROWS - position_table.shape[0])))
    labels, values = pick(rel8, maps, table_rows)
    bias = bias_all(values, wide8, spread)

    region = region_ids[:, hwt_order()]
    region = jnp.broadcast_to(region[None], (clips, wins, toks)).reshape(-1, toks)
    mask_keys = (region[:, :, None] == jnp.arange(128)).astype(BF)
    mask_queries = jnp.where(region[:, None, :] == jnp.arange(32)[:, None], 0.0, BIG).astype(BF)

    rows_in = enter(tokens, plan).astype(F32)
    out_grad = enter(cotangent, plan)
    first, normed_one, inverse_one = norm_forward(rows_in, gain_one, bias_one)
    first = first.astype(BF)
    feature = jnp.einsum("de,wnd->wen", w_qkv, first, preferred_element_type=F32)
    q_t = ((feature[:, :width] + qv_full[:width, None]) * (SCALE * LOG2E)).astype(BF)
    k_t = feature[:, width : 2 * width].astype(BF)
    v_t = (feature[:, 2 * width :] + qv_full[width:, None]).astype(BF)
    token_k = jnp.einsum("wnd,de->wne", first, w_qkv[:, width : 2 * width], preferred_element_type=F32).astype(BF)
    token_v = jnp.einsum("wnd,de->wne", first, w_qkv[:, 2 * width :], preferred_element_type=F32)
    token_v = (token_v + qv_full[width:]).astype(BF)

    context_t, expo, inverse_sum = attend(q_t, token_k, v_t, bias, mask_queries, mask_keys)

    branch = jnp.einsum("wdn,ed->wne", context_t, w_proj_t, preferred_element_type=F32) + b_proj
    mid = rows_in + branch
    second, normed_two, inverse_two = norm_forward(mid, gain_two, bias_two)
    second = second.astype(BF)
    hidden = jnp.einsum("wnd,df->wnf", second, w_fc1, preferred_element_type=F32) + b_fc1
    act = gelu_exact(hidden).astype(BF)
    mlp = jnp.einsum("wnf,df->wnd", act, w_fc2_t, preferred_element_type=F32) + b_fc2
    block_out = leave((mid + mlp).astype(BF), plan, clips)

    fc2_grad = jnp.einsum("wnd,wnf->df", out_grad, act, preferred_element_type=F32)
    fc2_bias_grad = jnp.sum(out_grad.astype(F32), axis=(0, 1))
    act_grad = jnp.einsum("wnd,df->wnf", out_grad, w_fc2_t, preferred_element_type=F32)
    hidden_grad = (act_grad * gelu_slope(hidden)).astype(BF)
    fc1_grad = jnp.einsum("wnd,wnf->df", second, hidden_grad, preferred_element_type=F32)
    fc1_bias_grad = jnp.sum(hidden_grad.astype(F32), axis=(0, 1))
    second_grad = jnp.einsum("wnf,df->wnd", hidden_grad, w_fc1, preferred_element_type=F32)
    mid_grad = out_grad.astype(F32) + norm_backward(second_grad, normed_two, inverse_two, gain_two)
    norm2_gain_grad = jnp.sum(second_grad * normed_two, axis=(0, 1))
    norm2_bias_grad = jnp.sum(second_grad, axis=(0, 1))
    branch_grad = mid_grad.astype(BF)
    proj_grad = jnp.einsum("wne,wdn->ed", branch_grad, context_t, preferred_element_type=F32)
    proj_bias_grad = jnp.sum(branch_grad.astype(F32), axis=(0, 1))
    context_grad_t = jnp.einsum("wne,ed->wdn", branch_grad, w_proj_t, preferred_element_type=F32).astype(BF)

    dq_t, dk, dv, offsets = attend_back(expo, k_t, token_v, q_t, context_grad_t, context_t, inverse_sum, spread, wide16)

    wgrad_q = jnp.einsum("wnd,wen->de", first, dq_t, preferred_element_type=F32)
    wgrad_k = jnp.einsum("wnd,wne->de", first, dk, preferred_element_type=F32)
    wgrad_v = jnp.einsum("wnd,wne->de", first, dv, preferred_element_type=F32)
    qkv_wgrad = jnp.concatenate([wgrad_q, wgrad_k, wgrad_v], axis=1)
    qv_grad = jnp.concatenate([jnp.sum(dq_t.astype(F32), axis=(0, 2)), jnp.sum(dv.astype(F32), axis=(0, 1))])
    first_grad = (
        jnp.einsum("wen,de->wnd", dq_t, w_qkv[:, :width], preferred_element_type=F32)
        + jnp.einsum("wne,de->wnd", dk, w_qkv[:, width : 2 * width], preferred_element_type=F32)
        + jnp.einsum("wne,de->wnd", dv, w_qkv[:, 2 * width :], preferred_element_type=F32)
    )
    norm1_gain_grad = jnp.sum(first_grad * normed_one, axis=(0, 1))
    norm1_bias_grad = jnp.sum(first_grad, axis=(0, 1))
    input_grad = mid_grad + norm_backward(first_grad, normed_one, inverse_one, gain_one)
    input_grad = leave(input_grad.astype(BF), plan, clips).astype(F32)

    shards = lax.axis_size("shard")
    small = [norm1_gain_grad, norm1_bias_grad, qv_grad, proj_bias_grad, norm2_gain_grad, norm2_bias_grad, fc1_bias_grad, fc2_bias_grad]
    small = jnp.concatenate([part.reshape(shards, -1) for part in small], axis=1)
    offsets = offsets.reshape(HEADS, WIDE)
    fc_grads = jnp.concatenate([proj_grad, fc1_grad, fc2_grad], axis=1).astype(BF)
    if tree:
        both = lax.all_to_all(jnp.concatenate([small, offsets], axis=1), "shard", 0, 0, tiled=True)
        both = jnp.sum(both, axis=0)
        both = both + swap_cores(both)
        small, offsets = both[: small.shape[1]], to_all(both[small.shape[1] :])
        own_fc = scatter_grad(fc_grads, spots)
        own_qkv = scatter_grad(qkv_wgrad.astype(BF), spots)
    else:
        offsets = lax.psum(offsets, ("seq", "shard"))
        small = lax.psum(small, ("seq", "shard"))
        small = lax.dynamic_index_in_dim(small, lax.axis_index("shard"), 0, keepdims=False)

        def owned(grad):
            return lax.psum_scatter(lax.psum(grad, "seq"), "shard", scatter_dimension=0, tiled=True).astype(F32)

        own_fc = owned(fc_grads)
        own_qkv = owned(qkv_wgrad.astype(BF))
    table_grad = spill(labels, offsets)[:, : position_table.shape[0]].T
    own_proj, own_fc1, own_fc2 = jnp.split(own_fc, (width, width + hidden_width), axis=1)
    own_g1, own_b1, own_qv, own_pb, own_g2, own_b2, own_f1b, own_f2b = jnp.split(small, cuts)
    return (
        block_out, input_grad, own_g1, own_b1, own_qkv, own_qv, table_grad, own_proj.T, own_pb,
        own_g2, own_b2, own_fc1, own_f1b, own_fc2.T, own_f2b,
    )


def solution(mesh):
    return jax.shard_map(
        body,
        mesh=mesh,
        in_specs=(
            P("shard", "seq", None, None),
            P("shard"),
            P("shard"),
            P("shard", None),
            P("shard"),
            P(),
            P(None, "shard"),
            P("shard"),
            P("shard"),
            P("shard"),
            P("shard", None),
            P("shard"),
            P(None, "shard"),
            P("shard"),
            P(),
            P("seq", None),
            P("shard", "seq", None, None),
        ),
        out_specs=(
            P("shard", "seq", None, None),
            P("shard", "seq", None, None),
            P("shard"),
            P("shard"),
            P("shard", None),
            P("shard"),
            P(),
            P(None, "shard"),
            P("shard"),
            P("shard"),
            P("shard"),
            P("shard", None),
            P("shard"),
            P(None, "shard"),
            P("shard"),
        ),
        check_vma=False,
    )
```

```python
import jax
import jax.numpy as jnp
import numpy as np
from jax import lax
from jax.experimental import pallas as pl
from jax.experimental.pallas import tpu as pltpu
from jax.sharding import PartitionSpec as P

HEADS = 16
HEAD_DIM = 32
WT = 8
WH = 7
WW = 7
WIN_TOK = WT * WH * WW
EPS = 1e-05

BF=jnp.bfloat16; F32=jnp.float32
LOG2E=1.4426950408889634; LN2=0.6931471805599453
SCALE=HEAD_DIM**-0.5
BIG=-(2.0**30)
GROUP=4
VM=56*1024*1024

def cost(micros):
    return pl.CostEstimate(flops=int(micros * 1e9), bytes_accessed=int(micros * 3.6e6), transcendentals=0)


def nt(a,b): return lax.dot_general(a,b,(((1,),(1,)),((),())),preferred_element_type=F32)
def nn(a,b): return jnp.dot(a,b,preferred_element_type=F32)

def placed(block, at, rows):
    parts=[]
    if at: parts.append(jnp.zeros((at,block.shape[1]),block.dtype))
    parts.append(block)
    if rows-at-block.shape[0]: parts.append(jnp.zeros((rows-at-block.shape[0],block.shape[1]),block.dtype))
    return jnp.concatenate(parts,axis=0)

def attend_kernel(q_ref,k_ref,v_ref,bias_ref,mq_ref,mk_ref,ctx_ref,ctx_tok_ref,e_ref,r_ref):
    parts=[]
    lhs=jnp.concatenate([k_ref[0],mk_ref[0]],axis=1)
    ones=jnp.ones((16,q_ref.shape[2]),BF)
    for h in range(GROUP):
        rows=slice(h*HEAD_DIM,(h+1)*HEAD_DIM)
        rhs=jnp.concatenate([placed(q_ref[0,rows,:],h*HEAD_DIM,GROUP*HEAD_DIM),placed(mq_ref[0],0,128)],axis=0)
        s=nn(lhs,rhs)+bias_ref[h]
        m=jnp.max(s,axis=0,keepdims=True)
        e=jnp.exp2(s-m).astype(BF)
        e_ref[0,h]=e
        c=nn(jnp.concatenate([v_ref[0,rows,:],ones],axis=0),e)
        r=1.0/c[HEAD_DIM:HEAD_DIM+1]
        c=c[:HEAD_DIM]*r
        parts.append(c)
        ctx_ref[0,rows,:]=c.astype(BF)
        r_ref[0,0,h:h+1,:]=r
    ctx_tok_ref[0]=jnp.transpose(jnp.concatenate(parts,axis=0)).astype(BF)

def attend(side,qT,k,vT,bias,mq,mk):
    nw,width,n=qT.shape
    ng=width//256
    first=side*ng
    wins=mk.shape[0]
    return pl.pallas_call(
        attend_kernel,
        grid=(ng,nw),
        in_specs=[
            pl.BlockSpec((1,128,n),lambda g,w:(w,first+g,0)),
            pl.BlockSpec((1,n,128),lambda g,w:(w,0,first+g)),
            pl.BlockSpec((1,128,n),lambda g,w:(w,first+g,0)),
            pl.BlockSpec((GROUP,n,n),lambda g,w:(g,0,0)),
            pl.BlockSpec((1,32,n),lambda g,w:(w%wins,0,0)),
            pl.BlockSpec((1,n,128),lambda g,w:(w%wins,0,0)),
        ],
        out_specs=[
            pl.BlockSpec((1,128,n),lambda g,w:(w,g,0)),
            pl.BlockSpec((1,n,128),lambda g,w:(w,0,g)),
            pl.BlockSpec((1,GROUP,n,n),lambda g,w:(w,g,0,0)),
            pl.BlockSpec((1,1,GROUP,n),lambda g,w:(w,g,0,0)),
        ],
        out_shape=[
            jax.ShapeDtypeStruct((nw,width//2,n),BF),
            jax.ShapeDtypeStruct((nw,n,width//2),BF),
            jax.ShapeDtypeStruct((nw,ng*GROUP,n,n),BF),
            jax.ShapeDtypeStruct((nw,ng,GROUP,n),F32),
        ],
        compiler_params=pltpu.CompilerParams(vmem_limit_bytes=VM),
        name="attend", cost_estimate=cost(17),
    )(qT,k,vT,bias,mq,mk)

SPREAD=768
FLAT=1408
WIDE=2816

def spread_ones():
    n=WT*WH*WW
    tok=np.arange(n); c=tok//(WW*WT); e=tok//WT%WW; a=tok%WT
    out=np.zeros((n,SPREAD),np.float32); out[tok,c*104+e*8+a]=1
    return out

def lane16(mirror):
    out=np.zeros((128,256),np.float32)
    for u in range(16):
        for a in range(8):
            out[u*8+a,u*16+(7-a if mirror else a)]=1
    return out

def back_kernel(e_ref,k_ref,v_ref,q_ref,g_ref,ctx_ref,r_ref,sp_ref,l16_ref,dq_ref,dk_ref,dv_ref,tab_ref,tot,acc):
    w=pl.program_id(0); nw=pl.num_programs(0)
    n=q_ref.shape[2]
    dv=jnp.zeros((n,128),F32); dk=jnp.zeros((n,128),F32); dq=[]
    @pl.when(w==0)
    def _():
        tot[...]=jnp.zeros_like(tot)
    for h in range(GROUP):
        rows=slice(h*HEAD_DIM,(h+1)*HEAD_DIM)
        go=g_ref[0,rows,:].astype(F32)*r_ref[0,0,h:h+1,:]
        inner=jnp.sum(go*ctx_ref[0,rows,:].astype(F32),axis=0,keepdims=True)
        rhs=placed(go.astype(BF),h*HEAD_DIM,128)
        e=e_ref[0,h]
        dp=nn(v_ref[0],rhs)
        ds=(e.astype(F32)*(dp-inner))
        dsl=ds.astype(BF)
        tot[h]+=ds
        dv+=nt(e,rhs)
        dk+=nt(dsl,placed(q_ref[0,rows,:],h*HEAD_DIM,128))
        dq.append(nn(k_ref[0,rows,:],dsl)*SCALE)
    dq_ref[0]=jnp.transpose(jnp.concatenate(dq,axis=0)).astype(BF)
    dv_ref[0]=dv.astype(BF)
    dk_ref[0]=(dk*LN2).astype(BF)
    @pl.when(w==nw-1)
    def _():
        for h in range(GROUP):
            x=nn(tot[h].astype(BF),sp_ref[...])
            full=jnp.zeros((8,FLAT),F32)
            for d in range(WH):
                part=jnp.zeros((8,SPREAD),F32)
                for f in range(WW):
                    j=(d*WW+f)*8
                    part=part+pltpu.roll(x[j:j+8,:],8*(WW-1-f),1) if f<WW-1 else part+x[j:j+8,:]
                wide=jnp.concatenate([part,jnp.zeros((8,FLAT-SPREAD),F32)],axis=1)
                full=full+(pltpu.roll(wide,104*(WH-1-d),1) if d<WH-1 else wide)
            acc[h*8:(h+1)*8,:]=full
        a=acc[...]
        hi=a.astype(BF); lo=(a-hi.astype(F32)).astype(BF)
        wide=[]
        for t in range(FLAT//128):
            c=slice(t*128,(t+1)*128)
            wide.append(nn(hi[:,c],l16_ref[...])+nn(lo[:,c],l16_ref[...]))
        y=jnp.concatenate(wide,axis=1)
        for h in range(GROUP):
            z=pltpu.roll(y[h*8:(h+1)*8,:],0,1,stride=1,stride_axis=0)
            tab_ref[0,h:h+1,:]=jnp.sum(z,axis=0,keepdims=True)

def attend_back(g,e,kT,v,qT,gT,ctxT,r,sp,l16):
    nw,width,n=qT.shape
    feat=pl.BlockSpec((1,128,n),lambda w:(w,g,0))
    tok=pl.BlockSpec((1,n,128),lambda w:(w,0,g))
    own=pl.BlockSpec((1,n,128),lambda w:(w,0,0))
    return pl.pallas_call(
        back_kernel,
        grid=(nw,),
        in_specs=[
            pl.BlockSpec((1,GROUP,n,n),lambda w:(w,g%2,0,0)),
            feat,tok,feat,feat,pl.BlockSpec((1,128,n),lambda w:(w,g%2,0)),
            pl.BlockSpec((1,1,GROUP,n),lambda w:(w,g%2,0,0)),
            pl.BlockSpec(sp.shape,lambda w:(0,0)),
            pl.BlockSpec(l16.shape,lambda w:(0,0)),
        ],
        out_specs=[own,own,own,pl.BlockSpec((1,GROUP,WIDE),lambda w:(0,0,0))],
        out_shape=[
            jax.ShapeDtypeStruct((nw,n,128),BF),
            jax.ShapeDtypeStruct((nw,n,128),BF),
            jax.ShapeDtypeStruct((nw,n,128),BF),
            jax.ShapeDtypeStruct((1,GROUP,WIDE),F32),
        ],
        scratch_shapes=[pltpu.VMEM((GROUP,n,n),F32),pltpu.VMEM((GROUP*8,FLAT),F32)],
        compiler_params=pltpu.CompilerParams(vmem_limit_bytes=VM),
        name="attend_back", cost_estimate=cost(12),
    )(e,kT,v,qT,gT,ctxT,r,sp,l16)

def lane_maps(mirror):
    lane=np.arange(WIDE); pq=lane//16; o=lane%16
    p=pq//13; q=pq%13
    ok=(pq<169)&(o<15)
    if mirror: o=14-o
    A=o>=7; b=np.where(A,14-o,7-o); C=p>=6; d=np.where(C,12-p,6-p); E=q>=6; f=np.where(E,12-q,6-q)
    col=(b*WH+d)*WW+f
    corner=A*4+C*2+E*1
    return np.where(ok,col,-1).astype(np.int32), np.where(ok,corner,-1).astype(np.int32)

CORNER_ROWS=[(a*WH+c)*WW+e for a in (0,WT-1) for c in (0,WH-1) for e in (0,WW-1)]

def prepare_kernel(rel_ref,maps_ref,table_ref,region_ref,order_ref,lab_ref,val_ref,mk_ref,mq_ref):
    n=rel_ref.shape[1]
    rel=jnp.concatenate([rel_ref[row:row+1,:] for row in CORNER_ROWS],axis=0)
    hi=(rel>>6).astype(F32).astype(BF); lo=(rel&63).astype(F32).astype(BF)
    both=jnp.concatenate([hi,lo],axis=0)
    corners=lax.broadcasted_iota(jnp.int32,(8,256),0)
    rows=lax.broadcasted_iota(jnp.int32,(n,256),0)
    trow=lax.broadcasted_iota(jnp.int32,(table_ref.shape[1],256),0)
    for t in range(WIDE//256):
        c=slice(t*256,(t+1)*256)
        for version in range(2):
            col=maps_ref[2*version:2*version+1,c]; cor=maps_ref[2*version+1:2*version+2,c]
            m=jnp.where(rows==col,1.0,0.0).astype(BF)
            y=nn(both,m)
            full=y[:8]*64.0+y[8:]
            lab=jnp.sum(jnp.where(corners==cor,full,0.0),axis=0,keepdims=True)
            lab=jnp.where(cor>=0,lab,-1.0).astype(jnp.int32)
            lab_ref[version:version+1,c]=lab
            if version==0:
                hot=jnp.where(trow==lab,1.0,0.0).astype(BF)
                val_ref[:,0,c]=nn(table_ref[...],hot)
    wins=region_ref.shape[0]
    region=jnp.concatenate([region_ref[...].astype(F32),jnp.zeros((16-wins,n),F32)],axis=0).astype(BF)
    across=nt(region,order_ref[...])
    down=nt(order_ref[...],region)
    lanes=lax.broadcasted_iota(jnp.int32,(n,128),1).astype(F32)
    subs=lax.broadcasted_iota(jnp.int32,(32,n),0).astype(F32)
    for w in range(wins):
        mk_ref[w]=jnp.where(down[:,w:w+1]==lanes,1.0,0.0).astype(BF)
        mq_ref[w]=jnp.where(across[w:w+1,:]==subs,0.0,BIG).astype(BF)

def prepare(rel_index,maps,table_t,region_ids,order):
    wins,n=region_ids.shape
    return pl.pallas_call(
        prepare_kernel,
        out_shape=[
            jax.ShapeDtypeStruct((2,WIDE),jnp.int32),
            jax.ShapeDtypeStruct((HEADS,1,WIDE),F32),
            jax.ShapeDtypeStruct((wins,n,128),BF),
            jax.ShapeDtypeStruct((wins,32,n),BF),
        ],
        compiler_params=pltpu.CompilerParams(vmem_limit_bytes=VM),
        name="prepare", cost_estimate=cost(6),
    )(rel_index,maps,table_t,region_ids,order)

def bias_kernel(val_ref,l8_ref,sp_ref,bias_ref,x_ref):
    base=jnp.broadcast_to(val_ref[0],(8,WIDE))
    z=pltpu.roll(base,WIDE-7,1,stride=1,stride_axis=0).astype(BF)
    narrow=jnp.concatenate([nn(z[:,t*256:(t+1)*256],l8_ref[...]) for t in range(FLAT//128)],axis=1)
    for d in range(WH):
        s=FLAT-104*(WH-1-d)
        wide=(pltpu.roll(narrow,s,1) if d<WH-1 else narrow)[:,:SPREAD]
        for f in range(WW):
            j=(d*WW+f)*8
            x_ref[j:j+8,:]=pltpu.roll(wide,SPREAD-8*(WW-1-f),1) if f<WW-1 else wide
    bias_ref[0]=nt(x_ref[...].astype(BF),sp_ref[...])*LOG2E

def bias_half(side,val,l8,sp):
    n=sp.shape[0]
    heads=HEADS//2
    return pl.pallas_call(
        bias_kernel,
        grid=(heads,),
        in_specs=[pl.BlockSpec((1,1,WIDE),lambda h:(side*heads+h,0,0)),pl.BlockSpec(l8.shape,lambda h:(0,0)),pl.BlockSpec(sp.shape,lambda h:(0,0))],
        out_specs=pl.BlockSpec((1,n,n),lambda h:(h,0,0)),
        out_shape=jax.ShapeDtypeStruct((heads,n,n),F32),
        scratch_shapes=[pltpu.VMEM((n,SPREAD),F32)],
        compiler_params=pltpu.CompilerParams(vmem_limit_bytes=VM),
        name="position_bias", cost_estimate=cost(10),
    )(val,l8,sp)

def spill_kernel(lab_ref,g_ref,out_ref):
    g=g_ref[...]
    hi=g.astype(BF); r1=g-hi.astype(F32); mid=r1.astype(BF); lo=(r1-mid.astype(F32)).astype(BF)
    three=jnp.concatenate([hi,mid,lo],axis=0)
    rows=out_ref.shape[1]
    trow=lax.broadcasted_iota(jnp.int32,(rows,256),0)
    tot=jnp.zeros((48,rows),F32)
    for t in range(WIDE//256):
        c=slice(t*256,(t+1)*256)
        hot=jnp.where(trow==lab_ref[1:2,c],1.0,0.0).astype(BF)
        tot=tot+nt(three[:,c],hot)
    out_ref[...]=tot[:16]+tot[16:32]+tot[32:]

def spill(lab,g,rows):
    return pl.pallas_call(
        spill_kernel,
        out_shape=jax.ShapeDtypeStruct((HEADS,rows),F32),
        compiler_params=pltpu.CompilerParams(vmem_limit_bytes=VM),
        name="table_rows", cost_estimate=cost(5),
    )(lab,g)


BLOCK = 32
B_FC1, B_PROJ, GAIN2, BIAS2, B_FC2, GAIN1, BIAS1, B_QV = range(8)
VEC_LANES = {B_FC1: (0, 128), GAIN1: (128, 32), BIAS1: (160, 32), B_QV: (192, 64), B_PROJ: (256, 32), GAIN2: (288, 32), BIAS2: (320, 32), B_FC2: (352, 32)}
VECTOR = 384


def load_weight(own_ref, other_ref, places_ref, held, sem, vecs=None):
    core = places_ref[64]
    lanes = slice(0, held.shape[2])
    copies = []
    for i in range(16):
        rows = pl.ds(i * BLOCK, BLOCK)
        own = own_ref.at[places_ref[i]]
        copies.append(pltpu.make_async_copy(own.at[:, lanes], held.at[core, rows, :], sem.at[2 * i]))
        copies.append(
            pltpu.make_async_copy(other_ref.at[places_ref[16 + i]].at[:, lanes], held.at[1 - core, rows, :], sem.at[2 * i + 1])
        )
        if vecs is not None:
            copies.append(pltpu.make_async_copy(own.at[0:16, held.shape[2] :], vecs.at[i], sem.at[32 + i]))
    for copy in copies:
        copy.start()
    for copy in copies:
        copy.wait()


def store_grad(total, places_ref, own_ref, send_ref):
    core = places_ref[64]

    def block(i, carry):
        own_ref[i, :, : total.shape[2]] = total[core, pl.ds(pl.multiple_of(places_ref[32 + i] * BLOCK, BLOCK), BLOCK), :].astype(BF)
        send_ref[i, :, : total.shape[2]] = total[1 - core, pl.ds(pl.multiple_of(places_ref[48 + i] * BLOCK, BLOCK), BLOCK), :].astype(BF)
        return carry

    lax.fori_loop(0, 16, block, 0)


def normalise(values):
    mean = jnp.mean(values, axis=-1, keepdims=True)
    centred = values - mean
    inverse = lax.rsqrt(jnp.mean(centred * centred, axis=-1, keepdims=True) + EPS)
    return centred * inverse, inverse


def project_kernel(
    places_ref, x_ref, own_ref, other_ref, q_ref, kt_ref, vt_ref, k_ref, v_ref, vec_ref, held, loose, sem
):
    @pl.when(pl.program_id(0) == 0)
    def _():
        load_weight(own_ref, other_ref, places_ref, held, sem, loose)
        rows = [loose[i].astype(F32) for i in range(16)]
        for name, (at, count) in VEC_LANES.items():
            parts = [row[at // 128 : at // 128 + 1, at % 128 : at % 128 + count] for row in rows]
            vec_ref[name : name + 1, : 16 * count] = jnp.concatenate(parts, axis=1)

    width = x_ref.shape[2]
    normed, _ = normalise(x_ref[0].astype(F32))
    first = (normed * vec_ref[GAIN1 : GAIN1 + 1, :width] + vec_ref[BIAS1 : BIAS1 + 1, :width]).astype(BF)
    left, right = nn(first, held[0]), nn(first, held[1])
    half = width // 2
    q = (left[:, :width] + vec_ref[B_QV : B_QV + 1, :width]) * (SCALE * LOG2E)
    k = jnp.concatenate([left[:, width:], right[:, :half]], axis=1)
    v = right[:, half:] + vec_ref[B_QV : B_QV + 1, width : 2 * width]
    q_ref[0] = jnp.transpose(q).astype(BF)
    kt_ref[0] = jnp.transpose(k).astype(BF)
    vt_ref[0] = jnp.transpose(v).astype(BF)
    k_ref[0] = k.astype(BF)
    v_ref[0] = v.astype(BF)


def project(places, x, own, other, hidden_width):
    nw, n, width = x.shape
    tok = pl.BlockSpec((1, n, width), lambda w, s: (w, 0, 0))
    feat = pl.BlockSpec((1, width, n), lambda w, s: (w, 0, 0))
    anywhere = pl.BlockSpec(memory_space=pl.ANY)
    vecs = (8, hidden_width)
    return pl.pallas_call(
        project_kernel,
        grid_spec=pltpu.PrefetchScalarGridSpec(
            num_scalar_prefetch=1,
            grid=(nw,),
            in_specs=[tok, anywhere, anywhere],
            out_specs=[feat, feat, feat, tok, tok, pl.BlockSpec(vecs, lambda w, s: (0, 0))],
            scratch_shapes=[
                pltpu.VMEM((2, 16 * BLOCK, own.shape[2] - 128), BF),
                pltpu.VMEM((16, 16, 128), BF),
                pltpu.SemaphoreType.DMA((48,)),
            ],
        ),
        out_shape=[jax.ShapeDtypeStruct((nw, width, n), BF)] * 3
        + [jax.ShapeDtypeStruct((nw, n, width), BF)] * 2
        + [jax.ShapeDtypeStruct(vecs, F32)],
        compiler_params=pltpu.CompilerParams(vmem_limit_bytes=VM),
        name="project", cost_estimate=cost(9),
    )(places, x, own, other)


TAIL = (0.254829592, -0.284496736, 1.421413741, -1.453152027, 1.061405429)


def normal_parts(values):
    t = pl.reciprocal(1.0 + (0.3275911 * 0.7071067811865476) * jnp.abs(values), approx=False)
    series = TAIL[4]
    for factor in TAIL[3::-1]:
        series = series * t + factor
    bell = jnp.exp2(values * values * (-0.5 * LOG2E))
    upper = (0.5 * t) * series * bell
    return jnp.where(values >= 0, 1.0 - upper, upper), bell * 0.3989422804014327


def column_sums(values):
    return jnp.sum(values, axis=0, keepdims=True)


def feed_kernel(
    places_ref, x_ref, ctx0_ref, ctx1_ref, og_ref, vec_ref, own_ref, other_ref, out_ref, mid_grad_ref, gt_ref, own_grad_ref,
    send_grad_ref, sums_ref, held, total, sem,
):
    step = pl.program_id(0)

    @pl.when(step == 0)
    def _():
        total[...] = jnp.zeros_like(total)
        sums_ref[...] = jnp.zeros_like(sums_ref)
        load_weight(own_ref, other_ref, places_ref, held, sem)

    width = x_ref.shape[2]
    half = width // 2
    chunk = (held.shape[2] - half) // 2
    vec = lambda row: vec_ref[row : row + 1, :width]
    ctx = (ctx0_ref[0], ctx1_ref[0])
    branch = nt(ctx[0], held[0, :, :half]) + nt(ctx[1], held[1, :, :half])
    mid = x_ref[0].astype(F32) + (branch + vec(B_PROJ))
    normed, inverse = normalise(mid)
    second = normed * vec(GAIN2) + vec(BIAS2)
    second_t = jnp.transpose(second).astype(BF)
    second = second.astype(BF)
    og = og_ref[0]
    og_t = jnp.transpose(og.astype(F32)).astype(BF)
    mlp = jnp.zeros(mid.shape, F32)
    second_grad = jnp.zeros(mid.shape, F32)
    for j in range(2):
        for part in range(2):
            piece = chunk // 2
            c1 = slice(half + part * piece, half + (part + 1) * piece)
            c2 = slice(half + chunk + part * piece, half + chunk + (part + 1) * piece)
            cols = slice(j * chunk + part * piece, j * chunk + (part + 1) * piece)
            fc1, fc2_t = held[j, :, c1], held[j, :, c2]
            hidden = nn(second, fc1) + vec_ref[B_FC1 : B_FC1 + 1, cols]
            act_grad = nn(og, fc2_t)
            phi_sum, density = normal_parts(hidden)
            act = (hidden * phi_sum).astype(BF)
            hidden_grad = act_grad * (phi_sum + hidden * density)
            sums_ref[0:1, cols] += column_sums(hidden_grad)
            hidden_grad = hidden_grad.astype(BF)
            mlp += nt(act, fc2_t)
            second_grad += nt(hidden_grad, fc1)
            total[j, :, c1] += nn(second_t, hidden_grad)
            total[j, :, c2] += nn(og_t, act)
    out_ref[0] = (mid + (mlp + vec(B_FC2))).astype(BF)
    scaled = second_grad * vec(GAIN2)
    inner = jnp.mean(scaled, axis=-1, keepdims=True)
    along = jnp.mean(scaled * normed, axis=-1, keepdims=True)
    og = og.astype(F32)
    mid_grad = og + inverse * (scaled - inner - normed * along)
    mid_grad_ref[0] = mid_grad
    low = mid_grad.astype(BF)
    sums_ref[1:2, :width] += column_sums(mid_grad)
    sums_ref[2:3, :width] += column_sums(second_grad * normed)
    sums_ref[3:4, :width] += column_sums(second_grad)
    sums_ref[4:5, :width] += column_sums(og)
    low_t = jnp.transpose(mid_grad).astype(BF)
    for j in range(2):
        total[j, :, :half] += nn(low_t, ctx[j])
        proj = jnp.transpose(held[j, :, :half].astype(F32)).astype(BF)
        gt_ref[0, j * half : (j + 1) * half, :] = nn(proj, low_t).astype(BF)

    @pl.when(step == pl.num_programs(0) - 1)
    def _():
        store_grad(total, places_ref, own_grad_ref, send_grad_ref)


def feed(places, x, ctx0, ctx1, og, vecs, own, other):
    nw, n, width = x.shape
    tok = pl.BlockSpec((1, n, width), lambda w, s: (w, 0, 0))
    feat = pl.BlockSpec((1, width, n), lambda w, s: (w, 0, 0))
    whole = pl.BlockSpec(own.shape, lambda w, s: (0, 0, 0))
    anywhere = pl.BlockSpec(memory_space=pl.ANY)
    side = pl.BlockSpec((1, n, width // 2), lambda w, s: (w, 0, 0))
    hidden_width = own.shape[2] - width // 2
    return pl.pallas_call(
        feed_kernel,
        grid_spec=pltpu.PrefetchScalarGridSpec(
            num_scalar_prefetch=1,
            grid=(nw,),
            in_specs=[tok, side, side, tok, pl.BlockSpec(vecs.shape, lambda w, s: (0, 0)), anywhere, anywhere],
            out_specs=[tok, tok, feat, whole, whole, pl.BlockSpec((8, hidden_width), lambda w, s: (0, 0))],
            scratch_shapes=[
                pltpu.VMEM((2, 16 * BLOCK, own.shape[2]), BF),
                pltpu.VMEM((2, 16 * BLOCK, own.shape[2]), F32),
                pltpu.SemaphoreType.DMA((32,)),
            ],
        ),
        out_shape=[
            jax.ShapeDtypeStruct((nw, n, width), BF),
            jax.ShapeDtypeStruct((nw, n, width), F32),
            jax.ShapeDtypeStruct((nw, width, n), BF),
            jax.ShapeDtypeStruct(own.shape, BF),
            jax.ShapeDtypeStruct(own.shape, BF),
            jax.ShapeDtypeStruct((8, hidden_width), F32),
        ],
        compiler_params=pltpu.CompilerParams(vmem_limit_bytes=VM),
        name="feed_forward", cost_estimate=cost(44),
    )(places, x, ctx0, ctx1, og, vecs, own, other)


def input_kernel(
    places_ref, x_ref, dq0, dk0, dv0, dq1, dk1, dv1, dq2, dk2, dv2, dq3, dk3, dv3, mid_grad_ref, vec_ref, fc_sums_ref,
    own_ref, other_ref, out_ref, own_grad_ref, send_grad_ref, held, total, sums, small, sem,
):
    step = pl.program_id(0)

    @pl.when(step == 0)
    def _():
        total[...] = jnp.zeros_like(total)
        sums[...] = jnp.zeros_like(sums)
        load_weight(own_ref, other_ref, places_ref, held, sem)

    width = x_ref.shape[2]
    half = width // 2
    vec = lambda row: vec_ref[row : row + 1, :width]
    normed, inverse = normalise(x_ref[0].astype(F32))
    first_t = jnp.transpose(normed * vec(GAIN1) + vec(BIAS1)).astype(BF)
    left = jnp.concatenate([dq0[0], dq1[0], dq2[0], dq3[0], dk0[0], dk1[0]], axis=1)
    right = jnp.concatenate([dk2[0], dk3[0], dv0[0], dv1[0], dv2[0], dv3[0]], axis=1)
    total[0] += nn(first_t, left)
    total[1] += nn(first_t, right)
    first_grad = (nt(left, held[0]) + nt(right, held[1])).astype(BF).astype(F32)
    scaled = first_grad * vec(GAIN1)
    inner = jnp.mean(scaled, axis=-1, keepdims=True)
    along = jnp.mean(scaled * normed, axis=-1, keepdims=True)
    out_ref[0] = (mid_grad_ref[0] + inverse * (scaled - inner - normed * along)).astype(BF)
    sums[0:1, :width] += column_sums(first_grad * normed)
    sums[1:2, :width] += column_sums(first_grad)
    sums[2:3, :width] += column_sums(left[:, :width].astype(F32))
    sums[2:3, width:] += column_sums(right[:, half:].astype(F32))

    @pl.when(step == pl.num_programs(0) - 1)
    def _():
        columns = total.shape[2]
        store_grad(total, places_ref, own_grad_ref, send_grad_ref)
        rows = {
            B_FC1: fc_sums_ref[0:1, :], B_PROJ: fc_sums_ref[1:2, :], GAIN2: fc_sums_ref[2:3, :], BIAS2: fc_sums_ref[3:4, :],
            B_FC2: fc_sums_ref[4:5, :], GAIN1: sums[0:1, :], BIAS1: sums[1:2, :], B_QV: sums[2:3, :],
        }
        for i in range(16):
            parts = [rows[name][:, i * count : (i + 1) * count] for name, (_, count) in VEC_LANES.items()]
            line = jnp.concatenate(parts, axis=1)
            small[i] = jnp.concatenate([line[:, :128], line[:, 128:256], line[:, 256:], jnp.zeros((BLOCK - 3, 128), F32)], axis=0)

        def block(i, carry):
            own_grad_ref[i, :, columns:] = small[places_ref[32 + i]].astype(BF)
            send_grad_ref[i, :, columns:] = small[places_ref[48 + i]].astype(BF)
            return carry

        lax.fori_loop(0, 16, block, 0)


def input_side(places, x, groups, mid_grad, vecs, fc_sums, own, other):
    nw, n, width = x.shape
    tok = pl.BlockSpec((1, n, width), lambda w, s: (w, 0, 0))
    part = pl.BlockSpec((1, n, 128), lambda w, s: (w, 0, 0))
    flat = lambda shape: pl.BlockSpec(shape, lambda w, s: (0,) * len(shape))
    anywhere = pl.BlockSpec(memory_space=pl.ANY)
    columns = own.shape[2] - 128
    grad = own.shape
    return pl.pallas_call(
        input_kernel,
        grid_spec=pltpu.PrefetchScalarGridSpec(
            num_scalar_prefetch=1,
            grid=(nw,),
            in_specs=[tok] + [part] * 12 + [tok, flat(vecs.shape), flat(fc_sums.shape), anywhere, anywhere],
            out_specs=[tok, flat(grad), flat(grad)],
            scratch_shapes=[
                pltpu.VMEM((2, 16 * BLOCK, columns), BF),
                pltpu.VMEM((2, 16 * BLOCK, columns), F32),
                pltpu.VMEM((8, 2 * width), F32),
                pltpu.VMEM((16, BLOCK, 128), F32),
                pltpu.SemaphoreType.DMA((32,)),
            ],
        ),
        out_shape=[
            jax.ShapeDtypeStruct((nw, n, width), BF),
            jax.ShapeDtypeStruct(grad, BF),
            jax.ShapeDtypeStruct(grad, BF),
        ],
        compiler_params=pltpu.CompilerParams(vmem_limit_bytes=VM),
        name="input_side", cost_estimate=cost(15),
    )(places, x, *[part for group in groups for part in group[:3]], mid_grad, vecs, fc_sums, own, other)


def from_partner(shard, axis, stride):
    return lax.ppermute(shard, axis, [(i, i ^ 1 << stride) for i in range(lax.axis_size(axis))])


def to_block(windows, local_count):
    clip_count, chans = (windows.shape[0], windows.shape[-1])
    parted = windows.reshape(
        clip_count, local_count[0], local_count[1], local_count[2], WT, WH, WW, chans
    )
    parted = parted.transpose(0, 1, 4, 2, 5, 3, 6, 7)
    return parted.reshape(
        clip_count, local_count[0] * WT, local_count[1] * WH, local_count[2] * WW, chans
    )


def from_block(block, local_count):
    clip_count, chans = (block.shape[0], block.shape[-1])
    parted = block.reshape(
        clip_count, local_count[0], WT, local_count[1], WH, local_count[2], WW, chans
    )
    parted = parted.transpose(0, 1, 3, 5, 2, 4, 6, 7)
    return parted.reshape(clip_count, -1, WT * WH * WW, chans)


def roll_ahead(windows, local_count, bit_list):
    block = to_block(windows, local_count)
    for grid_dim, amount, bit_pos in (
        (1, WT // 2, bit_list[0]),
        (2, WH // 2, bit_list[1]),
        (3, WW // 2, bit_list[2]),
    ):
        if bit_pos < 0:
            block = jnp.roll(block, -amount, axis=grid_dim)
        else:
            front = lax.slice_in_dim(block, 0, amount, axis=grid_dim)
            arrived = from_partner(front, "seq", bit_pos)
            rest = lax.slice_in_dim(block, amount, block.shape[grid_dim], axis=grid_dim)
            block = jnp.concatenate([rest, arrived], axis=grid_dim)
    return from_block(block, local_count)


def roll_behind(windows, local_count, bit_list):
    block = to_block(windows, local_count)
    for grid_dim, amount, bit_pos in (
        (1, WT // 2, bit_list[0]),
        (2, WH // 2, bit_list[1]),
        (3, WW // 2, bit_list[2]),
    ):
        if bit_pos < 0:
            block = jnp.roll(block, amount, axis=grid_dim)
        else:
            extent = block.shape[grid_dim]
            trailing = lax.slice_in_dim(block, extent - amount, extent, axis=grid_dim)
            arrived = from_partner(trailing, "seq", bit_pos)
            rest = lax.slice_in_dim(block, 0, extent - amount, axis=grid_dim)
            block = jnp.concatenate([arrived, rest], axis=grid_dim)
    return from_block(block, local_count)


KEEP = WT // 2 * WH * WW


def hwt_order():
    place = np.arange(WIN_TOK)
    return (place % WT * WH + place // (WW * WT)) * WW + place // WT % WW


def order_ones(shift):
    place = np.arange(WIN_TOK)
    out = np.zeros((WIN_TOK, WIN_TOK), np.float32)
    out[place, ((place + shift) % WT * WH + place // (WW * WT)) * WW + place // WT % WW] = 1
    return out


def tile_runs(win):
    runs = []
    for c in range(WH):
        h = (win // 2 * WH + c + WH // 2) % (2 * WH)
        for e, count in ((0, WW - WW // 2), (WW - WW // 2, WW // 2)):
            w = (win % 2 * WW + e + WW // 2) % (2 * WW)
            runs.append((h // WH * 2 + w // WW, h % WH * WW + w % WW, count))
    return runs


def swap_cores(part):
    return lax.ppermute(part, "seq", [(0, 1), (1, 0)])


def enter_kernel(own_ref, arrived_ref, order_ref, out_ref, held):
    _, n, width = own_ref.shape
    rows = lax.broadcasted_iota(jnp.int32, (n, width), 0)
    for source in range(4):
        values = jnp.where(rows >= KEEP, own_ref[source].astype(F32), arrived_ref[source].astype(F32)).astype(BF)
        held[source] = nn(order_ref[...], values)
    for win in range(4):
        parts = [held[source, 8 * at : 8 * (at + count), :] for source, at, count in tile_runs(win)]
        out_ref[win] = jnp.concatenate(parts, axis=0).astype(BF)


def leave_kernel(rows_ref, order_ref, out_ref, send_ref, held):
    for win in range(4):
        values = rows_ref[win].astype(F32)
        start = 0
        for source, at, count in tile_runs(win):
            held[source, 8 * at : 8 * (at + count), :] = values[8 * start : 8 * (start + count), :]
            start += count
    for source in range(4):
        values = nn(order_ref[...], held[source].astype(BF)).astype(out_ref.dtype)
        out_ref[source] = values
        send_ref[source] = values[: send_ref.shape[1]].astype(BF)


SENT = 208


def enter(windows, plan, arrived=None):
    clips, wins, toks, width = windows.shape
    if plan["levels"] == 1 and clips == 1:
        own = windows.reshape(wins, toks, width)
        return pl.pallas_call(
            enter_kernel,
            out_shape=jax.ShapeDtypeStruct(own.shape, BF),
            scratch_shapes=[pltpu.VMEM(own.shape, F32)],
            compiler_params=pltpu.CompilerParams(vmem_limit_bytes=VM),
            name="enter", cost_estimate=cost(4),
        )(own, arrived.reshape(own.shape), plan["order"])
    rolled = roll_ahead(windows, plan["local"], plan["bits"])
    rolled = rolled.reshape(clips * wins, WT, WH * WW, width).transpose(0, 2, 1, 3)
    return rolled.reshape(clips * wins, toks, width)


def leave(windows, plan, kind):
    wins, toks, width = windows.shape
    return pl.pallas_call(
        leave_kernel,
        out_shape=[jax.ShapeDtypeStruct(windows.shape, kind), jax.ShapeDtypeStruct((wins, SENT, width), BF)],
        scratch_shapes=[pltpu.VMEM(windows.shape, F32)],
        compiler_params=pltpu.CompilerParams(vmem_limit_bytes=VM),
        name="leave", cost_estimate=cost(4),
    )(windows, plan["order"].T)


def joined(kept, arrived):
    arrived = jnp.pad(arrived.astype(kept.dtype), ((0, 0), (0, kept.shape[1] - SENT), (0, 0)))
    rows = lax.broadcasted_iota(jnp.int32, kept.shape, 1)
    return jnp.where(rows < KEEP, arrived, kept)[None]


def leave_any(windows, plan, clips, kind):
    count, toks, width = windows.shape
    wins = count // clips
    if plan["levels"] == 1 and clips == 1:
        kept, sent = leave(windows, plan, kind)
        return joined(kept, swap_cores(sent))
    rows = windows.reshape(count, WH * WW, WT, width).transpose(0, 2, 1, 3)
    return roll_behind(rows.reshape(clips, wins, toks, width), plan["local"], plan["bits"]).astype(kind)


def pack_kernel(core_ref, qkv_ref, proj_ref, fc1_ref, fc2_ref, *rest):
    vec_refs, (qkv_out, fc_out) = rest[:-2], rest[-2:]

    def emit(side):
        half = qkv_ref.shape[1] // 2
        qkv_out[:, :half] = qkv_ref[:, side * half : (side + 1) * half]
        at = 0
        for ref in (proj_ref, fc1_ref, fc2_ref):
            half = ref.shape[1] // 2
            fc_out[:, at : at + half] = ref[:, side * half : (side + 1) * half]
            at += half

    half = qkv_ref.shape[1] // 2
    line = jnp.concatenate([ref[...].astype(F32).reshape(1, -1) for ref in vec_refs], axis=1)
    lines = [line[:, at : at + 128] for at in range(0, VECTOR, 128)]
    qkv_out[:, half:] = jnp.concatenate(lines + [jnp.zeros((BLOCK - len(lines), 128), F32)], axis=0).astype(BF)
    for side in range(2):
        @pl.when(core_ref[0] == side)
        def _():
            emit(side)


def pack(core, qkv, proj_t, fc1, fc2_t, vectors):
    columns = (proj_t.shape[1] + fc1.shape[1] + fc2_t.shape[1]) // 2
    vmem = pl.BlockSpec(memory_space=pltpu.VMEM)
    return pl.pallas_call(
        pack_kernel,
        in_specs=[pl.BlockSpec(memory_space=pltpu.SMEM)] + [vmem] * (4 + len(vectors)),
        out_shape=[
            jax.ShapeDtypeStruct((BLOCK, qkv.shape[1] // 2 + 128), BF),
            jax.ShapeDtypeStruct((BLOCK, columns), BF),
        ],
        compiler_params=pltpu.CompilerParams(vmem_limit_bytes=VM),
        name="pack", cost_estimate=cost(2),
    )(core, qkv, proj_t, fc1, fc2_t, *vectors)


def hop(part, flips):
    pairs = [(16 * c + s, 16 * c + (s ^ flips[c])) for c in range(2) for s in range(16)]
    return lax.ppermute(part, ("seq", "shard"), pairs)


def tree_places():
    me = lax.axis_index("shard")
    core = lax.axis_index("seq")
    entry = jnp.arange(16, dtype=jnp.int32)
    v, u, z = entry // 8, entry // 4 % 2, entry % 4
    straight, crossed = me ^ (4 * z + 2 * u + v), me ^ (4 * z + 2 * v + u)
    rel = me ^ entry
    z, y, x = rel // 4, rel // 2 % 2, rel % 2
    place_straight, place_crossed = x * 8 + y * 4 + z, y * 8 + x * 4 + z
    even = core == 0
    pick_core = lambda left, right: jnp.where(even, left, right)
    return jnp.concatenate(
        [
            pick_core(place_straight, place_crossed),
            pick_core(place_crossed, place_straight),
            pick_core(straight, crossed),
            pick_core(crossed, straight),
            jnp.broadcast_to(core, (1,)),
        ]
    ).astype(jnp.int32)


def tree_gather(part):
    arrived = yield [hop(part, (4 * k, 4 * k)) for k in range(1, 4)]
    stack = jnp.stack([part] + arrived)
    arrived = yield hop(stack, (2, 1))
    stack = jnp.concatenate([stack, arrived])
    arrived = yield hop(stack, (1, 2))
    stack = jnp.concatenate([stack, arrived])
    other = yield swap_cores(stack)
    yield stack, other


def tie(*items):
    return lax.optimization_barrier(items)


def add_low(left, right):
    return (left.astype(F32) + right.astype(F32)).astype(BF)


def tree_scatter(own, send):
    arrived = yield swap_cores(send)
    stack = add_low(own, arrived)
    arrived = yield hop(stack[8:], (1, 2))
    stack = add_low(stack[:8], arrived)
    arrived = yield hop(stack[4:], (2, 1))
    stack = add_low(stack[:4], arrived)
    arrived = yield [hop(stack[k], (4 * k, 4 * k)) for k in range(1, 4)]
    arrived = [part.astype(F32) for part in arrived]
    yield (stack[0].astype(F32) + arrived[0]) + (arrived[1] + arrived[2])


def finish(steps, pending):
    while True:
        try:
            pending = steps.send(pending)
        except StopIteration:
            return pending


def sides(part, core):
    other = swap_low(part)
    return [jnp.where(core == 0, part, other), jnp.where(core == 0, other, part)]


def swap_low(part):
    return swap_cores(part.astype(BF)).astype(F32)


def to_all(part):
    return lax.all_to_all(jnp.broadcast_to(part[None], (lax.axis_size("shard"),) + part.shape), "shard", 0, 0, tiled=True)


def body(
    tokens, norm1_gain, norm1_bias, qkv_weight, qv_bias, position_table, proj_weight, proj_bias, norm2_gain,
    norm2_bias, fc1_weight, fc1_bias, fc2_weight, fc2_bias, rel_index, region_ids, cotangent,
):
    levels = lax.axis_size("seq").bit_length() - 1
    clips, wins, toks, width = tokens.shape
    hidden_width = fc1_weight.shape[1]
    plan = {
        "levels": levels,
        "local": [1 if levels > level_pos else 2 for level_pos in range(3)],
        "bits": [levels - 1 - level_pos for level_pos in range(3)],
        "order": jnp.asarray(order_ones(WT // 2), BF),
    }
    vectors = [fc1_bias, norm1_gain, norm1_bias, qv_bias, proj_bias, norm2_gain, norm2_bias, fc2_bias]
    sizes = [part.shape[0] for part in vectors]
    spread = jnp.asarray(spread_ones(), BF)
    wide8 = jnp.asarray(lane16(False).T, BF)
    wide16 = jnp.asarray(lane16(True), BF)
    maps = jnp.asarray(np.stack(lane_maps(False) + lane_maps(True)))
    table = prepare(rel_index, maps, position_table.T, region_ids, jnp.asarray(order_ones(0), BF))
    if clips == 1 and lax.axis_size("shard") == 16 and lax.axis_size("seq") == 2:
        core = lax.axis_index("seq")
        places = tree_places()
        qkv_part, fc_part = pack(
            jnp.reshape(core, (1,)), qkv_weight, proj_weight.T, fc1_weight, fc2_weight.T, vectors
        )
        qkv_steps, fc_steps = tree_gather(qkv_part), tree_gather(fc_part)
        qkv_hop = next(qkv_steps)
        arrived = swap_cores(tokens)
        table, qkv_hop, arrived = tie(table, qkv_hop, arrived)
        labels, values, mask_keys, mask_queries = table
        qkv_hop = qkv_steps.send(qkv_hop)
        fc_hop = next(fc_steps)
        shifted = enter(tokens, plan, arrived)
        bias_low = bias_half(0, values, wide8, spread)
        qkv_hop, bias_low, shifted, values = tie(qkv_hop, bias_low, shifted, values)
        qkv_hop = qkv_steps.send(qkv_hop)
        arrived = swap_cores(cotangent)
        bias_high = bias_half(1, values, wide8, spread)
        out_grad = enter(cotangent, plan, arrived)
        qkv_hop, bias_high, out_grad, fc_hop = tie(qkv_hop, bias_high, out_grad, fc_hop)
        qkv_own, qkv_other = qkv_steps.send(qkv_steps.send(qkv_hop))
        fc_hop = fc_steps.send(fc_hop)
        q_t, k_t, v_t, token_k, token_v, vecs = project(places, shifted, qkv_own, qkv_other, hidden_width)
        q_t, fc_hop = tie(q_t, fc_hop)
        fc_hop = fc_steps.send(fc_hop)
        low = attend(0, q_t, token_k, v_t, bias_low, mask_queries, mask_keys)
        q_t, low, fc_hop = tie(q_t, low, fc_hop)
        fc_hop = fc_steps.send(fc_hop)
        high = attend(1, q_t, token_k, v_t, bias_high, mask_queries, mask_keys)
        high, fc_hop = tie(high, fc_hop)
        fc_own, fc_other = fc_steps.send(fc_hop)
        block_out, mid_grad, context_grad_t, fc_keep, fc_send, fc_sums = feed(
            places, shifted, low[1], high[1], out_grad, vecs, fc_own, fc_other
        )
        fc_steps = tree_scatter(fc_keep, fc_send)
        fc_hop = next(fc_steps)
        kept, sent = leave(block_out, plan, BF)
        block_out = joined(kept, swap_cores(sent))
        groups = []
        for g in range(width // 128):
            context_t, _, expo, inverse_sum = low if g < 2 else high
            groups.append(
                attend_back(g, expo, k_t, token_v, q_t, context_grad_t, context_t, inverse_sum, spread, wide16)
            )
            if g != 1:
                groups[-1], fc_hop, context_grad_t = tie(groups[-1], fc_hop, context_grad_t)
                fc_hop = fc_steps.send(fc_hop)
            else:
                groups[-1], context_grad_t = tie(groups[-1], context_grad_t)
        input_grad, qkv_keep, qkv_send = input_side(
            places, shifted, groups, mid_grad, vecs, fc_sums, qkv_own, qkv_other
        )
        qkv_steps = tree_scatter(qkv_keep, qkv_send)
        qkv_hop = next(qkv_steps)
        offsets = jnp.concatenate([group[3] for group in groups]).reshape(HEADS, WIDE)
        input_grad, offsets = tie(input_grad, offsets)
        offsets = jnp.sum(lax.all_to_all(offsets, "shard", 0, 0, tiled=True), axis=0)
        qkv_hop, offsets, fc_hop = tie(qkv_hop, offsets, fc_hop)
        qkv_hop = qkv_steps.send(qkv_hop)
        offsets = offsets + swap_cores(offsets)
        own_fc = finish(fc_steps, fc_hop)
        kept, sent = leave(input_grad, plan, F32)
        offsets = to_all(offsets)
        qkv_hop, offsets, kept, sent = tie(qkv_hop, offsets, kept, sent)
        qkv_hop = qkv_steps.send(qkv_hop)
        arrived = swap_cores(sent)
        table_grad = spill(labels, offsets, position_table.shape[0])
        qkv_hop, table_grad, arrived = tie(qkv_hop, table_grad, arrived)
        qkv_hop = qkv_steps.send(qkv_hop)
        input_grad = joined(kept, arrived)
        own_qkv = finish(qkv_steps, qkv_hop)
        small = own_qkv[: VECTOR // 128, width * 3 // 2 :].reshape(-1)
        own_fc, own_qkv = sides(own_fc, core), sides(own_qkv[:, : width * 3 // 2], core)
    else:
        straight = np.arange(16)
        places = jnp.asarray(np.concatenate([straight, straight, straight, straight, np.zeros(1)]), jnp.int32)
        gather = lambda part: lax.all_gather(part, "shard", axis=0, tiled=True)
        halves = lambda part: jnp.split(part, 2, axis=1)
        parts = [halves(gather(part)) for part in (proj_weight.T, fc1_weight, fc2_weight.T)]
        fc_own, fc_other = (jnp.concatenate(pair, axis=1).reshape(16, BLOCK, -1) for pair in zip(*parts))
        rows = lax.all_gather(jnp.concatenate(vectors), "shard", axis=0, tiled=False)
        pieces = [piece.reshape(16, -1) for piece in jnp.split(rows, np.cumsum(sizes)[:-1], axis=1)]
        rows = jnp.pad(jnp.concatenate(pieces, axis=1).reshape(16, -1, 128), ((0, 0), (0, BLOCK - VECTOR // 128), (0, 0)))
        qkv_own, qkv_other = (
            jnp.concatenate([part.reshape(16, BLOCK, -1), rows], axis=2) for part in halves(gather(qkv_weight))
        )
        shifted = enter(tokens, plan, swap_cores(tokens) if levels == 1 else None)
        out_grad = enter(cotangent, plan, swap_cores(cotangent) if levels == 1 else None)
        labels, values, mask_keys, mask_queries = table
        bias_low, bias_high = (bias_half(side, values, wide8, spread) for side in range(2))
        q_t, k_t, v_t, token_k, token_v, vecs = project(places, shifted, qkv_own, qkv_other, hidden_width)
        low = attend(0, q_t, token_k, v_t, bias_low, mask_queries, mask_keys)
        high = attend(1, q_t, token_k, v_t, bias_high, mask_queries, mask_keys)
        block_out, mid_grad, context_grad_t, fc_keep, fc_send, fc_sums = feed(
            places, shifted, low[1], high[1], out_grad, vecs, fc_own, fc_other
        )
        groups = []
        for g in range(width // 128):
            context_t, _, expo, inverse_sum = low if g < 2 else high
            groups.append(
                attend_back(g, expo, k_t, token_v, q_t, context_grad_t, context_t, inverse_sum, spread, wide16)
            )
        input_grad, qkv_keep, qkv_send = input_side(
            places, shifted, groups, mid_grad, vecs, fc_sums, qkv_own, qkv_other
        )
        block_out = leave_any(block_out, plan, clips, BF)
        input_grad = leave_any(input_grad, plan, clips, F32)
        offsets = jnp.concatenate([group[3] for group in groups]).reshape(HEADS, WIDE)
        table_grad = spill(labels, lax.psum(offsets, ("seq", "shard")), position_table.shape[0])
        small = qkv_keep[:, : VECTOR // 128, width * 3 // 2 :].reshape(16, VECTOR)
        small = lax.psum(small.astype(F32), ("seq", "shard"))
        pieces = jnp.split(small, np.cumsum([count for _, count in VEC_LANES.values()])[:-1], axis=1)
        shards = lax.axis_size("shard")
        small = jnp.concatenate([piece.reshape(shards, -1) for piece in pieces], axis=1)
        small = lax.dynamic_index_in_dim(small, lax.axis_index("shard"), 0, keepdims=False)

        def owned(grad):
            grad = lax.psum(grad.reshape(16 * BLOCK, -1), "seq")
            return lax.psum_scatter(grad, "shard", scatter_dimension=0, tiled=True).astype(F32)

        own_fc = [owned(fc_keep), owned(fc_send)]
        own_qkv = [owned(qkv_keep[:, :, : width * 3 // 2]), owned(qkv_send[:, :, : width * 3 // 2])]
    own_proj, own_fc1, own_fc2 = (
        jnp.concatenate(pair, axis=1)
        for pair in zip(*(jnp.split(part, (width // 2, (width + hidden_width) // 2), axis=1) for part in own_fc))
    )
    own_qkv = jnp.concatenate(own_qkv, axis=1)
    own_f1b, own_g1, own_b1, own_qv, own_pb, own_g2, own_b2, own_f2b = jnp.split(small, np.cumsum(sizes)[:-1])
    return (
        block_out, input_grad, own_g1, own_b1, own_qkv, own_qv, table_grad.T, own_proj.T, own_pb,
        own_g2, own_b2, own_fc1, own_f1b, own_fc2.T, own_f2b,
    )


def solution(mesh):
    return jax.shard_map(
        body,
        mesh=mesh,
        in_specs=(
            P("shard", "seq", None, None),
            P("shard"),
            P("shard"),
            P("shard", None),
            P("shard"),
            P(),
            P(None, "shard"),
            P("shard"),
            P("shard"),
            P("shard"),
            P("shard", None),
            P("shard"),
            P(None, "shard"),
            P("shard"),
            P(),
            P("seq", None),
            P("shard", "seq", None, None),
        ),
        out_specs=(
            P("shard", "seq", None, None),
            P("shard", "seq", None, None),
            P("shard"),
            P("shard"),
            P("shard", None),
            P("shard"),
            P(),
            P(None, "shard"),
            P("shard"),
            P("shard"),
            P("shard"),
            P("shard", None),
            P("shard"),
            P(None, "shard"),
            P("shard"),
        ),
        check_vma=False,
    )
```

```python
import functools

import jax
import jax.numpy as jnp
import numpy as np
from jax import lax
from jax.experimental import pallas as pl
from jax.experimental.pallas import tpu as pltpu
from jax.sharding import PartitionSpec as P

HEADS = 16
HEAD_DIM = 32
WT = 8
WH = 7
WW = 7
WIN_TOK = WT * WH * WW
EPS = 1e-05

BF=jnp.bfloat16; F32=jnp.float32
LOG2E=1.4426950408889634; LN2=0.6931471805599453
SCALE=HEAD_DIM**-0.5
BIG=-(2.0**30)
GROUP=4
VM=56*1024*1024

def cost(micros):
    return pl.CostEstimate(flops=int(micros * 1e9), bytes_accessed=int(micros * 3.6e6), transcendentals=0)


def nt(a,b): return lax.dot_general(a,b,(((1,),(1,)),((),())),preferred_element_type=F32)
def nn(a,b): return jnp.dot(a,b,preferred_element_type=F32)

def placed(block, at, rows):
    parts=[]
    if at: parts.append(jnp.zeros((at,block.shape[1]),block.dtype))
    parts.append(block)
    if rows-at-block.shape[0]: parts.append(jnp.zeros((rows-at-block.shape[0],block.shape[1]),block.dtype))
    return jnp.concatenate(parts,axis=0)

PAIR = 2 * GROUP
SAFE = 2.0**60


def attend_kernel(
    q_ref, k_ref, v_ref, bias_ref, mq_ref, mk_ref, ctx_ref, ctx_tok_ref, e_ref, r_ref, scores
):
    n = q_ref.shape[2]
    ones = jnp.ones((16, n), BF)
    mask_rows = placed(mq_ref[0], 0, 128)
    lhs = [jnp.concatenate([k_ref[0, :, 128 * g : 128 * (g + 1)], mk_ref[0]], axis=1) for g in range(2)]
    rows = lambda h: slice(h * HEAD_DIM, (h + 1) * HEAD_DIM)

    def score(h):
        rhs = jnp.concatenate([placed(q_ref[0, rows(h), :], h % GROUP * HEAD_DIM, 128), mask_rows], axis=0)
        scores[h % 2] = nn(lhs[h // GROUP], rhs)

    def context(h):
        c = nn(jnp.concatenate([v_ref[0, rows(h), :], ones], axis=0), e_ref[0, h])
        total = c[HEAD_DIM : HEAD_DIM + 1]
        r = 1.0 / total
        ctx_ref[0, rows(h), :] = (c[:HEAD_DIM] * r).astype(BF)
        r_ref[0, h : h + 1, :] = r
        return total

    totals = []
    score(0)
    for h in range(PAIR):
        if h + 1 < PAIR:
            score(h + 1)
        e_ref[0, h] = jnp.exp(scores[h % 2] + bias_ref[h].astype(F32)).astype(BF)
        if h:
            totals.append(context(h - 1))
    totals.append(context(PAIR - 1))
    every = jnp.concatenate(totals, axis=0)
    ordinary = jnp.logical_and(jnp.min(every) > 1.0 / SAFE, jnp.max(every) < SAFE)

    @pl.when(jnp.logical_not(ordinary))
    def _():
        spot = lax.broadcasted_iota(jnp.int32, (128, n), 0) // HEAD_DIM

        def again(h, carry):
            at = pl.ds(pl.multiple_of(h * HEAD_DIM, HEAD_DIM), HEAD_DIM)
            group = pl.ds(pl.multiple_of(h // GROUP * 128, 128), 128)
            q = jnp.concatenate([q_ref[0, at, :].astype(F32)] * GROUP, axis=0)
            rhs = jnp.where(spot == h % GROUP, q, 0.0).astype(BF)
            s = nn(jnp.concatenate([k_ref[0, :, group], mk_ref[0]], axis=1), jnp.concatenate([rhs, mask_rows], axis=0))
            s = s + bias_ref[h].astype(F32)
            e = jnp.exp(s - jnp.max(s, axis=0, keepdims=True)).astype(BF)
            e_ref[0, h] = e
            c = nn(jnp.concatenate([v_ref[0, at, :], ones], axis=0), e)
            r = 1.0 / c[HEAD_DIM : HEAD_DIM + 1]
            ctx_ref[0, at, :] = (c[:HEAD_DIM] * r).astype(BF)
            r_ref[0, pl.ds(h, 1), :] = r
            return carry

        lax.fori_loop(0, PAIR, again, 0)

    ctx_tok_ref[0] = jnp.transpose(ctx_ref[0].astype(F32)).astype(BF)


def attend(side,qT,k,vT,bias,mq,mk):
    nw,width,n=qT.shape
    half=width//2
    wins=mk.shape[0]
    return pl.pallas_call(
        attend_kernel,
        grid=(nw,),
        in_specs=[
            pl.BlockSpec((1,half,n),lambda w:(w,side,0)),
            pl.BlockSpec((1,n,half),lambda w:(w,0,side)),
            pl.BlockSpec((1,half,n),lambda w:(w,side,0)),
            pl.BlockSpec((PAIR,n,n),lambda w:(0,0,0)),
            pl.BlockSpec((1,32,n),lambda w:(w%wins,0,0)),
            pl.BlockSpec((1,n,128),lambda w:(w%wins,0,0)),
        ],
        out_specs=[
            pl.BlockSpec((1,half,n),lambda w:(w,0,0)),
            pl.BlockSpec((1,n,half),lambda w:(w,0,0)),
            pl.BlockSpec((1,PAIR,n,n),lambda w:(w,0,0,0)),
            pl.BlockSpec((1,PAIR,n),lambda w:(w,0,0)),
        ],
        out_shape=[
            jax.ShapeDtypeStruct((nw,half,n),BF),
            jax.ShapeDtypeStruct((nw,n,half),BF),
            jax.ShapeDtypeStruct((nw,PAIR,n,n),BF),
            jax.ShapeDtypeStruct((nw,PAIR,n),F32),
        ],
        scratch_shapes=[pltpu.VMEM((2,n,n),F32)],
        compiler_params=pltpu.CompilerParams(vmem_limit_bytes=VM),
        name="attend", cost_estimate=cost(10),
    )(qT,k,vT,bias,mq,mk)

SPREAD=768
FLAT=1408
WIDE=2816

def spread_ones():
    n=WT*WH*WW
    tok=np.arange(n); c=tok//(WW*WT); e=tok//WT%WW; a=tok%WT
    out=np.zeros((n,SPREAD),np.float32); out[tok,c*104+e*8+a]=1
    return out

def lane16(mirror):
    out=np.zeros((128,256),np.float32)
    for u in range(16):
        for a in range(8):
            out[u*8+a,u*16+(7-a if mirror else a)]=1
    return out

def back_kernel(
    e_ref, k_ref, v_ref, q_ref, g_ref, ctx_ref, r_ref, sp_ref, l16_ref, dq_ref, dk_ref, dv_ref, tab_ref, tot, acc, prob, low
):
    w = pl.program_id(1)
    nw = pl.num_programs(1)
    first = pl.program_id(0) * GROUP
    n = q_ref.shape[2]
    rows = lambda h: slice(h * HEAD_DIM, (h + 1) * HEAD_DIM)

    @pl.when(w == 0)
    def _():
        tot[...] = jnp.zeros_like(tot)

    grads, inner = [], []
    for h in range(GROUP):
        go = g_ref[0, rows(h), :].astype(F32) * r_ref[0, pl.ds(first + h, 1), :]
        inner.append(jnp.sum(go * ctx_ref[0, rows(h), :].astype(F32), axis=0, keepdims=True))
        grads.append(placed(go.astype(BF), h * HEAD_DIM, 128))

    def prob_grad(h):
        prob[h % 2] = nn(v_ref[0], grads[h])

    dq, dk, dv = [], [], []

    def score_side(h):
        dk.append(nt(low[h % 2], placed(q_ref[0, rows(h), :], h * HEAD_DIM, 128)))
        dq.append(nn(k_ref[0, rows(h), :], low[h % 2]) * SCALE)

    prob_grad(0)
    for h in range(GROUP):
        ds = e_ref[0, h].astype(F32) * (prob[h % 2] - inner[h])
        low[h % 2] = ds.astype(BF)
        tot[h] += ds
        dv.append(nt(e_ref[0, h], grads[h]))
        if h + 1 < GROUP:
            prob_grad(h + 1)
        score_side(h)
    dq_ref[0] = jnp.transpose(jnp.concatenate(dq, axis=0)).astype(BF)
    dv_ref[0] = ((dv[0] + dv[1]) + (dv[2] + dv[3])).astype(BF)
    dk_ref[0] = ((dk[0] + dk[1]) + (dk[2] + dk[3])).astype(BF)

    @pl.when(w==nw-1)
    def _():
        for h in range(GROUP):
            x=nn(tot[h].astype(BF),sp_ref[...])
            full=jnp.zeros((8,FLAT),F32)
            for d in range(WH):
                part=jnp.zeros((8,SPREAD),F32)
                for f in range(WW):
                    j=(d*WW+f)*8
                    part=part+pltpu.roll(x[j:j+8,:],8*(WW-1-f),1) if f<WW-1 else part+x[j:j+8,:]
                wide=jnp.concatenate([part,jnp.zeros((8,FLAT-SPREAD),F32)],axis=1)
                full=full+(pltpu.roll(wide,104*(WH-1-d),1) if d<WH-1 else wide)
            acc[h*8:(h+1)*8,:]=full
        a=acc[...]
        hi=a.astype(BF); lo=(a-hi.astype(F32)).astype(BF)
        wide=[]
        for t in range(FLAT//128):
            c=slice(t*128,(t+1)*128)
            wide.append(nn(hi[:,c],l16_ref[...])+nn(lo[:,c],l16_ref[...]))
        y=jnp.concatenate(wide,axis=1)
        for h in range(GROUP):
            z=pltpu.roll(y[h*8:(h+1)*8,:],0,1,stride=1,stride_axis=0)
            tab_ref[0,h:h+1,:]=jnp.sum(z,axis=0,keepdims=True)

def attend_back(side,e,kT,v,qT,gT,ctxT,r,sp,l16):
    nw,width,n=qT.shape
    feat=pl.BlockSpec((1,128,n),lambda g,w:(w,2*side+g,0))
    tok=pl.BlockSpec((1,n,128),lambda g,w:(w,0,2*side+g))
    own=pl.BlockSpec((1,n,128),lambda g,w:(w,0,g))
    return pl.pallas_call(
        back_kernel,
        grid=(2,nw),
        in_specs=[
            pl.BlockSpec((1,GROUP,n,n),lambda g,w:(w,g,0,0)),
            feat,tok,feat,feat,pl.BlockSpec((1,128,n),lambda g,w:(w,g,0)),
            pl.BlockSpec((1,PAIR,n),lambda g,w:(w,0,0)),
            pl.BlockSpec(sp.shape,lambda g,w:(0,0)),
            pl.BlockSpec(l16.shape,lambda g,w:(0,0)),
        ],
        out_specs=[own,own,own,pl.BlockSpec((1,GROUP,WIDE),lambda g,w:(g,0,0))],
        out_shape=[
            jax.ShapeDtypeStruct((nw,n,256),BF),
            jax.ShapeDtypeStruct((nw,n,256),BF),
            jax.ShapeDtypeStruct((nw,n,256),BF),
            jax.ShapeDtypeStruct((2,GROUP,WIDE),F32),
        ],
        scratch_shapes=[
            pltpu.VMEM((GROUP,n,n),F32),pltpu.VMEM((GROUP*8,FLAT),F32),pltpu.VMEM((2,n,n),F32),pltpu.VMEM((2,n,n),BF),
        ],
        compiler_params=pltpu.CompilerParams(vmem_limit_bytes=VM),
        name="attend_back", cost_estimate=cost(20),
    )(e,kT,v,qT,gT,ctxT,r,sp,l16)

def lane_maps(mirror):
    lane=np.arange(WIDE); pq=lane//16; o=lane%16
    p=pq//13; q=pq%13
    ok=(pq<169)&(o<15)
    if mirror: o=14-o
    A=o>=7; b=np.where(A,14-o,7-o); C=p>=6; d=np.where(C,12-p,6-p); E=q>=6; f=np.where(E,12-q,6-q)
    col=(b*WH+d)*WW+f
    corner=A*4+C*2+E*1
    return np.where(ok,col,-1).astype(np.int32), np.where(ok,corner,-1).astype(np.int32)

CORNER_ROWS=[(a*WH+c)*WW+e for a in (0,WT-1) for c in (0,WH-1) for e in (0,WW-1)]

def prepare_kernel(rel_ref,maps_ref,table_ref,region_ref,order_ref,l8_ref,lab_ref,narrow_ref,mk_ref,mq_ref):
    values=[]
    n=rel_ref.shape[1]
    rel=jnp.concatenate([rel_ref[row:row+1,:] for row in CORNER_ROWS],axis=0)
    hi=(rel>>6).astype(F32).astype(BF); lo=(rel&63).astype(F32).astype(BF)
    both=jnp.concatenate([hi,lo],axis=0)
    corners=lax.broadcasted_iota(jnp.int32,(8,256),0)
    rows=lax.broadcasted_iota(jnp.int32,(n,256),0)
    trow=lax.broadcasted_iota(jnp.int32,(table_ref.shape[1],256),0)
    for t in range(WIDE//256):
        c=slice(t*256,(t+1)*256)
        for version in range(2):
            col=maps_ref[2*version:2*version+1,c]; cor=maps_ref[2*version+1:2*version+2,c]
            m=jnp.where(rows==col,1.0,0.0).astype(BF)
            y=nn(both,m)
            full=y[:8]*64.0+y[8:]
            lab=jnp.sum(jnp.where(corners==cor,full,0.0),axis=0,keepdims=True)
            lab=jnp.where(cor>=0,lab,-1.0).astype(jnp.int32)
            lab_ref[version:version+1,c]=lab
            if version==0:
                hot=jnp.where(trow==lab,1.0,0.0).astype(BF)
                values.append(nn(table_ref[...],hot))
    values=jnp.concatenate(values,axis=1)
    rolled=[]
    for h in range(HEADS):
        line=jnp.broadcast_to(values[h:h+1],(8,WIDE))
        rolled.append(pltpu.roll(line,WIDE-7,1,stride=1,stride_axis=0))
    rolled=jnp.concatenate(rolled,axis=0).astype(BF)
    for t in range(FLAT//128):
        narrow_ref[:,t*128:(t+1)*128]=nn(rolled[:,t*256:(t+1)*256],l8_ref[...])
    wins=region_ref.shape[0]
    region=jnp.concatenate([region_ref[...].astype(F32),jnp.zeros((16-wins,n),F32)],axis=0).astype(BF)
    across=nt(region,order_ref[...])
    down=nt(order_ref[...],region)
    lanes=lax.broadcasted_iota(jnp.int32,(n,128),1).astype(F32)
    subs=lax.broadcasted_iota(jnp.int32,(32,n),0).astype(F32)
    for w in range(wins):
        mk_ref[w]=jnp.where(down[:,w:w+1]==lanes,1.0,0.0).astype(BF)
        mq_ref[w]=jnp.where(across[w:w+1,:]==subs,0.0,BIG).astype(BF)

def prepare(rel_index,maps,table_t,region_ids,order,l8):
    wins,n=region_ids.shape
    return pl.pallas_call(
        prepare_kernel,
        out_shape=[
            jax.ShapeDtypeStruct((2,WIDE),jnp.int32),
            jax.ShapeDtypeStruct((HEADS*8,FLAT),F32),
            jax.ShapeDtypeStruct((wins,n,128),BF),
            jax.ShapeDtypeStruct((wins,32,n),BF),
        ],
        compiler_params=pltpu.CompilerParams(vmem_limit_bytes=VM),
        name="prepare", cost_estimate=cost(6),
    )(rel_index,maps,table_t,region_ids,order,l8)

def bias_kernel(narrow_ref,sp_ref,bias_ref,x_ref):
    heads=bias_ref.shape[0]

    def lay(h):
        narrow=narrow_ref[8*h:8*h+8,:]
        for d in range(WH):
            wide=(pltpu.roll(narrow,FLAT-104*(WH-1-d),1) if d<WH-1 else narrow)[:,:SPREAD]
            for f in range(0,WW-1,2):
                two=[pltpu.roll(wide,SPREAD-8*(WW-1-k),1) for k in (f,f+1)]
                x_ref[h%2,(d*WW+f)*8:(d*WW+f+2)*8,:]=jnp.concatenate(two,axis=0)
            x_ref[h%2,(d*WW+WW-1)*8:(d*WW+WW)*8,:]=wide

    lay(0)
    for h in range(heads):
        bias_ref[h]=nt(x_ref[h%2].astype(BF),sp_ref[...]).astype(BF)
        if h+1<heads:
            lay(h+1)

def bias_half(side,narrow,sp):
    n=sp.shape[0]
    heads=HEADS//2
    step=4
    return pl.pallas_call(
        bias_kernel,
        grid=(heads//step,),
        in_specs=[pl.BlockSpec((8*step,FLAT),lambda h:(side*heads//step+h,0)),pl.BlockSpec(sp.shape,lambda h:(0,0))],
        out_specs=pl.BlockSpec((step,n,n),lambda h:(h,0,0)),
        out_shape=jax.ShapeDtypeStruct((heads,n,n),BF),
        scratch_shapes=[pltpu.VMEM((2,n,SPREAD),F32)],
        compiler_params=pltpu.CompilerParams(vmem_limit_bytes=VM),
        name="position_bias", cost_estimate=cost(6),
    )(narrow,sp)

def spill_kernel(lab_ref,g_ref,out_ref):
    g=g_ref[...]
    hi=g.astype(BF); r1=g-hi.astype(F32); mid=r1.astype(BF); lo=(r1-mid.astype(F32)).astype(BF)
    three=jnp.concatenate([hi,mid,lo],axis=0)
    rows=out_ref.shape[1]
    trow=lax.broadcasted_iota(jnp.int32,(rows,256),0)
    tot=jnp.zeros((48,rows),F32)
    for t in range(WIDE//256):
        c=slice(t*256,(t+1)*256)
        hot=jnp.where(trow==lab_ref[1:2,c],1.0,0.0).astype(BF)
        tot=tot+nt(three[:,c],hot)
    out_ref[...]=tot[:16]+tot[16:32]+tot[32:]

def spill(lab,g,rows):
    return pl.pallas_call(
        spill_kernel,
        out_shape=jax.ShapeDtypeStruct((HEADS,rows),F32),
        compiler_params=pltpu.CompilerParams(vmem_limit_bytes=VM),
        name="table_rows", cost_estimate=cost(5),
    )(lab,g)


BLOCK = 32
B_FC1, B_PROJ, GAIN2, BIAS2, B_FC2, GAIN1, BIAS1, B_QV = range(8)
VEC_LANES = {B_FC1: (0, 128), GAIN1: (128, 32), BIAS1: (160, 32), B_QV: (192, 64), B_PROJ: (256, 32), GAIN2: (288, 32), BIAS2: (320, 32), B_FC2: (352, 32)}
VECTOR = 384


def load_weight(own_ref, other_ref, places_ref, held, sem, vecs=None):
    core = places_ref[64]
    lanes = slice(0, held.shape[2])
    copies = []
    for i in range(16):
        rows = pl.ds(i * BLOCK, BLOCK)
        own = own_ref.at[places_ref[i]]
        copies.append(pltpu.make_async_copy(own.at[:, lanes], held.at[core, rows, :], sem.at[2 * i]))
        copies.append(
            pltpu.make_async_copy(other_ref.at[places_ref[16 + i]].at[:, lanes], held.at[1 - core, rows, :], sem.at[2 * i + 1])
        )
        if vecs is not None:
            copies.append(pltpu.make_async_copy(own.at[0:16, held.shape[2] :], vecs.at[i], sem.at[32 + i]))
    for copy in copies:
        copy.start()
    for copy in copies:
        copy.wait()


def store_grad(total, places_ref, own_ref, send_ref):
    core = places_ref[64]

    def block(i, carry):
        own_ref[i, :, : total.shape[2]] = total[core, pl.ds(pl.multiple_of(places_ref[32 + i] * BLOCK, BLOCK), BLOCK), :].astype(BF)
        send_ref[i, :, : total.shape[2]] = total[1 - core, pl.ds(pl.multiple_of(places_ref[48 + i] * BLOCK, BLOCK), BLOCK), :].astype(BF)
        return carry

    lax.fori_loop(0, 16, block, 0)


def normalise(values):
    mean = jnp.mean(values, axis=-1, keepdims=True)
    centred = values - mean
    inverse = lax.rsqrt(jnp.mean(centred * centred, axis=-1, keepdims=True) + EPS)
    return centred * inverse, inverse


def project_kernel(
    places_ref, x_ref, own_ref, other_ref, q_ref, kt_ref, vt_ref, k_ref, v_ref, vec_ref, held, loose, sem
):
    @pl.when(pl.program_id(0) == 0)
    def _():
        load_weight(own_ref, other_ref, places_ref, held, sem, loose)
        rows = [loose[i].astype(F32) for i in range(16)]
        for name, (at, count) in VEC_LANES.items():
            parts = [row[at // 128 : at // 128 + 1, at % 128 : at % 128 + count] for row in rows]
            vec_ref[name : name + 1, : 16 * count] = jnp.concatenate(parts, axis=1)

    width = x_ref.shape[2]
    normed, _ = normalise(x_ref[0].astype(F32))
    first = (normed * vec_ref[GAIN1 : GAIN1 + 1, :width] + vec_ref[BIAS1 : BIAS1 + 1, :width]).astype(BF)
    left, right = nn(first, held[0]), nn(first, held[1])
    half = width // 2
    q = (left[:, :width] + vec_ref[B_QV : B_QV + 1, :width]) * SCALE
    k = jnp.concatenate([left[:, width:], right[:, :half]], axis=1)
    v = right[:, half:] + vec_ref[B_QV : B_QV + 1, width : 2 * width]
    q_ref[0] = jnp.transpose(q).astype(BF)
    kt_ref[0] = jnp.transpose(k).astype(BF)
    vt_ref[0] = jnp.transpose(v).astype(BF)
    k_ref[0] = k.astype(BF)
    v_ref[0] = v.astype(BF)


def project(places, x, own, other, hidden_width):
    nw, n, width = x.shape
    tok = pl.BlockSpec((1, n, width), lambda w, s: (w, 0, 0))
    feat = pl.BlockSpec((1, width, n), lambda w, s: (w, 0, 0))
    anywhere = pl.BlockSpec(memory_space=pl.ANY)
    vecs = (8, hidden_width)
    return pl.pallas_call(
        project_kernel,
        grid_spec=pltpu.PrefetchScalarGridSpec(
            num_scalar_prefetch=1,
            grid=(nw,),
            in_specs=[tok, anywhere, anywhere],
            out_specs=[feat, feat, feat, tok, tok, pl.BlockSpec(vecs, lambda w, s: (0, 0))],
            scratch_shapes=[
                pltpu.VMEM((2, 16 * BLOCK, own.shape[2] - 128), BF),
                pltpu.VMEM((16, 16, 128), BF),
                pltpu.SemaphoreType.DMA((48,)),
            ],
        ),
        out_shape=[jax.ShapeDtypeStruct((nw, width, n), BF)] * 3
        + [jax.ShapeDtypeStruct((nw, n, width), BF)] * 2
        + [jax.ShapeDtypeStruct(vecs, F32)],
        compiler_params=pltpu.CompilerParams(vmem_limit_bytes=VM),
        name="project", cost_estimate=cost(9),
    )(places, x, own, other)


TAIL = (0.254829592, -0.284496736, 1.421413741, -1.453152027, 1.061405429)


def normal_parts(values):
    t = pl.reciprocal(1.0 + (0.3275911 * 0.7071067811865476) * jnp.abs(values), approx=False)
    series = TAIL[4]
    for factor in TAIL[3::-1]:
        series = series * t + factor
    bell = jnp.exp2(values * values * (-0.5 * LOG2E))
    upper = (0.5 * t) * series * bell
    return jnp.where(values >= 0, 1.0 - upper, upper), bell * 0.3989422804014327


def column_sums(values):
    return jnp.sum(values, axis=0, keepdims=True)


def feed_kernel(
    places_ref, x_ref, ctx0_ref, ctx1_ref, og_ref, vec_ref, own_ref, other_ref, out_ref, mid_grad_ref, gt_ref, own_grad_ref,
    send_grad_ref, sums_ref, held, total, wide, thin, sem,
):
    step = pl.program_id(0)

    @pl.when(step == 0)
    def _():
        total[...] = jnp.zeros_like(total)
        sums_ref[...] = jnp.zeros_like(sums_ref)
        load_weight(own_ref, other_ref, places_ref, held, sem)

    width = x_ref.shape[2]
    half = width // 2
    chunk = (held.shape[2] - half) // 2
    vec = lambda row: vec_ref[row : row + 1, :width]
    ctx = (ctx0_ref[0], ctx1_ref[0])
    branch = nt(ctx[0], held[0, :, :half]) + nt(ctx[1], held[1, :, :half])
    mid = x_ref[0].astype(F32) + (branch + vec(B_PROJ))
    normed, inverse = normalise(mid)
    second = normed * vec(GAIN2) + vec(BIAS2)
    second_t = jnp.transpose(second).astype(BF)
    second = second.astype(BF)
    og = og_ref[0]
    og_t = jnp.transpose(og.astype(F32)).astype(BF)
    mlp = jnp.zeros(mid.shape, F32)
    second_grad = jnp.zeros(mid.shape, F32)
    piece = chunk // 2
    cuts = []
    for j in range(2):
        for part in range(2):
            at = half + part * piece
            cuts.append((j, slice(at, at + piece), slice(at + chunk, at + chunk + piece), slice(j * chunk + part * piece, j * chunk + (part + 1) * piece)))

    def widen(i):
        j, c1, c2, cols = cuts[i]
        wide[0, i % 2] = nn(second, held[j, :, c1]) + vec_ref[B_FC1 : B_FC1 + 1, cols]
        wide[1, i % 2] = nn(og, held[j, :, c2])

    widen(0)
    for i, (j, c1, c2, cols) in enumerate(cuts):
        hidden = wide[0, i % 2]
        phi_sum, density = normal_parts(hidden)
        thin[0, i % 2] = (hidden * phi_sum).astype(BF)
        hidden_grad = wide[1, i % 2] * (phi_sum + hidden * density)
        sums_ref[0:1, cols] += column_sums(hidden_grad)
        thin[1, i % 2] = hidden_grad.astype(BF)
        if i + 1 < len(cuts):
            widen(i + 1)
        mlp += nt(thin[0, i % 2], held[j, :, c2])
        second_grad += nt(thin[1, i % 2], held[j, :, c1])
        total[j, :, c1] += nn(second_t, thin[1, i % 2])
        total[j, :, c2] += nn(og_t, thin[0, i % 2])
    out_ref[0] = (mid + (mlp + vec(B_FC2))).astype(BF)
    scaled = second_grad * vec(GAIN2)
    inner = jnp.mean(scaled, axis=-1, keepdims=True)
    along = jnp.mean(scaled * normed, axis=-1, keepdims=True)
    og = og.astype(F32)
    mid_grad = og + inverse * (scaled - inner - normed * along)
    mid_grad_ref[0] = mid_grad
    low = mid_grad.astype(BF)
    sums_ref[1:2, :width] += column_sums(mid_grad)
    sums_ref[2:3, :width] += column_sums(second_grad * normed)
    sums_ref[3:4, :width] += column_sums(second_grad)
    sums_ref[4:5, :width] += column_sums(og)
    low_t = jnp.transpose(mid_grad).astype(BF)
    for j in range(2):
        total[j, :, :half] += nn(low_t, ctx[j])
        proj = jnp.transpose(held[j, :, :half].astype(F32)).astype(BF)
        gt_ref[0, j * half : (j + 1) * half, :] = nn(proj, low_t).astype(BF)

    @pl.when(step == pl.num_programs(0) - 1)
    def _():
        store_grad(total, places_ref, own_grad_ref, send_grad_ref)


def feed(places, x, ctx0, ctx1, og, vecs, own, other):
    nw, n, width = x.shape
    tok = pl.BlockSpec((1, n, width), lambda w, s: (w, 0, 0))
    feat = pl.BlockSpec((1, width, n), lambda w, s: (w, 0, 0))
    whole = pl.BlockSpec(own.shape, lambda w, s: (0, 0, 0))
    anywhere = pl.BlockSpec(memory_space=pl.ANY)
    side = pl.BlockSpec((1, n, width // 2), lambda w, s: (w, 0, 0))
    hidden_width = own.shape[2] - width // 2
    return pl.pallas_call(
        feed_kernel,
        grid_spec=pltpu.PrefetchScalarGridSpec(
            num_scalar_prefetch=1,
            grid=(nw,),
            in_specs=[tok, side, side, tok, pl.BlockSpec(vecs.shape, lambda w, s: (0, 0)), anywhere, anywhere],
            out_specs=[tok, tok, feat, whole, whole, pl.BlockSpec((8, hidden_width), lambda w, s: (0, 0))],
            scratch_shapes=[
                pltpu.VMEM((2, 16 * BLOCK, own.shape[2]), BF),
                pltpu.VMEM((2, 16 * BLOCK, own.shape[2]), F32),
                pltpu.VMEM((2, 2, n, hidden_width // 4), F32),
                pltpu.VMEM((2, 2, n, hidden_width // 4), BF),
                pltpu.SemaphoreType.DMA((32,)),
            ],
        ),
        out_shape=[
            jax.ShapeDtypeStruct((nw, n, width), BF),
            jax.ShapeDtypeStruct((nw, n, width), F32),
            jax.ShapeDtypeStruct((nw, width, n), BF),
            jax.ShapeDtypeStruct(own.shape, BF),
            jax.ShapeDtypeStruct(own.shape, BF),
            jax.ShapeDtypeStruct((8, hidden_width), F32),
        ],
        compiler_params=pltpu.CompilerParams(vmem_limit_bytes=VM),
        name="feed_forward", cost_estimate=cost(44),
    )(places, x, ctx0, ctx1, og, vecs, own, other)


def input_kernel(
    places_ref, x_ref, dq0, dk0, dv0, dq1, dk1, dv1, mid_grad_ref, vec_ref, fc_sums_ref,
    own_ref, other_ref, out_ref, own_grad_ref, send_grad_ref, held, total, sums, small, sem,
):
    step = pl.program_id(0)

    @pl.when(step == 0)
    def _():
        total[...] = jnp.zeros_like(total)
        sums[...] = jnp.zeros_like(sums)
        load_weight(own_ref, other_ref, places_ref, held, sem)

    width = x_ref.shape[2]
    half = width // 2
    vec = lambda row: vec_ref[row : row + 1, :width]
    normed, inverse = normalise(x_ref[0].astype(F32))
    first_t = jnp.transpose(normed * vec(GAIN1) + vec(BIAS1)).astype(BF)
    left = jnp.concatenate([dq0[0], dq1[0], dk0[0]], axis=1)
    right = jnp.concatenate([dk1[0], dv0[0], dv1[0]], axis=1)
    total[0] += nn(first_t, left)
    total[1] += nn(first_t, right)
    first_grad = (nt(left, held[0]) + nt(right, held[1])).astype(BF).astype(F32)
    scaled = first_grad * vec(GAIN1)
    inner = jnp.mean(scaled, axis=-1, keepdims=True)
    along = jnp.mean(scaled * normed, axis=-1, keepdims=True)
    out_ref[0] = (mid_grad_ref[0] + inverse * (scaled - inner - normed * along)).astype(BF)
    sums[0:1, :width] += column_sums(first_grad * normed)
    sums[1:2, :width] += column_sums(first_grad)
    sums[2:3, :width] += column_sums(left[:, :width].astype(F32))
    sums[2:3, width:] += column_sums(right[:, half:].astype(F32))

    @pl.when(step == pl.num_programs(0) - 1)
    def _():
        columns = total.shape[2]
        store_grad(total, places_ref, own_grad_ref, send_grad_ref)
        rows = {
            B_FC1: fc_sums_ref[0:1, :], B_PROJ: fc_sums_ref[1:2, :], GAIN2: fc_sums_ref[2:3, :], BIAS2: fc_sums_ref[3:4, :],
            B_FC2: fc_sums_ref[4:5, :], GAIN1: sums[0:1, :], BIAS1: sums[1:2, :], B_QV: sums[2:3, :],
        }
        for i in range(16):
            parts = [rows[name][:, i * count : (i + 1) * count] for name, (_, count) in VEC_LANES.items()]
            line = jnp.concatenate(parts, axis=1)
            small[i] = jnp.concatenate([line[:, :128], line[:, 128:256], line[:, 256:], jnp.zeros((BLOCK - 3, 128), F32)], axis=0)

        def block(i, carry):
            own_grad_ref[i, :, columns:] = small[places_ref[32 + i]].astype(BF)
            send_grad_ref[i, :, columns:] = small[places_ref[48 + i]].astype(BF)
            return carry

        lax.fori_loop(0, 16, block, 0)


def input_side(places, x, groups, mid_grad, vecs, fc_sums, own, other):
    nw, n, width = x.shape
    tok = pl.BlockSpec((1, n, width), lambda w, s: (w, 0, 0))
    part = pl.BlockSpec((1, n, width // 2), lambda w, s: (w, 0, 0))
    flat = lambda shape: pl.BlockSpec(shape, lambda w, s: (0,) * len(shape))
    anywhere = pl.BlockSpec(memory_space=pl.ANY)
    columns = own.shape[2] - 128
    grad = own.shape
    return pl.pallas_call(
        input_kernel,
        grid_spec=pltpu.PrefetchScalarGridSpec(
            num_scalar_prefetch=1,
            grid=(nw,),
            in_specs=[tok] + [part] * 6 + [tok, flat(vecs.shape), flat(fc_sums.shape), anywhere, anywhere],
            out_specs=[tok, flat(grad), flat(grad)],
            scratch_shapes=[
                pltpu.VMEM((2, 16 * BLOCK, columns), BF),
                pltpu.VMEM((2, 16 * BLOCK, columns), F32),
                pltpu.VMEM((8, 2 * width), F32),
                pltpu.VMEM((16, BLOCK, 128), F32),
                pltpu.SemaphoreType.DMA((32,)),
            ],
        ),
        out_shape=[
            jax.ShapeDtypeStruct((nw, n, width), BF),
            jax.ShapeDtypeStruct(grad, BF),
            jax.ShapeDtypeStruct(grad, BF),
        ],
        compiler_params=pltpu.CompilerParams(vmem_limit_bytes=VM),
        name="input_side", cost_estimate=cost(15),
    )(places, x, *[part for group in groups for part in group[:3]], mid_grad, vecs, fc_sums, own, other)


def from_partner(shard, axis, stride):
    return lax.ppermute(shard, axis, [(i, i ^ 1 << stride) for i in range(lax.axis_size(axis))])


def to_block(windows, local_count):
    clip_count, chans = (windows.shape[0], windows.shape[-1])
    parted = windows.reshape(
        clip_count, local_count[0], local_count[1], local_count[2], WT, WH, WW, chans
    )
    parted = parted.transpose(0, 1, 4, 2, 5, 3, 6, 7)
    return parted.reshape(
        clip_count, local_count[0] * WT, local_count[1] * WH, local_count[2] * WW, chans
    )


def from_block(block, local_count):
    clip_count, chans = (block.shape[0], block.shape[-1])
    parted = block.reshape(
        clip_count, local_count[0], WT, local_count[1], WH, local_count[2], WW, chans
    )
    parted = parted.transpose(0, 1, 3, 5, 2, 4, 6, 7)
    return parted.reshape(clip_count, -1, WT * WH * WW, chans)


def roll_ahead(windows, local_count, bit_list):
    block = to_block(windows, local_count)
    for grid_dim, amount, bit_pos in (
        (1, WT // 2, bit_list[0]),
        (2, WH // 2, bit_list[1]),
        (3, WW // 2, bit_list[2]),
    ):
        if bit_pos < 0:
            block = jnp.roll(block, -amount, axis=grid_dim)
        else:
            front = lax.slice_in_dim(block, 0, amount, axis=grid_dim)
            arrived = from_partner(front, "seq", bit_pos)
            rest = lax.slice_in_dim(block, amount, block.shape[grid_dim], axis=grid_dim)
            block = jnp.concatenate([rest, arrived], axis=grid_dim)
    return from_block(block, local_count)


def roll_behind(windows, local_count, bit_list):
    block = to_block(windows, local_count)
    for grid_dim, amount, bit_pos in (
        (1, WT // 2, bit_list[0]),
        (2, WH // 2, bit_list[1]),
        (3, WW // 2, bit_list[2]),
    ):
        if bit_pos < 0:
            block = jnp.roll(block, amount, axis=grid_dim)
        else:
            extent = block.shape[grid_dim]
            trailing = lax.slice_in_dim(block, extent - amount, extent, axis=grid_dim)
            arrived = from_partner(trailing, "seq", bit_pos)
            rest = lax.slice_in_dim(block, 0, extent - amount, axis=grid_dim)
            block = jnp.concatenate([arrived, rest], axis=grid_dim)
    return from_block(block, local_count)


KEEP = WT // 2 * WH * WW


def hwt_order():
    place = np.arange(WIN_TOK)
    return (place % WT * WH + place // (WW * WT)) * WW + place // WT % WW


def order_ones(shift):
    place = np.arange(WIN_TOK)
    out = np.zeros((WIN_TOK, WIN_TOK), np.float32)
    out[place, ((place + shift) % WT * WH + place // (WW * WT)) * WW + place // WT % WW] = 1
    return out


def tile_runs(win):
    runs = []
    for c in range(WH):
        h = (win // 2 * WH + c + WH // 2) % (2 * WH)
        for e, count in ((0, WW - WW // 2), (WW - WW // 2, WW // 2)):
            w = (win % 2 * WW + e + WW // 2) % (2 * WW)
            runs.append((h // WH * 2 + w // WW, h % WH * WW + w % WW, count))
    return runs


def swap_cores(part):
    return lax.ppermute(part, "seq", [(0, 1), (1, 0)])


def enter_kernel(own_ref, arrived_ref, order_ref, out_ref, held):
    _, n, width = own_ref.shape
    rows = lax.broadcasted_iota(jnp.int32, (n, width), 0)
    for source in range(4):
        values = jnp.where(rows >= KEEP, own_ref[source].astype(F32), arrived_ref[source].astype(F32)).astype(BF)
        held[source] = nn(order_ref[...], values)
    for win in range(4):
        parts = [held[source, 8 * at : 8 * (at + count), :] for source, at, count in tile_runs(win)]
        out_ref[win] = jnp.concatenate(parts, axis=0).astype(BF)


def leave_kernel(rows_ref, order_ref, out_ref, send_ref, held):
    for win in range(4):
        values = rows_ref[win].astype(F32)
        start = 0
        for source, at, count in tile_runs(win):
            held[source, 8 * at : 8 * (at + count), :] = values[8 * start : 8 * (start + count), :]
            start += count
    for source in range(4):
        values = nn(order_ref[...], held[source].astype(BF)).astype(out_ref.dtype)
        out_ref[source] = values
        send_ref[source] = values[: send_ref.shape[1]].astype(BF)


SENT = 208


def enter(windows, plan, arrived=None):
    clips, wins, toks, width = windows.shape
    if plan["levels"] == 1 and clips == 1:
        own = windows.reshape(wins, toks, width)
        return pl.pallas_call(
            enter_kernel,
            out_shape=jax.ShapeDtypeStruct(own.shape, BF),
            scratch_shapes=[pltpu.VMEM(own.shape, F32)],
            compiler_params=pltpu.CompilerParams(vmem_limit_bytes=VM),
            name="enter", cost_estimate=cost(4),
        )(own, arrived.reshape(own.shape), plan["order"])
    rolled = roll_ahead(windows, plan["local"], plan["bits"])
    rolled = rolled.reshape(clips * wins, WT, WH * WW, width).transpose(0, 2, 1, 3)
    return rolled.reshape(clips * wins, toks, width)


def leave(windows, plan, kind):
    wins, toks, width = windows.shape
    return pl.pallas_call(
        leave_kernel,
        out_shape=[jax.ShapeDtypeStruct(windows.shape, kind), jax.ShapeDtypeStruct((wins, SENT, width), BF)],
        scratch_shapes=[pltpu.VMEM(windows.shape, F32)],
        compiler_params=pltpu.CompilerParams(vmem_limit_bytes=VM),
        name="leave", cost_estimate=cost(4),
    )(windows, plan["order"].T)


def joined(kept, arrived):
    arrived = jnp.pad(arrived.astype(kept.dtype), ((0, 0), (0, kept.shape[1] - SENT), (0, 0)))
    rows = lax.broadcasted_iota(jnp.int32, kept.shape, 1)
    return jnp.where(rows < KEEP, arrived, kept)[None]


def leave_any(windows, plan, clips, kind):
    count, toks, width = windows.shape
    wins = count // clips
    if plan["levels"] == 1 and clips == 1:
        kept, sent = leave(windows, plan, kind)
        return joined(kept, swap_cores(sent))
    rows = windows.reshape(count, WH * WW, WT, width).transpose(0, 2, 1, 3)
    return roll_behind(rows.reshape(clips, wins, toks, width), plan["local"], plan["bits"]).astype(kind)


def pack_kernel(core_ref, qkv_ref, proj_ref, fc1_ref, fc2_ref, *rest):
    vec_refs, (qkv_out, fc_out) = rest[:-2], rest[-2:]

    def emit(side):
        half = qkv_ref.shape[1] // 2
        qkv_out[:, :half] = qkv_ref[:, side * half : (side + 1) * half]
        at = 0
        for ref in (proj_ref, fc1_ref, fc2_ref):
            half = ref.shape[1] // 2
            fc_out[:, at : at + half] = ref[:, side * half : (side + 1) * half]
            at += half

    half = qkv_ref.shape[1] // 2
    line = jnp.concatenate([ref[...].astype(F32).reshape(1, -1) for ref in vec_refs], axis=1)
    lines = [line[:, at : at + 128] for at in range(0, VECTOR, 128)]
    qkv_out[:, half:] = jnp.concatenate(lines + [jnp.zeros((BLOCK - len(lines), 128), F32)], axis=0).astype(BF)
    for side in range(2):
        @pl.when(core_ref[0] == side)
        def _():
            emit(side)


def pack(core, qkv, proj_t, fc1, fc2_t, vectors):
    columns = (proj_t.shape[1] + fc1.shape[1] + fc2_t.shape[1]) // 2
    vmem = pl.BlockSpec(memory_space=pltpu.VMEM)
    return pl.pallas_call(
        pack_kernel,
        in_specs=[pl.BlockSpec(memory_space=pltpu.SMEM)] + [vmem] * (4 + len(vectors)),
        out_shape=[
            jax.ShapeDtypeStruct((BLOCK, qkv.shape[1] // 2 + 128), BF),
            jax.ShapeDtypeStruct((BLOCK, columns), BF),
        ],
        compiler_params=pltpu.CompilerParams(vmem_limit_bytes=VM),
        name="pack", cost_estimate=cost(2),
    )(core, qkv, proj_t, fc1, fc2_t, *vectors)


def hop(part, flips):
    pairs = [(16 * c + s, 16 * c + (s ^ flips[c])) for c in range(2) for s in range(16)]
    return lax.ppermute(part, ("seq", "shard"), pairs)


def tree_places():
    me = lax.axis_index("shard")
    core = lax.axis_index("seq")
    entry = jnp.arange(16, dtype=jnp.int32)
    v, u, z = entry // 8, entry // 4 % 2, entry % 4
    straight, crossed = me ^ (4 * z + 2 * u + v), me ^ (4 * z + 2 * v + u)
    rel = me ^ entry
    z, y, x = rel // 4, rel // 2 % 2, rel % 2
    place_straight, place_crossed = x * 8 + y * 4 + z, y * 8 + x * 4 + z
    even = core == 0
    pick_core = lambda left, right: jnp.where(even, left, right)
    return jnp.concatenate(
        [
            pick_core(place_straight, place_crossed),
            pick_core(place_crossed, place_straight),
            pick_core(straight, crossed),
            pick_core(crossed, straight),
            jnp.broadcast_to(core, (1,)),
        ]
    ).astype(jnp.int32)


def tree_gather(part):
    arrived = yield [hop(part, (4 * k, 4 * k)) for k in range(1, 4)]
    stack = jnp.stack([part] + arrived)
    arrived = yield hop(stack, (2, 1))
    stack = jnp.concatenate([stack, arrived])
    arrived = yield hop(stack, (1, 2))
    stack = jnp.concatenate([stack, arrived])
    other = yield swap_cores(stack)
    yield stack, other


def tie(*items):
    return lax.optimization_barrier(items)


def add_low(left, right):
    return (left.astype(F32) + right.astype(F32)).astype(BF)


def tree_scatter(own, send):
    arrived = yield swap_cores(send)
    stack = add_low(own, arrived)
    arrived = yield hop(stack[8:], (1, 2))
    stack = add_low(stack[:8], arrived)
    arrived = yield hop(stack[4:], (2, 1))
    stack = add_low(stack[:4], arrived)
    arrived = yield [hop(stack[k], (4 * k, 4 * k)) for k in range(1, 4)]
    arrived = [part.astype(F32) for part in arrived]
    yield (stack[0].astype(F32) + arrived[0]) + (arrived[1] + arrived[2])


def finish(steps, pending):
    while True:
        try:
            pending = steps.send(pending)
        except StopIteration:
            return pending


def table_sum(table):
    for axis, flip in (("seq", 1), ("shard", 1), ("shard", 2), ("shard", 4), ("shard", 8)):
        pairs = [(i, i ^ flip) for i in range(2 if axis == "seq" else 16)]
        arrived = yield lax.ppermute(table, axis, pairs)
        table = add_low(table, arrived)
    yield table


def sides(part, core):
    other = swap_low(part)
    return [jnp.where(core == 0, part, other), jnp.where(core == 0, other, part)]


def swap_low(part):
    return swap_cores(part.astype(BF)).astype(F32)


def to_all(part):
    return lax.all_to_all(jnp.broadcast_to(part[None], (lax.axis_size("shard"),) + part.shape), "shard", 0, 0, tiled=True)


def body(
    tokens, norm1_gain, norm1_bias, qkv_weight, qv_bias, position_table, proj_weight, proj_bias, norm2_gain,
    norm2_bias, fc1_weight, fc1_bias, fc2_weight, fc2_bias, rel_index, region_ids, cotangent,
):
    levels = lax.axis_size("seq").bit_length() - 1
    clips, wins, toks, width = tokens.shape
    hidden_width = fc1_weight.shape[1]
    plan = {
        "levels": levels,
        "local": [1 if levels > level_pos else 2 for level_pos in range(3)],
        "bits": [levels - 1 - level_pos for level_pos in range(3)],
        "order": jnp.asarray(order_ones(WT // 2), BF),
    }
    vectors = [fc1_bias, norm1_gain, norm1_bias, qv_bias, proj_bias, norm2_gain, norm2_bias, fc2_bias]
    sizes = [part.shape[0] for part in vectors]
    spread = jnp.asarray(spread_ones(), BF)
    wide8 = jnp.asarray(lane16(False).T, BF)
    wide16 = jnp.asarray(lane16(True), BF)
    maps = jnp.asarray(np.stack(lane_maps(False) + lane_maps(True)))
    table = prepare(rel_index, maps, position_table.T, region_ids, jnp.asarray(order_ones(0), BF), wide8)
    if clips == 1 and lax.axis_size("shard") == 16 and lax.axis_size("seq") == 2:
        core = lax.axis_index("seq")
        places = tree_places()
        qkv_part, fc_part = pack(
            jnp.reshape(core, (1,)), qkv_weight, proj_weight.T, fc1_weight, fc2_weight.T, vectors
        )
        qkv_steps, fc_steps = tree_gather(qkv_part), tree_gather(fc_part)
        qkv_hop = next(qkv_steps)
        arrived = swap_cores(tokens)
        table, qkv_hop, arrived = tie(table, qkv_hop, arrived)
        labels, narrow, mask_keys, mask_queries = table
        qkv_hop = qkv_steps.send(qkv_hop)
        shifted = enter(tokens, plan, arrived)
        qkv_hop, shifted, narrow, fc_part = tie(qkv_hop, shifted, narrow, fc_part)
        qkv_hop = qkv_steps.send(qkv_hop)
        fc_hop = next(fc_steps)
        bias_low = bias_half(0, narrow, spread)
        arrived = swap_cores(cotangent)
        qkv_hop, bias_low, arrived, narrow = tie(qkv_hop, bias_low, arrived, narrow)
        qkv_hop = qkv_steps.send(qkv_hop)
        bias_high = bias_half(1, narrow, spread)
        out_grad = enter(cotangent, plan, arrived)
        qkv_hop, bias_high, out_grad, fc_hop = tie(qkv_hop, bias_high, out_grad, fc_hop)
        qkv_own, qkv_other = qkv_steps.send(qkv_hop)
        fc_hop = fc_steps.send(fc_hop)
        q_t, k_t, v_t, token_k, token_v, vecs = project(places, shifted, qkv_own, qkv_other, hidden_width)
        q_t, fc_hop = tie(q_t, fc_hop)
        fc_hop = fc_steps.send(fc_hop)
        low = attend(0, q_t, token_k, v_t, bias_low, mask_queries, mask_keys)
        q_t, low, fc_hop = tie(q_t, low, fc_hop)
        fc_hop = fc_steps.send(fc_hop)
        high = attend(1, q_t, token_k, v_t, bias_high, mask_queries, mask_keys)
        high, fc_hop = tie(high, fc_hop)
        fc_own, fc_other = fc_steps.send(fc_hop)
        block_out, mid_grad, context_grad_t, fc_keep, fc_send, fc_sums = feed(
            places, shifted, low[1], high[1], out_grad, vecs, fc_own, fc_other
        )
        fc_steps = tree_scatter(fc_keep, fc_send)
        fc_hop = next(fc_steps)
        groups = []
        for side, (context_t, _, expo, inverse_sum) in enumerate((low, high)):
            group = attend_back(
                side, expo, k_t, token_v, q_t, context_grad_t, context_t, inverse_sum, spread, wide16
            )
            group, fc_hop, context_grad_t, block_out = tie(group, fc_hop, context_grad_t, block_out)
            groups.append(group)
            fc_hop = fc_steps.send(fc_hop)
        offsets = jnp.concatenate([group[3] for group in groups]).reshape(HEADS, WIDE)
        table_steps = table_sum(offsets.astype(BF))
        table_hop = next(table_steps)
        input_grad, qkv_keep, qkv_send = input_side(
            places, shifted, groups, mid_grad, vecs, fc_sums, qkv_own, qkv_other
        )
        input_grad, qkv_send, fc_hop, table_hop, block_out = tie(input_grad, qkv_send, fc_hop, table_hop, block_out)
        qkv_steps = tree_scatter(qkv_keep, qkv_send)
        qkv_hop = next(qkv_steps)
        fc_hop = fc_steps.send(fc_hop)
        table_hop = table_steps.send(table_hop)
        kept, sent = leave(input_grad, plan, F32)
        qkv_hop, table_hop, kept, sent, block_out = tie(qkv_hop, table_hop, kept, sent, block_out)
        qkv_hop = qkv_steps.send(qkv_hop)
        table_hop = table_steps.send(table_hop)
        arrived = swap_cores(sent)
        out_kept, out_sent = leave(block_out, plan, BF)
        qkv_hop, table_hop, fc_hop, arrived, out_kept, out_sent = tie(qkv_hop, table_hop, fc_hop, arrived, out_kept, out_sent)
        qkv_hop = qkv_steps.send(qkv_hop)
        table_hop = table_steps.send(table_hop)
        own_fc = finish(fc_steps, fc_hop)
        out_arrived = swap_cores(out_sent)
        own_fc = sides(own_fc, core)
        input_grad = joined(kept, arrived)
        qkv_hop, table_hop, input_grad, own_fc = tie(qkv_hop, table_hop, input_grad, own_fc)
        qkv_hop = qkv_steps.send(qkv_hop)
        offsets = finish(table_steps, table_hop)
        block_out = joined(out_kept, out_arrived)
        table_grad = spill(labels, offsets.astype(F32), position_table.shape[0])
        own_qkv = finish(qkv_steps, qkv_hop)
        small = own_qkv[: VECTOR // 128, width * 3 // 2 :].reshape(-1)
        own_qkv = sides(own_qkv[:, : width * 3 // 2], core)
    else:
        straight = np.arange(16)
        places = jnp.asarray(np.concatenate([straight, straight, straight, straight, np.zeros(1)]), jnp.int32)
        gather = lambda part: lax.all_gather(part, "shard", axis=0, tiled=True)
        halves = lambda part: jnp.split(part, 2, axis=1)
        parts = [halves(gather(part)) for part in (proj_weight.T, fc1_weight, fc2_weight.T)]
        fc_own, fc_other = (jnp.concatenate(pair, axis=1).reshape(16, BLOCK, -1) for pair in zip(*parts))
        rows = lax.all_gather(jnp.concatenate(vectors), "shard", axis=0, tiled=False)
        pieces = [piece.reshape(16, -1) for piece in jnp.split(rows, np.cumsum(sizes)[:-1], axis=1)]
        rows = jnp.pad(jnp.concatenate(pieces, axis=1).reshape(16, -1, 128), ((0, 0), (0, BLOCK - VECTOR // 128), (0, 0)))
        qkv_own, qkv_other = (
            jnp.concatenate([part.reshape(16, BLOCK, -1), rows], axis=2) for part in halves(gather(qkv_weight))
        )
        shifted = enter(tokens, plan, swap_cores(tokens) if levels == 1 else None)
        out_grad = enter(cotangent, plan, swap_cores(cotangent) if levels == 1 else None)
        labels, narrow, mask_keys, mask_queries = table
        bias_low, bias_high = (bias_half(side, narrow, spread) for side in range(2))
        q_t, k_t, v_t, token_k, token_v, vecs = project(places, shifted, qkv_own, qkv_other, hidden_width)
        low = attend(0, q_t, token_k, v_t, bias_low, mask_queries, mask_keys)
        high = attend(1, q_t, token_k, v_t, bias_high, mask_queries, mask_keys)
        block_out, mid_grad, context_grad_t, fc_keep, fc_send, fc_sums = feed(
            places, shifted, low[1], high[1], out_grad, vecs, fc_own, fc_other
        )
        groups = [
            attend_back(side, expo, k_t, token_v, q_t, context_grad_t, context_t, inverse_sum, spread, wide16)
            for side, (context_t, _, expo, inverse_sum) in enumerate((low, high))
        ]
        input_grad, qkv_keep, qkv_send = input_side(
            places, shifted, groups, mid_grad, vecs, fc_sums, qkv_own, qkv_other
        )
        block_out = leave_any(block_out, plan, clips, BF)
        input_grad = leave_any(input_grad, plan, clips, F32)
        offsets = jnp.concatenate([group[3] for group in groups]).reshape(HEADS, WIDE)
        table_grad = spill(labels, lax.psum(offsets, ("seq", "shard")), position_table.shape[0])
        small = qkv_keep[:, : VECTOR // 128, width * 3 // 2 :].reshape(16, VECTOR)
        small = lax.psum(small.astype(F32), ("seq", "shard"))
        pieces = jnp.split(small, np.cumsum([count for _, count in VEC_LANES.values()])[:-1], axis=1)
        shards = lax.axis_size("shard")
        small = jnp.concatenate([piece.reshape(shards, -1) for piece in pieces], axis=1)
        small = lax.dynamic_index_in_dim(small, lax.axis_index("shard"), 0, keepdims=False)

        def owned(grad):
            grad = lax.psum(grad.reshape(16 * BLOCK, -1), "seq")
            return lax.psum_scatter(grad, "shard", scatter_dimension=0, tiled=True).astype(F32)

        own_fc = [owned(fc_keep), owned(fc_send)]
        own_qkv = [owned(qkv_keep[:, :, : width * 3 // 2]), owned(qkv_send[:, :, : width * 3 // 2])]
    own_proj, own_fc1, own_fc2 = (
        jnp.concatenate(pair, axis=1)
        for pair in zip(*(jnp.split(part, (width // 2, (width + hidden_width) // 2), axis=1) for part in own_fc))
    )
    own_qkv = jnp.concatenate(own_qkv, axis=1)
    own_f1b, own_g1, own_b1, own_qv, own_pb, own_g2, own_b2, own_f2b = jnp.split(small, np.cumsum(sizes)[:-1])
    return (
        block_out, input_grad, own_g1, own_b1, own_qkv, own_qv, table_grad.T, own_proj.T, own_pb,
        own_g2, own_b2, own_fc1, own_f1b, own_fc2.T, own_f2b,
    )


def solution(mesh):
    return jax.shard_map(
        body,
        mesh=mesh,
        in_specs=(
            P("shard", "seq", None, None),
            P("shard"),
            P("shard"),
            P("shard", None),
            P("shard"),
            P(),
            P(None, "shard"),
            P("shard"),
            P("shard"),
            P("shard"),
            P("shard", None),
            P("shard"),
            P(None, "shard"),
            P("shard"),
            P(),
            P("seq", None),
            P("shard", "seq", None, None),
        ),
        out_specs=(
            P("shard", "seq", None, None),
            P("shard", "seq", None, None),
            P("shard"),
            P("shard"),
            P("shard", None),
            P("shard"),
            P(),
            P(None, "shard"),
            P("shard"),
            P("shard"),
            P("shard"),
            P("shard", None),
            P("shard"),
            P(None, "shard"),
            P("shard"),
        ),
        check_vma=False,
    )
```

```python
import functools

import jax
import jax.numpy as jnp
import numpy as np
from jax import lax
from jax.experimental import pallas as pl
from jax.experimental.pallas import tpu as pltpu
from jax.sharding import PartitionSpec as P

HEADS = 16
HEAD_DIM = 32
WT = 8
WH = 7
WW = 7
WIN_TOK = WT * WH * WW
EPS = 1e-05

BF=jnp.bfloat16; F32=jnp.float32
LOG2E=1.4426950408889634; LN2=0.6931471805599453
SCALE=HEAD_DIM**-0.5
BIG=-(2.0**30)
GROUP=4
VM=56*1024*1024

def cost(micros):
    return pl.CostEstimate(flops=int(micros * 1e9), bytes_accessed=int(micros * 3.6e6), transcendentals=0)


def nt(a,b): return lax.dot_general(a,b,(((1,),(1,)),((),())),preferred_element_type=F32)
def nn(a,b): return jnp.dot(a,b,preferred_element_type=F32)

def placed(block, at, rows):
    parts=[]
    if at: parts.append(jnp.zeros((at,block.shape[1]),block.dtype))
    parts.append(block)
    if rows-at-block.shape[0]: parts.append(jnp.zeros((rows-at-block.shape[0],block.shape[1]),block.dtype))
    return jnp.concatenate(parts,axis=0)

PAIR = 2 * GROUP
SAFE = 2.0**60


def attend_kernel(
    q_ref, k_ref, v_ref, bias_ref, mq_ref, mk_ref, ctx_ref, ctx_tok_ref, e_ref, r_ref, scores
):
    n = q_ref.shape[2]
    ones = jnp.ones((16, n), BF)
    mask_rows = placed(mq_ref[0], 0, 128)
    lhs = [jnp.concatenate([k_ref[0, :, 128 * g : 128 * (g + 1)], mk_ref[0]], axis=1) for g in range(2)]
    rows = lambda h: slice(h * HEAD_DIM, (h + 1) * HEAD_DIM)

    def score(h):
        rhs = jnp.concatenate([placed(q_ref[0, rows(h), :], h % GROUP * HEAD_DIM, 128), mask_rows], axis=0)
        scores[h % 2] = nn(lhs[h // GROUP], rhs)

    def context(h):
        c = nn(jnp.concatenate([v_ref[0, rows(h), :], ones], axis=0), e_ref[0, h])
        total = c[HEAD_DIM : HEAD_DIM + 1]
        r = 1.0 / total
        ctx_ref[0, rows(h), :] = (c[:HEAD_DIM] * r).astype(BF)
        r_ref[0, h : h + 1, :] = r
        return total

    totals = []
    score(0)
    for h in range(PAIR):
        if h + 1 < PAIR:
            score(h + 1)
        e_ref[0, h] = jnp.exp(scores[h % 2] + bias_ref[h].astype(F32)).astype(BF)
        if h:
            totals.append(context(h - 1))
    totals.append(context(PAIR - 1))
    every = jnp.concatenate(totals, axis=0)
    ordinary = jnp.logical_and(jnp.min(every) > 1.0 / SAFE, jnp.max(every) < SAFE)

    @pl.when(jnp.logical_not(ordinary))
    def _():
        spot = lax.broadcasted_iota(jnp.int32, (128, n), 0) // HEAD_DIM

        def again(h, carry):
            at = pl.ds(pl.multiple_of(h * HEAD_DIM, HEAD_DIM), HEAD_DIM)
            group = pl.ds(pl.multiple_of(h // GROUP * 128, 128), 128)
            q = jnp.concatenate([q_ref[0, at, :].astype(F32)] * GROUP, axis=0)
            rhs = jnp.where(spot == h % GROUP, q, 0.0).astype(BF)
            s = nn(jnp.concatenate([k_ref[0, :, group], mk_ref[0]], axis=1), jnp.concatenate([rhs, mask_rows], axis=0))
            s = s + bias_ref[h].astype(F32)
            e = jnp.exp(s - jnp.max(s, axis=0, keepdims=True)).astype(BF)
            e_ref[0, h] = e
            c = nn(jnp.concatenate([v_ref[0, at, :], ones], axis=0), e)
            r = 1.0 / c[HEAD_DIM : HEAD_DIM + 1]
            ctx_ref[0, at, :] = (c[:HEAD_DIM] * r).astype(BF)
            r_ref[0, pl.ds(h, 1), :] = r
            return carry

        lax.fori_loop(0, PAIR, again, 0)

    ctx_tok_ref[0] = jnp.transpose(ctx_ref[0])


def attend(side,qT,k,vT,bias,mq,mk):
    nw,width,n=qT.shape
    half=width//2
    wins=mk.shape[0]
    return pl.pallas_call(
        attend_kernel,
        grid=(nw,),
        in_specs=[
            pl.BlockSpec((1,half,n),lambda w:(w,side,0)),
            pl.BlockSpec((1,n,half),lambda w:(w,0,side)),
            pl.BlockSpec((1,half,n),lambda w:(w,side,0)),
            pl.BlockSpec((PAIR,n,n),lambda w:(0,0,0)),
            pl.BlockSpec((1,32,n),lambda w:(w%wins,0,0)),
            pl.BlockSpec((1,n,128),lambda w:(w%wins,0,0)),
        ],
        out_specs=[
            pl.BlockSpec((1,half,n),lambda w:(w,0,0)),
            pl.BlockSpec((1,n,half),lambda w:(w,0,0)),
            pl.BlockSpec((1,PAIR,n,n),lambda w:(w,0,0,0)),
            pl.BlockSpec((1,PAIR,n),lambda w:(w,0,0)),
        ],
        out_shape=[
            jax.ShapeDtypeStruct((nw,half,n),BF),
            jax.ShapeDtypeStruct((nw,n,half),BF),
            jax.ShapeDtypeStruct((nw,PAIR,n,n),BF),
            jax.ShapeDtypeStruct((nw,PAIR,n),F32),
        ],
        scratch_shapes=[pltpu.VMEM((2,n,n),F32)],
        compiler_params=pltpu.CompilerParams(vmem_limit_bytes=VM),
        name="attend", cost_estimate=cost(10),
    )(qT,k,vT,bias,mq,mk)

SPREAD=768
FLAT=1408
WIDE=2816

def spread_ones():
    n=WT*WH*WW
    tok=np.arange(n); c=tok//(WW*WT); e=tok//WT%WW; a=tok%WT
    out=np.zeros((n,SPREAD),np.float32); out[tok,c*104+e*8+a]=1
    return out

def lane16(mirror):
    out=np.zeros((128,256),np.float32)
    for u in range(16):
        for a in range(8):
            out[u*8+a,u*16+(7-a if mirror else a)]=1
    return out

def back_kernel(
    e_ref, k_ref, v_ref, q_ref, g_ref, ctx_ref, r_ref, sp_ref, l16_ref, dq_ref, dk_ref, dv_ref, tab_ref, tot, acc, prob, low
):
    w = pl.program_id(1)
    nw = pl.num_programs(1)
    first = pl.program_id(0) * GROUP
    n = q_ref.shape[2]
    rows = lambda h: slice(h * HEAD_DIM, (h + 1) * HEAD_DIM)

    @pl.when(w == 0)
    def _():
        tot[...] = jnp.zeros_like(tot)

    grads, inner = [], []
    for h in range(GROUP):
        go = g_ref[0, rows(h), :].astype(F32) * r_ref[0, pl.ds(first + h, 1), :]
        inner.append(jnp.sum(go * ctx_ref[0, rows(h), :].astype(F32), axis=0, keepdims=True))
        grads.append(placed(go.astype(BF), h * HEAD_DIM, 128))

    def prob_grad(h):
        prob[h % 2] = nn(v_ref[0], grads[h])

    dq, dk, dv = [], [], []

    def score_side(h):
        dk.append(nt(low[h % 2], placed(q_ref[0, rows(h), :], h * HEAD_DIM, 128)))
        dq.append(nn(k_ref[0, rows(h), :], low[h % 2]) * SCALE)

    def fold(h):
        x = nn(tot[h].astype(BF), sp_ref[...])
        full = jnp.zeros((8, FLAT), F32)
        for d in range(WH):
            part = jnp.zeros((8, SPREAD), F32)
            for f in range(WW):
                j = (d * WW + f) * 8
                part = part + (pltpu.roll(x[j : j + 8, :], 8 * (WW - 1 - f), 1) if f < WW - 1 else x[j : j + 8, :])
            broad = jnp.concatenate([part, jnp.zeros((8, FLAT - SPREAD), F32)], axis=1)
            full = full + (pltpu.roll(broad, 104 * (WH - 1 - d), 1) if d < WH - 1 else broad)
        acc[h * 8 : (h + 1) * 8, :] = full

    def sweep(last):
        prob_grad(0)
        for h in range(GROUP):
            ds = e_ref[0, h].astype(F32) * (prob[h % 2] - inner[h])
            low[h % 2] = ds.astype(BF)
            tot[h] += ds
            dv.append(nt(e_ref[0, h], grads[h]))
            if h + 1 < GROUP:
                prob_grad(h + 1)
            score_side(h)
            if last:
                fold(h)
        dq_ref[0] = jnp.transpose(jnp.concatenate(dq, axis=0).astype(BF))
        dv_ref[0] = ((dv[0] + dv[1]) + (dv[2] + dv[3])).astype(BF)
        dk_ref[0] = ((dk[0] + dk[1]) + (dk[2] + dk[3])).astype(BF)
        dq.clear()
        dk.clear()
        dv.clear()

    @pl.when(w < nw - 1)
    def _():
        sweep(False)

    @pl.when(w == nw - 1)
    def _():
        sweep(True)
        a = acc[...]
        hi = a.astype(BF)
        rest = (a - hi.astype(F32)).astype(BF)
        wide = []
        for t in range(FLAT // 128):
            c = slice(t * 128, (t + 1) * 128)
            wide.append(nn(hi[:, c], l16_ref[...]) + nn(rest[:, c], l16_ref[...]))
        y = jnp.concatenate(wide, axis=1)
        for h in range(GROUP):
            z = pltpu.roll(y[h * 8 : (h + 1) * 8, :], 0, 1, stride=1, stride_axis=0)
            tab_ref[0, h : h + 1, :] = jnp.sum(z, axis=0, keepdims=True)


def attend_back(side,e,kT,v,qT,gT,ctxT,r,sp,l16):
    nw,width,n=qT.shape
    feat=pl.BlockSpec((1,128,n),lambda g,w:(w,2*side+g,0))
    tok=pl.BlockSpec((1,n,128),lambda g,w:(w,0,2*side+g))
    own=pl.BlockSpec((1,n,128),lambda g,w:(w,0,g))
    return pl.pallas_call(
        back_kernel,
        grid=(2,nw),
        in_specs=[
            pl.BlockSpec((1,GROUP,n,n),lambda g,w:(w,g,0,0)),
            feat,tok,feat,feat,pl.BlockSpec((1,128,n),lambda g,w:(w,g,0)),
            pl.BlockSpec((1,PAIR,n),lambda g,w:(w,0,0)),
            pl.BlockSpec(sp.shape,lambda g,w:(0,0)),
            pl.BlockSpec(l16.shape,lambda g,w:(0,0)),
        ],
        out_specs=[own,own,own,pl.BlockSpec((1,GROUP,WIDE),lambda g,w:(g,0,0))],
        out_shape=[
            jax.ShapeDtypeStruct((nw,n,256),BF),
            jax.ShapeDtypeStruct((nw,n,256),BF),
            jax.ShapeDtypeStruct((nw,n,256),BF),
            jax.ShapeDtypeStruct((2,GROUP,WIDE),F32),
        ],
        scratch_shapes=[
            pltpu.VMEM((GROUP,n,n),F32),pltpu.VMEM((GROUP*8,FLAT),F32),pltpu.VMEM((2,n,n),F32),pltpu.VMEM((2,n,n),BF),
        ],
        compiler_params=pltpu.CompilerParams(vmem_limit_bytes=VM),
        name="attend_back", cost_estimate=cost(20),
    )(e,kT,v,qT,gT,ctxT,r,sp,l16)

def lane_maps(mirror):
    lane=np.arange(WIDE); pq=lane//16; o=lane%16
    p=pq//13; q=pq%13
    ok=(pq<169)&(o<15)
    if mirror: o=14-o
    A=o>=7; b=np.where(A,14-o,7-o); C=p>=6; d=np.where(C,12-p,6-p); E=q>=6; f=np.where(E,12-q,6-q)
    col=(b*WH+d)*WW+f
    corner=A*4+C*2+E*1
    return np.where(ok,col,-1).astype(np.int32), np.where(ok,corner,-1).astype(np.int32)

CORNER_ROWS=[(a*WH+c)*WW+e for a in (0,WT-1) for c in (0,WH-1) for e in (0,WW-1)]

def prepare_kernel(rel_ref,maps_ref,table_ref,region_ref,order_ref,l8_ref,lab_ref,narrow_ref,mk_ref,mq_ref):
    values=[]
    n=rel_ref.shape[1]
    rel=jnp.concatenate([rel_ref[row:row+1,:] for row in CORNER_ROWS],axis=0)
    hi=(rel>>6).astype(F32).astype(BF); lo=(rel&63).astype(F32).astype(BF)
    both=jnp.concatenate([hi,lo],axis=0)
    corners=lax.broadcasted_iota(jnp.int32,(8,256),0)
    rows=lax.broadcasted_iota(jnp.int32,(n,256),0)
    trow=lax.broadcasted_iota(jnp.int32,(table_ref.shape[1],256),0)
    for t in range(WIDE//256):
        c=slice(t*256,(t+1)*256)
        for version in range(2):
            col=maps_ref[2*version:2*version+1,c]; cor=maps_ref[2*version+1:2*version+2,c]
            m=jnp.where(rows==col,1.0,0.0).astype(BF)
            y=nn(both,m)
            full=y[:8]*64.0+y[8:]
            lab=jnp.sum(jnp.where(corners==cor,full,0.0),axis=0,keepdims=True)
            lab=jnp.where(cor>=0,lab,-1.0).astype(jnp.int32)
            lab_ref[version:version+1,c]=lab
            if version==0:
                hot=jnp.where(trow==lab,1.0,0.0).astype(BF)
                values.append(nn(table_ref[...],hot))
    values=jnp.concatenate(values,axis=1)
    rolled=[]
    for h in range(HEADS):
        line=jnp.broadcast_to(values[h:h+1],(8,WIDE))
        rolled.append(pltpu.roll(line,WIDE-7,1,stride=1,stride_axis=0))
    rolled=jnp.concatenate(rolled,axis=0).astype(BF)
    for t in range(FLAT//128):
        narrow_ref[:,t*128:(t+1)*128]=nn(rolled[:,t*256:(t+1)*256],l8_ref[...])
    wins=region_ref.shape[0]
    region=jnp.concatenate([region_ref[...].astype(F32),jnp.zeros((16-wins,n),F32)],axis=0).astype(BF)
    across=nt(region,order_ref[...])
    down=nt(order_ref[...],region)
    lanes=lax.broadcasted_iota(jnp.int32,(n,128),1).astype(F32)
    subs=lax.broadcasted_iota(jnp.int32,(32,n),0).astype(F32)
    for w in range(wins):
        mk_ref[w]=jnp.where(down[:,w:w+1]==lanes,1.0,0.0).astype(BF)
        mq_ref[w]=jnp.where(across[w:w+1,:]==subs,0.0,BIG).astype(BF)

def prepare(rel_index,maps,table_t,region_ids,order,l8):
    wins,n=region_ids.shape
    return pl.pallas_call(
        prepare_kernel,
        out_shape=[
            jax.ShapeDtypeStruct((2,WIDE),jnp.int32),
            jax.ShapeDtypeStruct((HEADS*8,FLAT),F32),
            jax.ShapeDtypeStruct((wins,n,128),BF),
            jax.ShapeDtypeStruct((wins,32,n),BF),
        ],
        compiler_params=pltpu.CompilerParams(vmem_limit_bytes=VM),
        name="prepare", cost_estimate=cost(6),
    )(rel_index,maps,table_t,region_ids,order,l8)

def spread_spots():
    place = np.arange(WIN_TOK)
    lane = place // (WW * WT) * 104 + place // WT % WW * 8 + place % WT + 8 * (WW - 1)
    return np.broadcast_to(lane[:, None], (WIN_TOK, 128)).astype(np.int32)


def bias_kernel(narrow_ref, spot_ref, bias_ref, held):
    heads, n, _ = bias_ref.shape
    rows = []
    for h in range(heads):
        line = narrow_ref[8 * h : 8 * h + 8, :]
        for d in range(WH):
            rows.append((pltpu.roll(line, FLAT - 104 * (WH - 1 - d), 1) if d < WH - 1 else line)[:, :SPREAD])
    rows = jnp.concatenate(rows, axis=0).astype(BF)
    spots = jnp.concatenate([spot_ref[...]] * (SPREAD // 128), axis=1)
    lanes = lax.broadcasted_iota(jnp.int32, (n, SPREAD), 1)
    for f in range(WW):
        hot = jnp.where(lanes == spots - 8 * f, 1.0, 0.0).astype(BF)
        y = nt(rows, hot)
        for h in range(heads):
            for d in range(WH):
                at = (h * WH + d) * 8
                held[h, (d * WW + f) * 8 : (d * WW + f + 1) * 8, :] = y[at : at + 8, :]
    for h in range(heads):
        bias_ref[h] = held[h].astype(BF)


def bias_half(side, narrow, spots):
    n = spots.shape[0]
    heads = HEADS // 2
    return pl.pallas_call(
        bias_kernel,
        grid=(1,),
        in_specs=[pl.BlockSpec((8 * heads, FLAT), lambda i: (side, 0)), pl.BlockSpec(spots.shape, lambda i: (0, 0))],
        out_specs=pl.BlockSpec((heads, n, n), lambda i: (0, 0, 0)),
        out_shape=jax.ShapeDtypeStruct((heads, n, n), BF),
        scratch_shapes=[pltpu.VMEM((heads, n, n), F32)],
        compiler_params=pltpu.CompilerParams(vmem_limit_bytes=VM),
        name="position_bias", cost_estimate=cost(5),
    )(narrow, spots)


def spill_kernel(lab_ref,g_ref,out_ref):
    g=g_ref[...]
    hi=g.astype(BF); r1=g-hi.astype(F32); mid=r1.astype(BF); lo=(r1-mid.astype(F32)).astype(BF)
    three=jnp.concatenate([hi,mid,lo],axis=0)
    rows=out_ref.shape[1]
    trow=lax.broadcasted_iota(jnp.int32,(rows,256),0)
    tot=jnp.zeros((48,rows),F32)
    for t in range(WIDE//256):
        c=slice(t*256,(t+1)*256)
        hot=jnp.where(trow==lab_ref[1:2,c],1.0,0.0).astype(BF)
        tot=tot+nt(three[:,c],hot)
    out_ref[...]=tot[:16]+tot[16:32]+tot[32:]

def spill(lab,g,rows):
    return pl.pallas_call(
        spill_kernel,
        out_shape=jax.ShapeDtypeStruct((HEADS,rows),F32),
        compiler_params=pltpu.CompilerParams(vmem_limit_bytes=VM),
        name="table_rows", cost_estimate=cost(5),
    )(lab,g)


BLOCK = 32
B_FC1, B_PROJ, GAIN2, BIAS2, B_FC2, GAIN1, BIAS1, B_QV = range(8)
VEC_LANES = {B_FC1: (0, 128), GAIN1: (128, 32), BIAS1: (160, 32), B_QV: (192, 64), B_PROJ: (256, 32), GAIN2: (288, 32), BIAS2: (320, 32), B_FC2: (352, 32)}
VECTOR = 384


def load_weight(own_ref, other_ref, places_ref, held, sem, vecs=None, start=True):
    core = places_ref[64]
    lanes = slice(0, held.shape[2])
    copies = []
    for i in range(16):
        rows = pl.ds(i * BLOCK, BLOCK)
        own = own_ref.at[places_ref[i]]
        copies.append(pltpu.make_async_copy(own.at[:, lanes], held.at[core, rows, :], sem.at[2 * i]))
        copies.append(
            pltpu.make_async_copy(other_ref.at[places_ref[16 + i]].at[:, lanes], held.at[1 - core, rows, :], sem.at[2 * i + 1])
        )
        if vecs is not None:
            copies.append(pltpu.make_async_copy(own.at[0:16, held.shape[2] :], vecs.at[i], sem.at[32 + i]))
    if start:
        for copy in copies:
            copy.start()
    return copies


def await_all(copies):
    for copy in copies:
        copy.wait()


def store_grad(total, places_ref, own_ref, send_ref):
    core = places_ref[64]

    def block(i, carry):
        own_ref[i, :, : total.shape[2]] = total[core, pl.ds(pl.multiple_of(places_ref[32 + i] * BLOCK, BLOCK), BLOCK), :].astype(BF)
        send_ref[i, :, : total.shape[2]] = total[1 - core, pl.ds(pl.multiple_of(places_ref[48 + i] * BLOCK, BLOCK), BLOCK), :].astype(BF)
        return carry

    lax.fori_loop(0, 16, block, 0)


def normalise(values):
    mean = jnp.mean(values, axis=-1, keepdims=True)
    centred = values - mean
    inverse = lax.rsqrt(jnp.mean(centred * centred, axis=-1, keepdims=True) + EPS)
    return centred * inverse, inverse


def project_kernel(
    places_ref, x_ref, own_ref, other_ref, q_ref, kt_ref, vt_ref, k_ref, v_ref, vec_ref, held, loose, sem
):
    @pl.when(pl.program_id(0) == 0)
    def _():
        await_all(load_weight(own_ref, other_ref, places_ref, held, sem, loose))
        rows = [loose[i].astype(F32) for i in range(16)]
        for name, (at, count) in VEC_LANES.items():
            parts = [row[at // 128 : at // 128 + 1, at % 128 : at % 128 + count] for row in rows]
            vec_ref[name : name + 1, : 16 * count] = jnp.concatenate(parts, axis=1)

    width = x_ref.shape[2]
    normed, _ = normalise(x_ref[0].astype(F32))
    first = (normed * vec_ref[GAIN1 : GAIN1 + 1, :width] + vec_ref[BIAS1 : BIAS1 + 1, :width]).astype(BF)
    left, right = nn(first, held[0]), nn(first, held[1])
    half = width // 2
    q = (left[:, :width] + vec_ref[B_QV : B_QV + 1, :width]) * SCALE
    k = jnp.concatenate([left[:, width:], right[:, :half]], axis=1)
    v = right[:, half:] + vec_ref[B_QV : B_QV + 1, width : 2 * width]
    q_ref[0] = jnp.transpose(q.astype(BF))
    kt_ref[0] = jnp.transpose(k.astype(BF))
    vt_ref[0] = jnp.transpose(v.astype(BF))
    k_ref[0] = k.astype(BF)
    v_ref[0] = v.astype(BF)


def project(places, x, own, other, hidden_width):
    nw, n, width = x.shape
    tok = pl.BlockSpec((1, n, width), lambda w, s: (w, 0, 0))
    feat = pl.BlockSpec((1, width, n), lambda w, s: (w, 0, 0))
    anywhere = pl.BlockSpec(memory_space=pl.ANY)
    vecs = (8, hidden_width)
    return pl.pallas_call(
        project_kernel,
        grid_spec=pltpu.PrefetchScalarGridSpec(
            num_scalar_prefetch=1,
            grid=(nw,),
            in_specs=[tok, anywhere, anywhere],
            out_specs=[feat, feat, feat, tok, tok, pl.BlockSpec(vecs, lambda w, s: (0, 0))],
            scratch_shapes=[
                pltpu.VMEM((2, 16 * BLOCK, own.shape[2] - 128), BF),
                pltpu.VMEM((16, 16, 128), BF),
                pltpu.SemaphoreType.DMA((48,)),
            ],
        ),
        out_shape=[jax.ShapeDtypeStruct((nw, width, n), BF)] * 3
        + [jax.ShapeDtypeStruct((nw, n, width), BF)] * 2
        + [jax.ShapeDtypeStruct(vecs, F32)],
        compiler_params=pltpu.CompilerParams(vmem_limit_bytes=VM),
        name="project", cost_estimate=cost(9),
    )(places, x, own, other)


TAIL = (0.254829592, -0.284496736, 1.421413741, -1.453152027, 1.061405429)


def normal_parts(values):
    t = pl.reciprocal(1.0 + (0.3275911 * 0.7071067811865476) * jnp.abs(values), approx=False)
    series = TAIL[4]
    for factor in TAIL[3::-1]:
        series = series * t + factor
    bell = jnp.exp2(values * values * (-0.5 * LOG2E))
    upper = (0.5 * t) * series * bell
    return jnp.where(values >= 0, 1.0 - upper, upper), bell * 0.3989422804014327


def column_sums(values):
    return jnp.sum(values, axis=0, keepdims=True)


def feed_kernel(
    places_ref, x_ref, ctx0_ref, ctx1_ref, og_ref, vec_ref, own_ref, other_ref, out_ref, mid_grad_ref, gt_ref, own_grad_ref,
    send_grad_ref, sums_ref, held, total, wide, thin, projt, sem,
):
    step = pl.program_id(0)

    @pl.when(step == 0)
    def _():
        total[...] = jnp.zeros_like(total)
        sums_ref[...] = jnp.zeros_like(sums_ref)
        await_all(load_weight(own_ref, other_ref, places_ref, held, sem))

    width = x_ref.shape[2]
    half = width // 2

    @pl.when(step == 0)
    def _():
        for j in range(2):
            projt[j] = jnp.transpose(held[j, :, :half].astype(F32)).astype(BF)

    chunk = (held.shape[2] - half) // 2
    vec = lambda row: vec_ref[row : row + 1, :width]
    ctx = (ctx0_ref[0], ctx1_ref[0])
    branch = nt(ctx[0], held[0, :, :half]) + nt(ctx[1], held[1, :, :half])
    mid = x_ref[0].astype(F32) + (branch + vec(B_PROJ))
    normed, inverse = normalise(mid)
    second = normed * vec(GAIN2) + vec(BIAS2)
    second = second.astype(BF)
    second_t = jnp.transpose(second)
    og = og_ref[0]
    og_t = jnp.transpose(og)
    mlp = jnp.zeros(mid.shape, F32)
    second_grad = jnp.zeros(mid.shape, F32)
    piece = chunk // 2
    cuts = []
    for j in range(2):
        for part in range(2):
            at = half + part * piece
            cuts.append((j, slice(at, at + piece), slice(at + chunk, at + chunk + piece), slice(j * chunk + part * piece, j * chunk + (part + 1) * piece)))

    def widen(i):
        j, c1, c2, cols = cuts[i]
        wide[0, i % 2] = nn(second, held[j, :, c1]) + vec_ref[B_FC1 : B_FC1 + 1, cols]
        wide[1, i % 2] = nn(og, held[j, :, c2])

    widen(0)
    for i, (j, c1, c2, cols) in enumerate(cuts):
        hidden = wide[0, i % 2]
        phi_sum, density = normal_parts(hidden)
        thin[0, i % 2] = (hidden * phi_sum).astype(BF)
        hidden_grad = wide[1, i % 2] * (phi_sum + hidden * density)
        sums_ref[0:1, cols] += column_sums(hidden_grad)
        thin[1, i % 2] = hidden_grad.astype(BF)
        if i + 1 < len(cuts):
            widen(i + 1)
        mlp += nt(thin[0, i % 2], held[j, :, c2])
        second_grad += nt(thin[1, i % 2], held[j, :, c1])
        total[j, :, c1] += nn(second_t, thin[1, i % 2])
        total[j, :, c2] += nn(og_t, thin[0, i % 2])
    out_ref[0] = (mid + (mlp + vec(B_FC2))).astype(BF)
    scaled = second_grad * vec(GAIN2)
    inner = jnp.mean(scaled, axis=-1, keepdims=True)
    along = jnp.mean(scaled * normed, axis=-1, keepdims=True)
    og = og.astype(F32)
    mid_grad = og + inverse * (scaled - inner - normed * along)
    mid_grad_ref[0] = mid_grad
    low = mid_grad.astype(BF)
    sums_ref[1:2, :width] += column_sums(mid_grad)
    sums_ref[2:3, :width] += column_sums(second_grad * normed)
    sums_ref[3:4, :width] += column_sums(second_grad)
    sums_ref[4:5, :width] += column_sums(og)
    low_t = jnp.transpose(low)
    for j in range(2):
        total[j, :, :half] += nn(low_t, ctx[j])
        proj = projt[j]
        gt_ref[0, j * half : (j + 1) * half, :] = nn(proj, low_t).astype(BF)

    @pl.when(step == pl.num_programs(0) - 1)
    def _():
        store_grad(total, places_ref, own_grad_ref, send_grad_ref)


def feed(places, x, ctx0, ctx1, og, vecs, own, other):
    nw, n, width = x.shape
    tok = pl.BlockSpec((1, n, width), lambda w, s: (w, 0, 0))
    feat = pl.BlockSpec((1, width, n), lambda w, s: (w, 0, 0))
    whole = pl.BlockSpec(own.shape, lambda w, s: (0, 0, 0))
    anywhere = pl.BlockSpec(memory_space=pl.ANY)
    side = pl.BlockSpec((1, n, width // 2), lambda w, s: (w, 0, 0))
    hidden_width = own.shape[2] - width // 2
    return pl.pallas_call(
        feed_kernel,
        grid_spec=pltpu.PrefetchScalarGridSpec(
            num_scalar_prefetch=1,
            grid=(nw,),
            in_specs=[tok, side, side, tok, pl.BlockSpec(vecs.shape, lambda w, s: (0, 0)), anywhere, anywhere],
            out_specs=[tok, tok, feat, whole, whole, pl.BlockSpec((8, hidden_width), lambda w, s: (0, 0))],
            scratch_shapes=[
                pltpu.VMEM((2, 16 * BLOCK, own.shape[2]), BF),
                pltpu.VMEM((2, 16 * BLOCK, own.shape[2]), F32),
                pltpu.VMEM((2, 2, n, hidden_width // 4), F32),
                pltpu.VMEM((2, 2, n, hidden_width // 4), BF),
                pltpu.VMEM((2, width // 2, 16 * BLOCK), BF),
                pltpu.SemaphoreType.DMA((32,)),
            ],
        ),
        out_shape=[
            jax.ShapeDtypeStruct((nw, n, width), BF),
            jax.ShapeDtypeStruct((nw, n, width), F32),
            jax.ShapeDtypeStruct((nw, width, n), BF),
            jax.ShapeDtypeStruct(own.shape, BF),
            jax.ShapeDtypeStruct(own.shape, BF),
            jax.ShapeDtypeStruct((8, hidden_width), F32),
        ],
        compiler_params=pltpu.CompilerParams(vmem_limit_bytes=VM),
        name="feed_forward", cost_estimate=cost(44),
    )(places, x, ctx0, ctx1, og, vecs, own, other)


def input_kernel(
    places_ref, x_ref, dq0, dk0, dv0, dq1, dk1, dv1, mid_grad_ref, vec_ref, fc_sums_ref,
    own_ref, other_ref, out_ref, own_grad_ref, send_grad_ref, held, total, sums, small, sem,
):
    step = pl.program_id(0)

    @pl.when(step == 0)
    def _():
        total[...] = jnp.zeros_like(total)
        sums[...] = jnp.zeros_like(sums)
        load_weight(own_ref, other_ref, places_ref, held, sem)

    width = x_ref.shape[2]
    half = width // 2
    vec = lambda row: vec_ref[row : row + 1, :width]
    normed, inverse = normalise(x_ref[0].astype(F32))
    first_t = jnp.transpose((normed * vec(GAIN1) + vec(BIAS1)).astype(BF))
    left = jnp.concatenate([dq0[0], dq1[0], dk0[0]], axis=1)
    right = jnp.concatenate([dk1[0], dv0[0], dv1[0]], axis=1)
    total[0] += nn(first_t, left)
    total[1] += nn(first_t, right)

    @pl.when(step == 0)
    def _():
        await_all(load_weight(own_ref, other_ref, places_ref, held, sem, start=False))

    first_grad = (nt(left, held[0]) + nt(right, held[1])).astype(BF).astype(F32)
    scaled = first_grad * vec(GAIN1)
    inner = jnp.mean(scaled, axis=-1, keepdims=True)
    along = jnp.mean(scaled * normed, axis=-1, keepdims=True)
    out_ref[0] = (mid_grad_ref[0] + inverse * (scaled - inner - normed * along)).astype(BF)
    sums[0:1, :width] += column_sums(first_grad * normed)
    sums[1:2, :width] += column_sums(first_grad)
    sums[2:3, :width] += column_sums(left[:, :width].astype(F32))
    sums[2:3, width:] += column_sums(right[:, half:].astype(F32))

    @pl.when(step == pl.num_programs(0) - 1)
    def _():
        columns = total.shape[2]
        store_grad(total, places_ref, own_grad_ref, send_grad_ref)
        rows = {
            B_FC1: fc_sums_ref[0:1, :], B_PROJ: fc_sums_ref[1:2, :], GAIN2: fc_sums_ref[2:3, :], BIAS2: fc_sums_ref[3:4, :],
            B_FC2: fc_sums_ref[4:5, :], GAIN1: sums[0:1, :], BIAS1: sums[1:2, :], B_QV: sums[2:3, :],
        }
        for i in range(16):
            parts = [rows[name][:, i * count : (i + 1) * count] for name, (_, count) in VEC_LANES.items()]
            line = jnp.concatenate(parts, axis=1)
            small[i] = jnp.concatenate([line[:, :128], line[:, 128:256], line[:, 256:], jnp.zeros((BLOCK - 3, 128), F32)], axis=0)

        def block(i, carry):
            own_grad_ref[i, :, columns:] = small[places_ref[32 + i]].astype(BF)
            send_grad_ref[i, :, columns:] = small[places_ref[48 + i]].astype(BF)
            return carry

        lax.fori_loop(0, 16, block, 0)


def input_side(places, x, groups, mid_grad, vecs, fc_sums, own, other):
    nw, n, width = x.shape
    tok = pl.BlockSpec((1, n, width), lambda w, s: (w, 0, 0))
    part = pl.BlockSpec((1, n, width // 2), lambda w, s: (w, 0, 0))
    flat = lambda shape: pl.BlockSpec(shape, lambda w, s: (0,) * len(shape))
    anywhere = pl.BlockSpec(memory_space=pl.ANY)
    columns = own.shape[2] - 128
    grad = own.shape
    return pl.pallas_call(
        input_kernel,
        grid_spec=pltpu.PrefetchScalarGridSpec(
            num_scalar_prefetch=1,
            grid=(nw,),
            in_specs=[tok] + [part] * 6 + [tok, flat(vecs.shape), flat(fc_sums.shape), anywhere, anywhere],
            out_specs=[tok, flat(grad), flat(grad)],
            scratch_shapes=[
                pltpu.VMEM((2, 16 * BLOCK, columns), BF),
                pltpu.VMEM((2, 16 * BLOCK, columns), F32),
                pltpu.VMEM((8, 2 * width), F32),
                pltpu.VMEM((16, BLOCK, 128), F32),
                pltpu.SemaphoreType.DMA((32,)),
            ],
        ),
        out_shape=[
            jax.ShapeDtypeStruct((nw, n, width), BF),
            jax.ShapeDtypeStruct(grad, BF),
            jax.ShapeDtypeStruct(grad, BF),
        ],
        compiler_params=pltpu.CompilerParams(vmem_limit_bytes=VM),
        name="input_side", cost_estimate=cost(15),
    )(places, x, *[part for group in groups for part in group[:3]], mid_grad, vecs, fc_sums, own, other)


def from_partner(shard, axis, stride):
    return lax.ppermute(shard, axis, [(i, i ^ 1 << stride) for i in range(lax.axis_size(axis))])


def to_block(windows, local_count):
    clip_count, chans = (windows.shape[0], windows.shape[-1])
    parted = windows.reshape(
        clip_count, local_count[0], local_count[1], local_count[2], WT, WH, WW, chans
    )
    parted = parted.transpose(0, 1, 4, 2, 5, 3, 6, 7)
    return parted.reshape(
        clip_count, local_count[0] * WT, local_count[1] * WH, local_count[2] * WW, chans
    )


def from_block(block, local_count):
    clip_count, chans = (block.shape[0], block.shape[-1])
    parted = block.reshape(
        clip_count, local_count[0], WT, local_count[1], WH, local_count[2], WW, chans
    )
    parted = parted.transpose(0, 1, 3, 5, 2, 4, 6, 7)
    return parted.reshape(clip_count, -1, WT * WH * WW, chans)


def roll_ahead(windows, local_count, bit_list):
    block = to_block(windows, local_count)
    for grid_dim, amount, bit_pos in (
        (1, WT // 2, bit_list[0]),
        (2, WH // 2, bit_list[1]),
        (3, WW // 2, bit_list[2]),
    ):
        if bit_pos < 0:
            block = jnp.roll(block, -amount, axis=grid_dim)
        else:
            front = lax.slice_in_dim(block, 0, amount, axis=grid_dim)
            arrived = from_partner(front, "seq", bit_pos)
            rest = lax.slice_in_dim(block, amount, block.shape[grid_dim], axis=grid_dim)
            block = jnp.concatenate([rest, arrived], axis=grid_dim)
    return from_block(block, local_count)


def roll_behind(windows, local_count, bit_list):
    block = to_block(windows, local_count)
    for grid_dim, amount, bit_pos in (
        (1, WT // 2, bit_list[0]),
        (2, WH // 2, bit_list[1]),
        (3, WW // 2, bit_list[2]),
    ):
        if bit_pos < 0:
            block = jnp.roll(block, amount, axis=grid_dim)
        else:
            extent = block.shape[grid_dim]
            trailing = lax.slice_in_dim(block, extent - amount, extent, axis=grid_dim)
            arrived = from_partner(trailing, "seq", bit_pos)
            rest = lax.slice_in_dim(block, 0, extent - amount, axis=grid_dim)
            block = jnp.concatenate([arrived, rest], axis=grid_dim)
    return from_block(block, local_count)


KEEP = WT // 2 * WH * WW


def hwt_order():
    place = np.arange(WIN_TOK)
    return (place % WT * WH + place // (WW * WT)) * WW + place // WT % WW


def order_ones(shift):
    place = np.arange(WIN_TOK)
    out = np.zeros((WIN_TOK, WIN_TOK), np.float32)
    out[place, ((place + shift) % WT * WH + place // (WW * WT)) * WW + place // WT % WW] = 1
    return out


def tile_runs(win):
    runs = []
    for c in range(WH):
        h = (win // 2 * WH + c + WH // 2) % (2 * WH)
        for e, count in ((0, WW - WW // 2), (WW - WW // 2, WW // 2)):
            w = (win % 2 * WW + e + WW // 2) % (2 * WW)
            runs.append((h // WH * 2 + w // WW, h % WH * WW + w % WW, count))
    return runs


def swap_cores(part):
    return lax.ppermute(part, "seq", [(0, 1), (1, 0)])


def enter_kernel(own_ref, arrived_ref, order_ref, out_ref, held):
    _, n, width = own_ref.shape
    rows = lax.broadcasted_iota(jnp.int32, (n, width), 0)
    for source in range(4):
        values = jnp.where(rows >= KEEP, own_ref[source].astype(F32), arrived_ref[source].astype(F32)).astype(BF)
        held[source] = nn(order_ref[...], values)
    for win in range(4):
        parts = [held[source, 8 * at : 8 * (at + count), :] for source, at, count in tile_runs(win)]
        out_ref[win] = jnp.concatenate(parts, axis=0).astype(BF)


def leave_kernel(rows_ref, order_ref, out_ref, send_ref, held):
    for win in range(4):
        values = rows_ref[win].astype(F32)
        start = 0
        for source, at, count in tile_runs(win):
            held[source, 8 * at : 8 * (at + count), :] = values[8 * start : 8 * (start + count), :]
            start += count
    for source in range(4):
        values = nn(order_ref[...], held[source].astype(BF)).astype(out_ref.dtype)
        out_ref[source] = values
        send_ref[source] = values[: send_ref.shape[1]].astype(BF)


SENT = 208


def enter(windows, plan, arrived=None):
    clips, wins, toks, width = windows.shape
    if plan["levels"] == 1 and clips == 1:
        own = windows.reshape(wins, toks, width)
        block = (wins, toks, width // 2)
        part = pl.BlockSpec(block, lambda i: (0, 0, i))
        return pl.pallas_call(
            enter_kernel,
            grid=(2,),
            in_specs=[part, part, pl.BlockSpec((toks, toks), lambda i: (0, 0))],
            out_specs=part,
            out_shape=jax.ShapeDtypeStruct(own.shape, BF),
            scratch_shapes=[pltpu.VMEM(block, F32)],
            compiler_params=pltpu.CompilerParams(vmem_limit_bytes=VM),
            name="enter", cost_estimate=cost(4),
        )(own, arrived.reshape(own.shape), plan["order"])
    rolled = roll_ahead(windows, plan["local"], plan["bits"])
    rolled = rolled.reshape(clips * wins, WT, WH * WW, width).transpose(0, 2, 1, 3)
    return rolled.reshape(clips * wins, toks, width)


def leave(windows, plan, kind):
    wins, toks, width = windows.shape
    block = (wins, toks, width // 2)
    part = pl.BlockSpec(block, lambda i: (0, 0, i))
    return pl.pallas_call(
        leave_kernel,
        grid=(2,),
        in_specs=[part, pl.BlockSpec((toks, toks), lambda i: (0, 0))],
        out_specs=[part, pl.BlockSpec((wins, SENT, width // 2), lambda i: (0, 0, i))],
        out_shape=[jax.ShapeDtypeStruct(windows.shape, kind), jax.ShapeDtypeStruct((wins, SENT, width), BF)],
        scratch_shapes=[pltpu.VMEM(block, F32)],
        compiler_params=pltpu.CompilerParams(vmem_limit_bytes=VM),
        name="leave", cost_estimate=cost(4),
    )(windows, plan["order"].T)


def joined(kept, arrived):
    arrived = jnp.pad(arrived.astype(kept.dtype), ((0, 0), (0, kept.shape[1] - SENT), (0, 0)))
    rows = lax.broadcasted_iota(jnp.int32, kept.shape, 1)
    return jnp.where(rows < KEEP, arrived, kept)[None]


def leave_any(windows, plan, clips, kind):
    count, toks, width = windows.shape
    wins = count // clips
    if plan["levels"] == 1 and clips == 1:
        kept, sent = leave(windows, plan, kind)
        return joined(kept, swap_cores(sent))
    rows = windows.reshape(count, WH * WW, WT, width).transpose(0, 2, 1, 3)
    return roll_behind(rows.reshape(clips, wins, toks, width), plan["local"], plan["bits"]).astype(kind)


def pack_kernel(core_ref, qkv_ref, proj_ref, fc1_ref, fc2_ref, *rest):
    vec_refs, (qkv_out, fc_out) = rest[:-2], rest[-2:]

    def emit(side):
        half = qkv_ref.shape[1] // 2
        qkv_out[:, :half] = qkv_ref[:, side * half : (side + 1) * half]
        at = 0
        for ref in (proj_ref, fc1_ref, fc2_ref):
            half = ref.shape[1] // 2
            fc_out[:, at : at + half] = ref[:, side * half : (side + 1) * half]
            at += half

    half = qkv_ref.shape[1] // 2
    line = jnp.concatenate([ref[...].astype(F32).reshape(1, -1) for ref in vec_refs], axis=1)
    lines = [line[:, at : at + 128] for at in range(0, VECTOR, 128)]
    qkv_out[:, half:] = jnp.concatenate(lines + [jnp.zeros((BLOCK - len(lines), 128), F32)], axis=0).astype(BF)
    for side in range(2):
        @pl.when(core_ref[0] == side)
        def _():
            emit(side)


def pack(core, qkv, proj_t, fc1, fc2_t, vectors):
    columns = (proj_t.shape[1] + fc1.shape[1] + fc2_t.shape[1]) // 2
    vmem = pl.BlockSpec(memory_space=pltpu.VMEM)
    return pl.pallas_call(
        pack_kernel,
        in_specs=[pl.BlockSpec(memory_space=pltpu.SMEM)] + [vmem] * (4 + len(vectors)),
        out_shape=[
            jax.ShapeDtypeStruct((BLOCK, qkv.shape[1] // 2 + 128), BF),
            jax.ShapeDtypeStruct((BLOCK, columns), BF),
        ],
        compiler_params=pltpu.CompilerParams(vmem_limit_bytes=VM),
        name="pack", cost_estimate=cost(2),
    )(core, qkv, proj_t, fc1, fc2_t, *vectors)


def hop(part, flips):
    pairs = [(16 * c + s, 16 * c + (s ^ flips[c])) for c in range(2) for s in range(16)]
    return lax.ppermute(part, ("seq", "shard"), pairs)


def tree_places():
    me = lax.axis_index("shard")
    core = lax.axis_index("seq")
    entry = jnp.arange(16, dtype=jnp.int32)
    v, u, z = entry // 8, entry // 4 % 2, entry % 4
    straight, crossed = me ^ (4 * z + 2 * u + v), me ^ (4 * z + 2 * v + u)
    rel = me ^ entry
    z, y, x = rel // 4, rel // 2 % 2, rel % 2
    place_straight, place_crossed = x * 8 + y * 4 + z, y * 8 + x * 4 + z
    even = core == 0
    pick_core = lambda left, right: jnp.where(even, left, right)
    return jnp.concatenate(
        [
            pick_core(place_straight, place_crossed),
            pick_core(place_crossed, place_straight),
            pick_core(straight, crossed),
            pick_core(crossed, straight),
            jnp.broadcast_to(core, (1,)),
        ]
    ).astype(jnp.int32)


def tree_gather(part):
    arrived = yield [hop(part, (4 * k, 4 * k)) for k in range(1, 4)]
    stack = jnp.stack([part] + arrived)
    arrived = yield hop(stack, (2, 1))
    stack = jnp.concatenate([stack, arrived])
    arrived = yield hop(stack, (1, 2))
    stack = jnp.concatenate([stack, arrived])
    other = yield swap_cores(stack)
    yield stack, other


def tie(*items):
    return lax.optimization_barrier(items)


def add_low(left, right):
    return (left.astype(F32) + right.astype(F32)).astype(BF)


def tree_scatter(own, send):
    arrived = yield swap_cores(send)
    stack = add_low(own, arrived)
    arrived = yield hop(stack[8:], (1, 2))
    stack = add_low(stack[:8], arrived)
    arrived = yield hop(stack[4:], (2, 1))
    stack = add_low(stack[:4], arrived)
    arrived = yield [hop(stack[k], (4 * k, 4 * k)) for k in range(1, 4)]
    arrived = [part.astype(F32) for part in arrived]
    yield (stack[0].astype(F32) + arrived[0]) + (arrived[1] + arrived[2])


def finish(steps, pending):
    while True:
        try:
            pending = steps.send(pending)
        except StopIteration:
            return pending


def table_sum(table):
    for axis, flip in (("seq", 1), ("shard", 1), ("shard", 2)):
        pairs = [(i, i ^ flip) for i in range(2 if axis == "seq" else 16)]
        arrived = yield lax.ppermute(table, axis, pairs)
        table = add_low(table, arrived)
    arrived = yield [hop(table, (4 * k, 4 * k)) for k in range(1, 4)]
    arrived = [part.astype(F32) for part in arrived]
    yield (table.astype(F32) + arrived[0]) + (arrived[1] + arrived[2])


def sides(part, other, core):
    other = other.astype(F32)
    return [jnp.where(core == 0, part, other), jnp.where(core == 0, other, part)]


def body(
    tokens, norm1_gain, norm1_bias, qkv_weight, qv_bias, position_table, proj_weight, proj_bias, norm2_gain,
    norm2_bias, fc1_weight, fc1_bias, fc2_weight, fc2_bias, rel_index, region_ids, cotangent,
):
    levels = lax.axis_size("seq").bit_length() - 1
    clips, wins, toks, width = tokens.shape
    hidden_width = fc1_weight.shape[1]
    plan = {
        "levels": levels,
        "local": [1 if levels > level_pos else 2 for level_pos in range(3)],
        "bits": [levels - 1 - level_pos for level_pos in range(3)],
        "order": jnp.asarray(order_ones(WT // 2), BF),
    }

    def fc_outputs(pair):
        cut = (width // 2, (width + hidden_width) // 2)
        return [jnp.concatenate(two, axis=1) for two in zip(*(jnp.split(part, cut, axis=1) for part in pair))]

    vectors = [fc1_bias, norm1_gain, norm1_bias, qv_bias, proj_bias, norm2_gain, norm2_bias, fc2_bias]
    sizes = [part.shape[0] for part in vectors]
    spread = jnp.asarray(spread_ones(), BF)
    spots = jnp.asarray(spread_spots())
    wide8 = jnp.asarray(lane16(False).T, BF)
    wide16 = jnp.asarray(lane16(True), BF)
    maps = jnp.asarray(np.stack(lane_maps(False) + lane_maps(True)))
    table = prepare(rel_index, maps, position_table.T, region_ids, jnp.asarray(order_ones(0), BF), wide8)
    if clips == 1 and lax.axis_size("shard") == 16 and lax.axis_size("seq") == 2:
        core = lax.axis_index("seq")
        places = tree_places()
        qkv_part, fc_part = pack(
            jnp.reshape(core, (1,)), qkv_weight, proj_weight.T, fc1_weight, fc2_weight.T, vectors
        )
        qkv_steps, fc_steps = tree_gather(qkv_part), tree_gather(fc_part)
        qkv_hop = next(qkv_steps)
        arrived = swap_cores(tokens)
        table, qkv_hop, arrived = tie(table, qkv_hop, arrived)
        labels, narrow, mask_keys, mask_queries = table
        qkv_hop = qkv_steps.send(qkv_hop)
        shifted = enter(tokens, plan, arrived)
        qkv_hop, shifted, narrow, fc_part = tie(qkv_hop, shifted, narrow, fc_part)
        qkv_hop = qkv_steps.send(qkv_hop)
        fc_hop = next(fc_steps)
        bias_low = bias_half(0, narrow, spots)
        arrived = swap_cores(cotangent)
        qkv_hop, bias_low, arrived, narrow = tie(qkv_hop, bias_low, arrived, narrow)
        qkv_hop = qkv_steps.send(qkv_hop)
        out_grad = enter(cotangent, plan, arrived)
        qkv_hop, out_grad, fc_hop = tie(qkv_hop, out_grad, fc_hop)
        qkv_own, qkv_other = qkv_steps.send(qkv_hop)
        fc_hop = fc_steps.send(fc_hop)
        q_t, k_t, v_t, token_k, token_v, vecs = project(places, shifted, qkv_own, qkv_other, hidden_width)
        q_t, fc_hop = tie(q_t, fc_hop)
        fc_hop = fc_steps.send(fc_hop)
        low = attend(0, q_t, token_k, v_t, bias_low, mask_queries, mask_keys)
        narrow, low = tie(narrow, low)
        bias_high = bias_half(1, narrow, spots)
        q_t, low, fc_hop, bias_high = tie(q_t, low, fc_hop, bias_high)
        fc_hop = fc_steps.send(fc_hop)
        high = attend(1, q_t, token_k, v_t, bias_high, mask_queries, mask_keys)
        high, fc_hop = tie(high, fc_hop)
        fc_own, fc_other = fc_steps.send(fc_hop)
        block_out, mid_grad, context_grad_t, fc_keep, fc_send, fc_sums = feed(
            places, shifted, low[1], high[1], out_grad, vecs, fc_own, fc_other
        )
        fc_steps = tree_scatter(fc_keep, fc_send)
        fc_hop = next(fc_steps)
        groups = []
        for side, (context_t, _, expo, inverse_sum) in enumerate((low, high)):
            group = attend_back(
                side, expo, k_t, token_v, q_t, context_grad_t, context_t, inverse_sum, spread, wide16
            )
            group, fc_hop, context_grad_t, block_out = tie(group, fc_hop, context_grad_t, block_out)
            groups.append(group)
            fc_hop = fc_steps.send(fc_hop)
        offsets = jnp.concatenate([group[3] for group in groups]).reshape(HEADS, WIDE)
        table_steps = table_sum(offsets.astype(BF))
        table_hop = next(table_steps)
        input_grad, qkv_keep, qkv_send = input_side(
            places, shifted, groups, mid_grad, vecs, fc_sums, qkv_own, qkv_other
        )
        input_grad, qkv_send, fc_hop, table_hop, block_out = tie(input_grad, qkv_send, fc_hop, table_hop, block_out)
        qkv_steps = tree_scatter(qkv_keep, qkv_send)
        qkv_hop = next(qkv_steps)
        fc_hop = fc_steps.send(fc_hop)
        table_hop = table_steps.send(table_hop)
        kept, sent = leave(input_grad, plan, F32)
        qkv_hop, table_hop, kept, sent, block_out = tie(qkv_hop, table_hop, kept, sent, block_out)
        qkv_hop = qkv_steps.send(qkv_hop)
        table_hop = table_steps.send(table_hop)
        arrived = swap_cores(sent)
        out_kept, out_sent = leave(block_out, plan, BF)
        qkv_hop, table_hop, fc_hop, arrived, out_kept, out_sent = tie(qkv_hop, table_hop, fc_hop, arrived, out_kept, out_sent)
        qkv_hop = qkv_steps.send(qkv_hop)
        table_hop = table_steps.send(table_hop)
        own_fc = finish(fc_steps, fc_hop)
        out_arrived = swap_cores(out_sent)
        fc_swap = swap_cores(own_fc.astype(BF))
        input_grad = joined(kept, arrived)
        qkv_hop, table_hop, input_grad, fc_swap, out_arrived = tie(qkv_hop, table_hop, input_grad, fc_swap, out_arrived)
        qkv_hop = qkv_steps.send(qkv_hop)
        offsets = finish(table_steps, table_hop)
        block_out = joined(out_kept, out_arrived)
        own_fc = fc_outputs(sides(own_fc, fc_swap, core))
        table_grad = spill(labels, offsets, position_table.shape[0])
        qkv_hop, block_out, own_fc, table_grad = tie(qkv_hop, block_out, own_fc, table_grad)
        own_qkv = finish(qkv_steps, qkv_hop)
        small = own_qkv[: VECTOR // 128, width * 3 // 2 :].reshape(-1)
        own_qkv = own_qkv[:, : width * 3 // 2]
        own_qkv = sides(own_qkv, swap_cores(own_qkv.astype(BF)), core)
    else:
        straight = np.arange(16)
        places = jnp.asarray(np.concatenate([straight, straight, straight, straight, np.zeros(1)]), jnp.int32)
        gather = lambda part: lax.all_gather(part, "shard", axis=0, tiled=True)
        halves = lambda part: jnp.split(part, 2, axis=1)
        parts = [halves(gather(part)) for part in (proj_weight.T, fc1_weight, fc2_weight.T)]
        fc_own, fc_other = (jnp.concatenate(pair, axis=1).reshape(16, BLOCK, -1) for pair in zip(*parts))
        rows = lax.all_gather(jnp.concatenate(vectors), "shard", axis=0, tiled=False)
        pieces = [piece.reshape(16, -1) for piece in jnp.split(rows, np.cumsum(sizes)[:-1], axis=1)]
        rows = jnp.pad(jnp.concatenate(pieces, axis=1).reshape(16, -1, 128), ((0, 0), (0, BLOCK - VECTOR // 128), (0, 0)))
        qkv_own, qkv_other = (
            jnp.concatenate([part.reshape(16, BLOCK, -1), rows], axis=2) for part in halves(gather(qkv_weight))
        )
        shifted = enter(tokens, plan, swap_cores(tokens) if levels == 1 else None)
        out_grad = enter(cotangent, plan, swap_cores(cotangent) if levels == 1 else None)
        labels, narrow, mask_keys, mask_queries = table
        bias_low, bias_high = (bias_half(side, narrow, spots) for side in range(2))
        q_t, k_t, v_t, token_k, token_v, vecs = project(places, shifted, qkv_own, qkv_other, hidden_width)
        low = attend(0, q_t, token_k, v_t, bias_low, mask_queries, mask_keys)
        high = attend(1, q_t, token_k, v_t, bias_high, mask_queries, mask_keys)
        block_out, mid_grad, context_grad_t, fc_keep, fc_send, fc_sums = feed(
            places, shifted, low[1], high[1], out_grad, vecs, fc_own, fc_other
        )
        groups = [
            attend_back(side, expo, k_t, token_v, q_t, context_grad_t, context_t, inverse_sum, spread, wide16)
            for side, (context_t, _, expo, inverse_sum) in enumerate((low, high))
        ]
        input_grad, qkv_keep, qkv_send = input_side(
            places, shifted, groups, mid_grad, vecs, fc_sums, qkv_own, qkv_other
        )
        block_out = leave_any(block_out, plan, clips, BF)
        input_grad = leave_any(input_grad, plan, clips, F32)
        offsets = jnp.concatenate([group[3] for group in groups]).reshape(HEADS, WIDE)
        table_grad = spill(labels, lax.psum(offsets, ("seq", "shard")), position_table.shape[0])
        small = qkv_keep[:, : VECTOR // 128, width * 3 // 2 :].reshape(16, VECTOR)
        small = lax.psum(small.astype(F32), ("seq", "shard"))
        pieces = jnp.split(small, np.cumsum([count for _, count in VEC_LANES.values()])[:-1], axis=1)
        shards = lax.axis_size("shard")
        small = jnp.concatenate([piece.reshape(shards, -1) for piece in pieces], axis=1)
        small = lax.dynamic_index_in_dim(small, lax.axis_index("shard"), 0, keepdims=False)

        def owned(grad):
            grad = lax.psum(grad.reshape(16 * BLOCK, -1), "seq")
            return lax.psum_scatter(grad, "shard", scatter_dimension=0, tiled=True).astype(F32)

        own_fc = fc_outputs([owned(fc_keep), owned(fc_send)])
        own_qkv = [owned(qkv_keep[:, :, : width * 3 // 2]), owned(qkv_send[:, :, : width * 3 // 2])]
    own_proj, own_fc1, own_fc2 = own_fc
    own_qkv = jnp.concatenate(own_qkv, axis=1)
    own_f1b, own_g1, own_b1, own_qv, own_pb, own_g2, own_b2, own_f2b = jnp.split(small, np.cumsum(sizes)[:-1])
    return (
        block_out, input_grad, own_g1, own_b1, own_qkv, own_qv, table_grad.T, own_proj.T, own_pb,
        own_g2, own_b2, own_fc1, own_f1b, own_fc2.T, own_f2b,
    )


def solution(mesh):
    return jax.shard_map(
        body,
        mesh=mesh,
        in_specs=(
            P("shard", "seq", None, None),
            P("shard"),
            P("shard"),
            P("shard", None),
            P("shard"),
            P(),
            P(None, "shard"),
            P("shard"),
            P("shard"),
            P("shard"),
            P("shard", None),
            P("shard"),
            P(None, "shard"),
            P("shard"),
            P(),
            P("seq", None),
            P("shard", "seq", None, None),
        ),
        out_specs=(
            P("shard", "seq", None, None),
            P("shard", "seq", None, None),
            P("shard"),
            P("shard"),
            P("shard", None),
            P("shard"),
            P(),
            P(None, "shard"),
            P("shard"),
            P("shard"),
            P("shard"),
            P("shard", None),
            P("shard"),
            P(None, "shard"),
            P("shard"),
        ),
        check_vma=False,
    )
```

```python
import functools

import jax
import jax.numpy as jnp
import numpy as np
from jax import lax
from jax.experimental import pallas as pl
from jax.experimental.pallas import tpu as pltpu
from jax.sharding import PartitionSpec as P

HEADS = 16
HEAD_DIM = 32
WT = 8
WH = 7
WW = 7
WIN_TOK = WT * WH * WW
EPS = 1e-05

BF=jnp.bfloat16; F32=jnp.float32
LOG2E=1.4426950408889634; LN2=0.6931471805599453
SCALE=HEAD_DIM**-0.5
BIG=-(2.0**30)
GROUP=4
VM=54*1024*1024

def cost(micros):
    return pl.CostEstimate(flops=int(micros * 1e9), bytes_accessed=int(micros * 3.6e6), transcendentals=0)


def nt(a,b): return lax.dot_general(a,b,(((1,),(1,)),((),())),preferred_element_type=F32)
def nn(a,b): return jnp.dot(a,b,preferred_element_type=F32)

def placed(block, at, rows):
    parts=[]
    if at: parts.append(jnp.zeros((at,block.shape[1]),block.dtype))
    parts.append(block)
    if rows-at-block.shape[0]: parts.append(jnp.zeros((rows-at-block.shape[0],block.shape[1]),block.dtype))
    return jnp.concatenate(parts,axis=0)

PAIR = 2 * GROUP
SAFE = 2.0**60


def attend_kernel(
    q_ref, k_ref, v_ref, bias_ref, mq_ref, mk_ref, ctx_ref, ctx_tok_ref, e_ref, r_ref, scores
):
    n = q_ref.shape[2]
    ones = jnp.ones((16, n), BF)
    mask_rows = placed(mq_ref[0], 0, 128)
    lhs = [jnp.concatenate([k_ref[0, :, 128 * g : 128 * (g + 1)], mk_ref[0]], axis=1) for g in range(2)]
    rows = lambda h: slice(h * HEAD_DIM, (h + 1) * HEAD_DIM)

    def score(h):
        rhs = jnp.concatenate([placed(q_ref[0, rows(h), :], h % GROUP * HEAD_DIM, 128), mask_rows], axis=0)
        scores[h % 2] = nn(lhs[h // GROUP], rhs)

    def context(h):
        c = nn(jnp.concatenate([v_ref[0, rows(h), :], ones], axis=0), e_ref[0, h])
        total = c[HEAD_DIM : HEAD_DIM + 1]
        r = 1.0 / total
        ctx_ref[0, rows(h), :] = (c[:HEAD_DIM] * r).astype(BF)
        r_ref[0, h : h + 1, :] = r
        return total

    totals = []
    score(0)
    for h in range(PAIR):
        if h + 1 < PAIR:
            score(h + 1)
        e_ref[0, h] = jnp.exp(scores[h % 2] + bias_ref[h].astype(F32)).astype(BF)
        if h:
            totals.append(context(h - 1))
    totals.append(context(PAIR - 1))
    every = jnp.concatenate(totals, axis=0)
    ordinary = jnp.logical_and(jnp.min(every) > 1.0 / SAFE, jnp.max(every) < SAFE)

    @pl.when(jnp.logical_not(ordinary))
    def _():
        spot = lax.broadcasted_iota(jnp.int32, (128, n), 0) // HEAD_DIM

        def again(h, carry):
            at = pl.ds(pl.multiple_of(h * HEAD_DIM, HEAD_DIM), HEAD_DIM)
            group = pl.ds(pl.multiple_of(h // GROUP * 128, 128), 128)
            q = jnp.concatenate([q_ref[0, at, :].astype(F32)] * GROUP, axis=0)
            rhs = jnp.where(spot == h % GROUP, q, 0.0).astype(BF)
            s = nn(jnp.concatenate([k_ref[0, :, group], mk_ref[0]], axis=1), jnp.concatenate([rhs, mask_rows], axis=0))
            s = s + bias_ref[h].astype(F32)
            e = jnp.exp(s - jnp.max(s, axis=0, keepdims=True)).astype(BF)
            e_ref[0, h] = e
            c = nn(jnp.concatenate([v_ref[0, at, :], ones], axis=0), e)
            r = 1.0 / c[HEAD_DIM : HEAD_DIM + 1]
            ctx_ref[0, at, :] = (c[:HEAD_DIM] * r).astype(BF)
            r_ref[0, pl.ds(h, 1), :] = r
            return carry

        lax.fori_loop(0, PAIR, again, 0)

    ctx_tok_ref[0] = jnp.transpose(ctx_ref[0])


def attend(side,qT,k,vT,bias,mq,mk):
    nw,width,n=qT.shape
    half=width//2
    wins=mk.shape[0]
    return pl.pallas_call(
        attend_kernel,
        grid=(nw,),
        in_specs=[
            pl.BlockSpec((1,half,n),lambda w:(w,side,0)),
            pl.BlockSpec((1,n,half),lambda w:(w,0,side)),
            pl.BlockSpec((1,half,n),lambda w:(w,side,0)),
            pl.BlockSpec((PAIR,n,n),lambda w:(0,0,0)),
            pl.BlockSpec((1,32,n),lambda w:(w%wins,0,0)),
            pl.BlockSpec((1,n,128),lambda w:(w%wins,0,0)),
        ],
        out_specs=[
            pl.BlockSpec((1,half,n),lambda w:(w,0,0)),
            pl.BlockSpec((1,n,half),lambda w:(w,0,0)),
            pl.BlockSpec((1,PAIR,n,n),lambda w:(w,0,0,0)),
            pl.BlockSpec((1,PAIR,n),lambda w:(w,0,0)),
        ],
        out_shape=[
            jax.ShapeDtypeStruct((nw,half,n),BF),
            jax.ShapeDtypeStruct((nw,n,half),BF),
            jax.ShapeDtypeStruct((nw,PAIR,n,n),BF),
            jax.ShapeDtypeStruct((nw,PAIR,n),F32),
        ],
        scratch_shapes=[pltpu.VMEM((2,n,n),F32)],
        compiler_params=pltpu.CompilerParams(vmem_limit_bytes=VM),
        name="attend", cost_estimate=cost(10),
    )(qT,k,vT,bias,mq,mk)

SPREAD=768
FLAT=1408
WIDE=2816

def spread_ones():
    n=WT*WH*WW
    tok=np.arange(n); c=tok//(WW*WT); e=tok//WT%WW; a=tok%WT
    out=np.zeros((n,SPREAD),np.float32); out[tok,c*104+e*8+a]=1
    return out

def lane16(mirror):
    out=np.zeros((128,256),np.float32)
    for u in range(16):
        for a in range(8):
            out[u*8+a,u*16+(7-a if mirror else a)]=1
    return out

def back_kernel(
    e_ref, k_ref, v_ref, q_ref, g_ref, ctx_ref, r_ref, sp_ref, l16_ref, dq_ref, dk_ref, dv_ref, tab_ref, tot, acc, prob, low
):
    w = pl.program_id(1)
    nw = pl.num_programs(1)
    first = pl.program_id(0) * GROUP
    n = q_ref.shape[2]
    rows = lambda h: slice(h * HEAD_DIM, (h + 1) * HEAD_DIM)

    @pl.when(w == 0)
    def _():
        tot[...] = jnp.zeros_like(tot)

    grads, inner = [], []
    for h in range(GROUP):
        go = g_ref[0, rows(h), :].astype(F32) * r_ref[0, pl.ds(first + h, 1), :]
        inner.append(jnp.sum(go * ctx_ref[0, rows(h), :].astype(F32), axis=0, keepdims=True))
        grads.append(placed(go.astype(BF), h * HEAD_DIM, 128))

    def prob_grad(h):
        prob[h % 2] = nn(v_ref[0], grads[h])

    dq, dk, dv = [], [], []

    def score_side(h):
        dk.append(nt(low[h % 2], placed(q_ref[0, rows(h), :], h * HEAD_DIM, 128)))
        dq.append(nn(k_ref[0, rows(h), :], low[h % 2]) * SCALE)

    def fold(h):
        x = nn(tot[h].astype(BF), sp_ref[...])
        full = jnp.zeros((8, FLAT), F32)
        for d in range(WH):
            part = jnp.zeros((8, SPREAD), F32)
            for f in range(WW):
                j = (d * WW + f) * 8
                part = part + (pltpu.roll(x[j : j + 8, :], 8 * (WW - 1 - f), 1) if f < WW - 1 else x[j : j + 8, :])
            broad = jnp.concatenate([part, jnp.zeros((8, FLAT - SPREAD), F32)], axis=1)
            full = full + (pltpu.roll(broad, 104 * (WH - 1 - d), 1) if d < WH - 1 else broad)
        acc[h * 8 : (h + 1) * 8, :] = full

    def sweep(last):
        prob_grad(0)
        for h in range(GROUP):
            ds = e_ref[0, h].astype(F32) * (prob[h % 2] - inner[h])
            low[h % 2] = ds.astype(BF)
            tot[h] += ds
            dv.append(nt(e_ref[0, h], grads[h]))
            if h + 1 < GROUP:
                prob_grad(h + 1)
            score_side(h)
            if last:
                fold(h)
        dq_ref[0] = jnp.transpose(jnp.concatenate(dq, axis=0).astype(BF))
        dv_ref[0] = ((dv[0] + dv[1]) + (dv[2] + dv[3])).astype(BF)
        dk_ref[0] = ((dk[0] + dk[1]) + (dk[2] + dk[3])).astype(BF)
        dq.clear()
        dk.clear()
        dv.clear()

    @pl.when(w < nw - 1)
    def _():
        sweep(False)

    @pl.when(w == nw - 1)
    def _():
        sweep(True)
        a = acc[...]
        hi = a.astype(BF)
        rest = (a - hi.astype(F32)).astype(BF)
        wide = []
        for t in range(FLAT // 128):
            c = slice(t * 128, (t + 1) * 128)
            wide.append(nn(hi[:, c], l16_ref[...]) + nn(rest[:, c], l16_ref[...]))
        y = jnp.concatenate(wide, axis=1)
        for h in range(GROUP):
            z = pltpu.roll(y[h * 8 : (h + 1) * 8, :], 0, 1, stride=1, stride_axis=0)
            tab_ref[0, h : h + 1, :] = jnp.sum(z, axis=0, keepdims=True)


def attend_back(side,e,kT,v,qT,gT,ctxT,r,sp,l16):
    nw,width,n=qT.shape
    feat=pl.BlockSpec((1,128,n),lambda g,w:(w,2*side+g,0))
    tok=pl.BlockSpec((1,n,128),lambda g,w:(w,0,2*side+g))
    own=pl.BlockSpec((1,n,128),lambda g,w:(w,0,g))
    return pl.pallas_call(
        back_kernel,
        grid=(2,nw),
        in_specs=[
            pl.BlockSpec((1,GROUP,n,n),lambda g,w:(w,g,0,0)),
            feat,tok,feat,feat,pl.BlockSpec((1,128,n),lambda g,w:(w,g,0)),
            pl.BlockSpec((1,PAIR,n),lambda g,w:(w,0,0)),
            pl.BlockSpec(sp.shape,lambda g,w:(0,0)),
            pl.BlockSpec(l16.shape,lambda g,w:(0,0)),
        ],
        out_specs=[own,own,own,pl.BlockSpec((1,GROUP,WIDE),lambda g,w:(g,0,0))],
        out_shape=[
            jax.ShapeDtypeStruct((nw,n,256),BF),
            jax.ShapeDtypeStruct((nw,n,256),BF),
            jax.ShapeDtypeStruct((nw,n,256),BF),
            jax.ShapeDtypeStruct((2,GROUP,WIDE),F32),
        ],
        scratch_shapes=[
            pltpu.VMEM((GROUP,n,n),F32),pltpu.VMEM((GROUP*8,FLAT),F32),pltpu.VMEM((2,n,n),F32),pltpu.VMEM((2,n,n),BF),
        ],
        compiler_params=pltpu.CompilerParams(vmem_limit_bytes=VM),
        name="attend_back", cost_estimate=cost(20),
    )(e,kT,v,qT,gT,ctxT,r,sp,l16)

def lane_maps(mirror):
    lane=np.arange(WIDE); pq=lane//16; o=lane%16
    p=pq//13; q=pq%13
    ok=(pq<169)&(o<15)
    if mirror: o=14-o
    A=o>=7; b=np.where(A,14-o,7-o); C=p>=6; d=np.where(C,12-p,6-p); E=q>=6; f=np.where(E,12-q,6-q)
    col=(b*WH+d)*WW+f
    corner=A*4+C*2+E*1
    return np.where(ok,col,-1).astype(np.int32), np.where(ok,corner,-1).astype(np.int32)

CORNER_ROWS=[(a*WH+c)*WW+e for a in (0,WT-1) for c in (0,WH-1) for e in (0,WW-1)]

def prepare_kernel(rel_ref,maps_ref,table_ref,region_ref,order_ref,l8_ref,lab_ref,narrow_ref,mk_ref,mq_ref):
    values=[]
    n=rel_ref.shape[1]
    rel=jnp.concatenate([rel_ref[row:row+1,:] for row in CORNER_ROWS],axis=0)
    hi=(rel>>6).astype(F32).astype(BF); lo=(rel&63).astype(F32).astype(BF)
    both=jnp.concatenate([hi,lo],axis=0)
    corners=lax.broadcasted_iota(jnp.int32,(8,256),0)
    rows=lax.broadcasted_iota(jnp.int32,(n,256),0)
    trow=lax.broadcasted_iota(jnp.int32,(table_ref.shape[1],256),0)
    for t in range(WIDE//256):
        c=slice(t*256,(t+1)*256)
        for version in range(2):
            col=maps_ref[2*version:2*version+1,c]; cor=maps_ref[2*version+1:2*version+2,c]
            m=jnp.where(rows==col,1.0,0.0).astype(BF)
            y=nn(both,m)
            full=y[:8]*64.0+y[8:]
            lab=jnp.sum(jnp.where(corners==cor,full,0.0),axis=0,keepdims=True)
            lab=jnp.where(cor>=0,lab,-1.0).astype(jnp.int32)
            lab_ref[version:version+1,c]=lab
            if version==0:
                hot=jnp.where(trow==lab,1.0,0.0).astype(BF)
                values.append(nn(table_ref[...],hot))
    values=jnp.concatenate(values,axis=1)
    rolled=[]
    for h in range(HEADS):
        line=jnp.broadcast_to(values[h:h+1],(8,WIDE))
        rolled.append(pltpu.roll(line,WIDE-7,1,stride=1,stride_axis=0))
    rolled=jnp.concatenate(rolled,axis=0).astype(BF)
    for t in range(FLAT//128):
        narrow_ref[:,t*128:(t+1)*128]=nn(rolled[:,t*256:(t+1)*256],l8_ref[...])
    wins=region_ref.shape[0]
    region=jnp.concatenate([region_ref[...].astype(F32),jnp.zeros((16-wins,n),F32)],axis=0).astype(BF)
    across=nt(region,order_ref[...])
    down=nt(order_ref[...],region)
    lanes=lax.broadcasted_iota(jnp.int32,(n,128),1).astype(F32)
    subs=lax.broadcasted_iota(jnp.int32,(32,n),0).astype(F32)
    for w in range(wins):
        mk_ref[w]=jnp.where(down[:,w:w+1]==lanes,1.0,0.0).astype(BF)
        mq_ref[w]=jnp.where(across[w:w+1,:]==subs,0.0,BIG).astype(BF)

def prepare(rel_index,maps,table_t,region_ids,order,l8):
    wins,n=region_ids.shape
    return pl.pallas_call(
        prepare_kernel,
        out_shape=[
            jax.ShapeDtypeStruct((2,WIDE),jnp.int32),
            jax.ShapeDtypeStruct((HEADS*8,FLAT),F32),
            jax.ShapeDtypeStruct((wins,n,128),BF),
            jax.ShapeDtypeStruct((wins,32,n),BF),
        ],
        compiler_params=pltpu.CompilerParams(vmem_limit_bytes=VM),
        name="prepare", cost_estimate=cost(6),
    )(rel_index,maps,table_t,region_ids,order,l8)

def spread_spots():
    place = np.arange(WIN_TOK)
    lane = place // (WW * WT) * 104 + place // WT % WW * 8 + place % WT + 8 * (WW - 1)
    return np.broadcast_to(lane[:, None], (WIN_TOK, 128)).astype(np.int32)


def bias_kernel(narrow_ref, spot_ref, bias_ref, held):
    heads, n, _ = bias_ref.shape
    rows = []
    for h in range(heads):
        line = narrow_ref[8 * h : 8 * h + 8, :]
        for d in range(WH):
            rows.append((pltpu.roll(line, FLAT - 104 * (WH - 1 - d), 1) if d < WH - 1 else line)[:, :SPREAD])
    rows = jnp.concatenate(rows, axis=0).astype(BF)
    spots = jnp.concatenate([spot_ref[...]] * (SPREAD // 128), axis=1)
    lanes = lax.broadcasted_iota(jnp.int32, (n, SPREAD), 1)
    for f in range(WW):
        hot = jnp.where(lanes == spots - 8 * f, 1.0, 0.0).astype(BF)
        y = nt(rows, hot)
        for h in range(heads):
            for d in range(WH):
                at = (h * WH + d) * 8
                held[h, (d * WW + f) * 8 : (d * WW + f + 1) * 8, :] = y[at : at + 8, :]
    for h in range(heads):
        bias_ref[h] = held[h].astype(BF)


def bias_half(side, narrow, spots):
    n = spots.shape[0]
    heads = HEADS // 2
    return pl.pallas_call(
        bias_kernel,
        grid=(1,),
        in_specs=[pl.BlockSpec((8 * heads, FLAT), lambda i: (side, 0)), pl.BlockSpec(spots.shape, lambda i: (0, 0))],
        out_specs=pl.BlockSpec((heads, n, n), lambda i: (0, 0, 0)),
        out_shape=jax.ShapeDtypeStruct((heads, n, n), BF),
        scratch_shapes=[pltpu.VMEM((heads, n, n), F32)],
        compiler_params=pltpu.CompilerParams(vmem_limit_bytes=VM),
        name="position_bias", cost_estimate=cost(5),
    )(narrow, spots)


def spill_kernel(lab_ref,g_ref,out_ref):
    g=g_ref[...]
    hi=g.astype(BF); r1=g-hi.astype(F32); mid=r1.astype(BF); lo=(r1-mid.astype(F32)).astype(BF)
    three=jnp.concatenate([hi,mid,lo],axis=0)
    rows=out_ref.shape[1]
    trow=lax.broadcasted_iota(jnp.int32,(rows,256),0)
    tot=jnp.zeros((48,rows),F32)
    for t in range(WIDE//256):
        c=slice(t*256,(t+1)*256)
        hot=jnp.where(trow==lab_ref[1:2,c],1.0,0.0).astype(BF)
        tot=tot+nt(three[:,c],hot)
    out_ref[...]=tot[:16]+tot[16:32]+tot[32:]

def spill(lab,g,rows):
    return pl.pallas_call(
        spill_kernel,
        out_shape=jax.ShapeDtypeStruct((HEADS,rows),F32),
        compiler_params=pltpu.CompilerParams(vmem_limit_bytes=VM),
        name="table_rows", cost_estimate=cost(5),
    )(lab,g)


BLOCK = 32
B_FC1, B_PROJ, GAIN2, BIAS2, B_FC2, GAIN1, BIAS1, B_QV = range(8)
VEC_LANES = {B_FC1: (0, 128), GAIN1: (128, 32), BIAS1: (160, 32), B_QV: (192, 64), B_PROJ: (256, 32), GAIN2: (288, 32), BIAS2: (320, 32), B_FC2: (352, 32)}
VECTOR = 384


def load_weight(own_ref, other_ref, places_ref, held, sem, vecs=None, start=True):
    core = places_ref[64]
    lanes = slice(0, held.shape[2])
    copies = []
    for i in range(16):
        rows = pl.ds(i * BLOCK, BLOCK)
        own = own_ref.at[places_ref[i]]
        copies.append(pltpu.make_async_copy(own.at[:, lanes], held.at[core, rows, :], sem.at[2 * i]))
        copies.append(
            pltpu.make_async_copy(other_ref.at[places_ref[16 + i]].at[:, lanes], held.at[1 - core, rows, :], sem.at[2 * i + 1])
        )
        if vecs is not None:
            copies.append(pltpu.make_async_copy(own.at[0:16, held.shape[2] :], vecs.at[i], sem.at[32 + i]))
    if start:
        for copy in copies:
            copy.start()
    return copies


def await_all(copies):
    for copy in copies:
        copy.wait()


def store_grad(total, places_ref, own_ref, send_ref):
    core = places_ref[64]

    def block(i, carry):
        own_ref[i, :, : total.shape[2]] = total[core, pl.ds(pl.multiple_of(places_ref[32 + i] * BLOCK, BLOCK), BLOCK), :].astype(BF)
        send_ref[i, :, : total.shape[2]] = total[1 - core, pl.ds(pl.multiple_of(places_ref[48 + i] * BLOCK, BLOCK), BLOCK), :].astype(BF)
        return carry

    lax.fori_loop(0, 16, block, 0)


def normalise(values):
    mean = jnp.mean(values, axis=-1, keepdims=True)
    centred = values - mean
    inverse = lax.rsqrt(jnp.mean(centred * centred, axis=-1, keepdims=True) + EPS)
    return centred * inverse, inverse


def project_kernel(
    places_ref, x_ref, own_ref, other_ref, q_ref, kt_ref, vt_ref, k_ref, v_ref, vec_ref, held, loose, sem
):
    @pl.when(pl.program_id(0) == 0)
    def _():
        await_all(load_weight(own_ref, other_ref, places_ref, held, sem, loose))
        rows = [loose[i].astype(F32) for i in range(16)]
        for name, (at, count) in VEC_LANES.items():
            parts = [row[at // 128 : at // 128 + 1, at % 128 : at % 128 + count] for row in rows]
            vec_ref[name : name + 1, : 16 * count] = jnp.concatenate(parts, axis=1)

    width = x_ref.shape[2]
    normed, _ = normalise(x_ref[0].astype(F32))
    first = (normed * vec_ref[GAIN1 : GAIN1 + 1, :width] + vec_ref[BIAS1 : BIAS1 + 1, :width]).astype(BF)
    left, right = nn(first, held[0]), nn(first, held[1])
    half = width // 2
    q = (left[:, :width] + vec_ref[B_QV : B_QV + 1, :width]) * SCALE
    k = jnp.concatenate([left[:, width:], right[:, :half]], axis=1)
    v = right[:, half:] + vec_ref[B_QV : B_QV + 1, width : 2 * width]
    q_ref[0] = jnp.transpose(q.astype(BF))
    kt_ref[0] = jnp.transpose(k.astype(BF))
    vt_ref[0] = jnp.transpose(v.astype(BF))
    k_ref[0] = k.astype(BF)
    v_ref[0] = v.astype(BF)


def project(places, x, own, other, hidden_width):
    nw, n, width = x.shape
    tok = pl.BlockSpec((1, n, width), lambda w, s: (w, 0, 0))
    feat = pl.BlockSpec((1, width, n), lambda w, s: (w, 0, 0))
    anywhere = pl.BlockSpec(memory_space=pl.ANY)
    vecs = (8, hidden_width)
    return pl.pallas_call(
        project_kernel,
        grid_spec=pltpu.PrefetchScalarGridSpec(
            num_scalar_prefetch=1,
            grid=(nw,),
            in_specs=[tok, anywhere, anywhere],
            out_specs=[feat, feat, feat, tok, tok, pl.BlockSpec(vecs, lambda w, s: (0, 0))],
            scratch_shapes=[
                pltpu.VMEM((2, 16 * BLOCK, own.shape[2] - 128), BF),
                pltpu.VMEM((16, 16, 128), BF),
                pltpu.SemaphoreType.DMA((48,)),
            ],
        ),
        out_shape=[jax.ShapeDtypeStruct((nw, width, n), BF)] * 3
        + [jax.ShapeDtypeStruct((nw, n, width), BF)] * 2
        + [jax.ShapeDtypeStruct(vecs, F32)],
        compiler_params=pltpu.CompilerParams(vmem_limit_bytes=VM),
        name="project", cost_estimate=cost(9),
    )(places, x, own, other)


TAIL = (0.254829592, -0.284496736, 1.421413741, -1.453152027, 1.061405429)


def normal_parts(values):
    t = pl.reciprocal(1.0 + (0.3275911 * 0.7071067811865476) * jnp.abs(values), approx=False)
    series = TAIL[4]
    for factor in TAIL[3::-1]:
        series = series * t + factor
    bell = jnp.exp2(values * values * (-0.5 * LOG2E))
    upper = (0.5 * t) * series * bell
    return jnp.where(values >= 0, 1.0 - upper, upper), bell * 0.3989422804014327


def column_sums(values):
    return jnp.sum(values, axis=0, keepdims=True)


def feed_kernel(
    places_ref, x_ref, ctx0_ref, ctx1_ref, og_ref, vec_ref, own_ref, other_ref, out_ref, mid_grad_ref, gt_ref, own_grad_ref,
    send_grad_ref, sums_ref, held, total, wide, thin, projt, sem,
):
    step = pl.program_id(0)

    @pl.when(step == 0)
    def _():
        total[...] = jnp.zeros_like(total)
        sums_ref[...] = jnp.zeros_like(sums_ref)
        await_all(load_weight(own_ref, other_ref, places_ref, held, sem))

    width = x_ref.shape[2]
    half = width // 2

    @pl.when(step == 0)
    def _():
        for j in range(2):
            projt[j] = jnp.transpose(held[j, :, :half].astype(F32)).astype(BF)

    chunk = (held.shape[2] - half) // 2
    vec = lambda row: vec_ref[row : row + 1, :width]
    ctx = (ctx0_ref[0], ctx1_ref[0])
    branch = nt(ctx[0], held[0, :, :half]) + nt(ctx[1], held[1, :, :half])
    mid = x_ref[0].astype(F32) + (branch + vec(B_PROJ))
    normed, inverse = normalise(mid)
    second = normed * vec(GAIN2) + vec(BIAS2)
    second = second.astype(BF)
    second_t = jnp.transpose(second)
    og = og_ref[0]
    og_t = jnp.transpose(og)
    mlp = jnp.zeros(mid.shape, F32)
    second_grad = jnp.zeros(mid.shape, F32)
    piece = chunk // 2
    cuts = []
    for j in range(2):
        for part in range(2):
            at = half + part * piece
            cuts.append((j, slice(at, at + piece), slice(at + chunk, at + chunk + piece), slice(j * chunk + part * piece, j * chunk + (part + 1) * piece)))

    def widen(i):
        j, c1, c2, cols = cuts[i]
        wide[0, i % 2] = nn(second, held[j, :, c1]) + vec_ref[B_FC1 : B_FC1 + 1, cols]
        wide[1, i % 2] = nn(og, held[j, :, c2])

    widen(0)
    for i, (j, c1, c2, cols) in enumerate(cuts):
        hidden = wide[0, i % 2]
        phi_sum, density = normal_parts(hidden)
        thin[0, i % 2] = (hidden * phi_sum).astype(BF)
        hidden_grad = wide[1, i % 2] * (phi_sum + hidden * density)
        sums_ref[0:1, cols] += column_sums(hidden_grad)
        thin[1, i % 2] = hidden_grad.astype(BF)
        if i + 1 < len(cuts):
            widen(i + 1)
        mlp += nt(thin[0, i % 2], held[j, :, c2])
        second_grad += nt(thin[1, i % 2], held[j, :, c1])
        total[j, :, c1] += nn(second_t, thin[1, i % 2])
        total[j, :, c2] += nn(og_t, thin[0, i % 2])
    out_ref[0] = (mid + (mlp + vec(B_FC2))).astype(BF)
    scaled = second_grad * vec(GAIN2)
    inner = jnp.mean(scaled, axis=-1, keepdims=True)
    along = jnp.mean(scaled * normed, axis=-1, keepdims=True)
    og = og.astype(F32)
    mid_grad = og + inverse * (scaled - inner - normed * along)
    mid_grad_ref[0] = mid_grad
    low = mid_grad.astype(BF)
    sums_ref[1:2, :width] += column_sums(mid_grad)
    sums_ref[2:3, :width] += column_sums(second_grad * normed)
    sums_ref[3:4, :width] += column_sums(second_grad)
    sums_ref[4:5, :width] += column_sums(og)
    low_t = jnp.transpose(low)
    for j in range(2):
        total[j, :, :half] += nn(low_t, ctx[j])
        proj = projt[j]
        gt_ref[0, j * half : (j + 1) * half, :] = nn(proj, low_t).astype(BF)

    @pl.when(step == pl.num_programs(0) - 1)
    def _():
        store_grad(total, places_ref, own_grad_ref, send_grad_ref)


def feed(places, x, ctx0, ctx1, og, vecs, own, other):
    nw, n, width = x.shape
    tok = pl.BlockSpec((1, n, width), lambda w, s: (w, 0, 0))
    feat = pl.BlockSpec((1, width, n), lambda w, s: (w, 0, 0))
    whole = pl.BlockSpec(own.shape, lambda w, s: (0, 0, 0))
    anywhere = pl.BlockSpec(memory_space=pl.ANY)
    side = pl.BlockSpec((1, n, width // 2), lambda w, s: (w, 0, 0))
    hidden_width = own.shape[2] - width // 2
    return pl.pallas_call(
        feed_kernel,
        grid_spec=pltpu.PrefetchScalarGridSpec(
            num_scalar_prefetch=1,
            grid=(nw,),
            in_specs=[tok, side, side, tok, pl.BlockSpec(vecs.shape, lambda w, s: (0, 0)), anywhere, anywhere],
            out_specs=[tok, tok, feat, whole, whole, pl.BlockSpec((8, hidden_width), lambda w, s: (0, 0))],
            scratch_shapes=[
                pltpu.VMEM((2, 16 * BLOCK, own.shape[2]), BF),
                pltpu.VMEM((2, 16 * BLOCK, own.shape[2]), F32),
                pltpu.VMEM((2, 2, n, hidden_width // 4), F32),
                pltpu.VMEM((2, 2, n, hidden_width // 4), BF),
                pltpu.VMEM((2, width // 2, 16 * BLOCK), BF),
                pltpu.SemaphoreType.DMA((32,)),
            ],
        ),
        out_shape=[
            jax.ShapeDtypeStruct((nw, n, width), BF),
            jax.ShapeDtypeStruct((nw, n, width), F32),
            jax.ShapeDtypeStruct((nw, width, n), BF),
            jax.ShapeDtypeStruct(own.shape, BF),
            jax.ShapeDtypeStruct(own.shape, BF),
            jax.ShapeDtypeStruct((8, hidden_width), F32),
        ],
        compiler_params=pltpu.CompilerParams(vmem_limit_bytes=VM),
        name="feed_forward", cost_estimate=cost(44),
    )(places, x, ctx0, ctx1, og, vecs, own, other)


def input_kernel(
    places_ref, x_ref, dq0, dk0, dv0, dq1, dk1, dv1, mid_grad_ref, vec_ref, fc_sums_ref,
    own_ref, other_ref, out_ref, own_grad_ref, send_grad_ref, held, total, sums, small, sem,
):
    step = pl.program_id(0)

    @pl.when(step == 0)
    def _():
        total[...] = jnp.zeros_like(total)
        sums[...] = jnp.zeros_like(sums)
        load_weight(own_ref, other_ref, places_ref, held, sem)

    width = x_ref.shape[2]
    half = width // 2
    vec = lambda row: vec_ref[row : row + 1, :width]
    normed, inverse = normalise(x_ref[0].astype(F32))
    first_t = jnp.transpose((normed * vec(GAIN1) + vec(BIAS1)).astype(BF))
    left = jnp.concatenate([dq0[0], dq1[0], dk0[0]], axis=1)
    right = jnp.concatenate([dk1[0], dv0[0], dv1[0]], axis=1)
    total[0] += nn(first_t, left)
    total[1] += nn(first_t, right)

    @pl.when(step == 0)
    def _():
        await_all(load_weight(own_ref, other_ref, places_ref, held, sem, start=False))

    first_grad = (nt(left, held[0]) + nt(right, held[1])).astype(BF).astype(F32)
    scaled = first_grad * vec(GAIN1)
    inner = jnp.mean(scaled, axis=-1, keepdims=True)
    along = jnp.mean(scaled * normed, axis=-1, keepdims=True)
    out_ref[0] = (mid_grad_ref[0] + inverse * (scaled - inner - normed * along)).astype(BF)
    sums[0:1, :width] += column_sums(first_grad * normed)
    sums[1:2, :width] += column_sums(first_grad)
    sums[2:3, :width] += column_sums(left[:, :width].astype(F32))
    sums[2:3, width:] += column_sums(right[:, half:].astype(F32))

    @pl.when(step == pl.num_programs(0) - 1)
    def _():
        columns = total.shape[2]
        store_grad(total, places_ref, own_grad_ref, send_grad_ref)
        rows = {
            B_FC1: fc_sums_ref[0:1, :], B_PROJ: fc_sums_ref[1:2, :], GAIN2: fc_sums_ref[2:3, :], BIAS2: fc_sums_ref[3:4, :],
            B_FC2: fc_sums_ref[4:5, :], GAIN1: sums[0:1, :], BIAS1: sums[1:2, :], B_QV: sums[2:3, :],
        }
        for i in range(16):
            parts = [rows[name][:, i * count : (i + 1) * count] for name, (_, count) in VEC_LANES.items()]
            line = jnp.concatenate(parts, axis=1)
            small[i] = jnp.concatenate([line[:, :128], line[:, 128:256], line[:, 256:], jnp.zeros((BLOCK - 3, 128), F32)], axis=0)

        def block(i, carry):
            own_grad_ref[i, :, columns:] = small[places_ref[32 + i]].astype(BF)
            send_grad_ref[i, :, columns:] = small[places_ref[48 + i]].astype(BF)
            return carry

        lax.fori_loop(0, 16, block, 0)


def input_side(places, x, groups, mid_grad, vecs, fc_sums, own, other):
    nw, n, width = x.shape
    tok = pl.BlockSpec((1, n, width), lambda w, s: (w, 0, 0))
    part = pl.BlockSpec((1, n, width // 2), lambda w, s: (w, 0, 0))
    flat = lambda shape: pl.BlockSpec(shape, lambda w, s: (0,) * len(shape))
    anywhere = pl.BlockSpec(memory_space=pl.ANY)
    columns = own.shape[2] - 128
    grad = own.shape
    return pl.pallas_call(
        input_kernel,
        grid_spec=pltpu.PrefetchScalarGridSpec(
            num_scalar_prefetch=1,
            grid=(nw,),
            in_specs=[tok] + [part] * 6 + [tok, flat(vecs.shape), flat(fc_sums.shape), anywhere, anywhere],
            out_specs=[tok, flat(grad), flat(grad)],
            scratch_shapes=[
                pltpu.VMEM((2, 16 * BLOCK, columns), BF),
                pltpu.VMEM((2, 16 * BLOCK, columns), F32),
                pltpu.VMEM((8, 2 * width), F32),
                pltpu.VMEM((16, BLOCK, 128), F32),
                pltpu.SemaphoreType.DMA((32,)),
            ],
        ),
        out_shape=[
            jax.ShapeDtypeStruct((nw, n, width), BF),
            jax.ShapeDtypeStruct(grad, BF),
            jax.ShapeDtypeStruct(grad, BF),
        ],
        compiler_params=pltpu.CompilerParams(vmem_limit_bytes=VM),
        name="input_side", cost_estimate=cost(15),
    )(places, x, *[part for group in groups for part in group[:3]], mid_grad, vecs, fc_sums, own, other)


def from_partner(shard, axis, stride):
    return lax.ppermute(shard, axis, [(i, i ^ 1 << stride) for i in range(lax.axis_size(axis))])


def to_block(windows, local_count):
    clip_count, chans = (windows.shape[0], windows.shape[-1])
    parted = windows.reshape(
        clip_count, local_count[0], local_count[1], local_count[2], WT, WH, WW, chans
    )
    parted = parted.transpose(0, 1, 4, 2, 5, 3, 6, 7)
    return parted.reshape(
        clip_count, local_count[0] * WT, local_count[1] * WH, local_count[2] * WW, chans
    )


def from_block(block, local_count):
    clip_count, chans = (block.shape[0], block.shape[-1])
    parted = block.reshape(
        clip_count, local_count[0], WT, local_count[1], WH, local_count[2], WW, chans
    )
    parted = parted.transpose(0, 1, 3, 5, 2, 4, 6, 7)
    return parted.reshape(clip_count, -1, WT * WH * WW, chans)


def roll_ahead(windows, local_count, bit_list):
    block = to_block(windows, local_count)
    for grid_dim, amount, bit_pos in (
        (1, WT // 2, bit_list[0]),
        (2, WH // 2, bit_list[1]),
        (3, WW // 2, bit_list[2]),
    ):
        if bit_pos < 0:
            block = jnp.roll(block, -amount, axis=grid_dim)
        else:
            front = lax.slice_in_dim(block, 0, amount, axis=grid_dim)
            arrived = from_partner(front, "seq", bit_pos)
            rest = lax.slice_in_dim(block, amount, block.shape[grid_dim], axis=grid_dim)
            block = jnp.concatenate([rest, arrived], axis=grid_dim)
    return from_block(block, local_count)


def roll_behind(windows, local_count, bit_list):
    block = to_block(windows, local_count)
    for grid_dim, amount, bit_pos in (
        (1, WT // 2, bit_list[0]),
        (2, WH // 2, bit_list[1]),
        (3, WW // 2, bit_list[2]),
    ):
        if bit_pos < 0:
            block = jnp.roll(block, amount, axis=grid_dim)
        else:
            extent = block.shape[grid_dim]
            trailing = lax.slice_in_dim(block, extent - amount, extent, axis=grid_dim)
            arrived = from_partner(trailing, "seq", bit_pos)
            rest = lax.slice_in_dim(block, 0, extent - amount, axis=grid_dim)
            block = jnp.concatenate([arrived, rest], axis=grid_dim)
    return from_block(block, local_count)


KEEP = WT // 2 * WH * WW


def hwt_order():
    place = np.arange(WIN_TOK)
    return (place % WT * WH + place // (WW * WT)) * WW + place // WT % WW


def order_ones(shift):
    place = np.arange(WIN_TOK)
    out = np.zeros((WIN_TOK, WIN_TOK), np.float32)
    out[place, ((place + shift) % WT * WH + place // (WW * WT)) * WW + place // WT % WW] = 1
    return out


def tile_runs(win):
    runs = []
    for c in range(WH):
        h = (win // 2 * WH + c + WH // 2) % (2 * WH)
        for e, count in ((0, WW - WW // 2), (WW - WW // 2, WW // 2)):
            w = (win % 2 * WW + e + WW // 2) % (2 * WW)
            runs.append((h // WH * 2 + w // WW, h % WH * WW + w % WW, count))
    return runs


def swap_cores(part):
    return lax.ppermute(part, "seq", [(0, 1), (1, 0)])


def enter_kernel(own_ref, arrived_ref, order_ref, out_ref, held):
    _, n, width = own_ref.shape
    rows = lax.broadcasted_iota(jnp.int32, (n, width), 0)
    for source in range(4):
        values = jnp.where(rows >= KEEP, own_ref[source].astype(F32), arrived_ref[source].astype(F32)).astype(BF)
        held[source] = nn(order_ref[...], values)
    for win in range(4):
        parts = [held[source, 8 * at : 8 * (at + count), :] for source, at, count in tile_runs(win)]
        out_ref[win] = jnp.concatenate(parts, axis=0).astype(BF)


def leave_kernel(rows_ref, order_ref, out_ref, send_ref, held):
    for win in range(4):
        values = rows_ref[win].astype(F32)
        start = 0
        for source, at, count in tile_runs(win):
            held[source, 8 * at : 8 * (at + count), :] = values[8 * start : 8 * (start + count), :]
            start += count
    for source in range(4):
        values = nn(order_ref[...], held[source].astype(BF)).astype(out_ref.dtype)
        out_ref[source] = values
        send_ref[source] = values[: send_ref.shape[1]].astype(BF)


SENT = 208


def enter(windows, plan, arrived=None):
    clips, wins, toks, width = windows.shape
    if plan["levels"] == 1 and clips == 1:
        own = windows.reshape(wins, toks, width)
        block = (wins, toks, width // 2)
        part = pl.BlockSpec(block, lambda i: (0, 0, i))
        return pl.pallas_call(
            enter_kernel,
            grid=(2,),
            in_specs=[part, part, pl.BlockSpec((toks, toks), lambda i: (0, 0))],
            out_specs=part,
            out_shape=jax.ShapeDtypeStruct(own.shape, BF),
            scratch_shapes=[pltpu.VMEM(block, F32)],
            compiler_params=pltpu.CompilerParams(vmem_limit_bytes=VM),
            name="enter", cost_estimate=cost(4),
        )(own, arrived.reshape(own.shape), plan["order"])
    rolled = roll_ahead(windows, plan["local"], plan["bits"])
    rolled = rolled.reshape(clips * wins, WT, WH * WW, width).transpose(0, 2, 1, 3)
    return rolled.reshape(clips * wins, toks, width)


def leave(windows, plan, kind):
    wins, toks, width = windows.shape
    block = (wins, toks, width // 2)
    part = pl.BlockSpec(block, lambda i: (0, 0, i))
    return pl.pallas_call(
        leave_kernel,
        grid=(2,),
        in_specs=[part, pl.BlockSpec((toks, toks), lambda i: (0, 0))],
        out_specs=[part, pl.BlockSpec((wins, SENT, width // 2), lambda i: (0, 0, i))],
        out_shape=[jax.ShapeDtypeStruct(windows.shape, kind), jax.ShapeDtypeStruct((wins, SENT, width), BF)],
        scratch_shapes=[pltpu.VMEM(block, F32)],
        compiler_params=pltpu.CompilerParams(vmem_limit_bytes=VM),
        name="leave", cost_estimate=cost(4),
    )(windows, plan["order"].T)


def joined(kept, arrived):
    arrived = jnp.pad(arrived.astype(kept.dtype), ((0, 0), (0, kept.shape[1] - SENT), (0, 0)))
    rows = lax.broadcasted_iota(jnp.int32, kept.shape, 1)
    return jnp.where(rows < KEEP, arrived, kept)[None]


def leave_any(windows, plan, clips, kind):
    count, toks, width = windows.shape
    wins = count // clips
    if plan["levels"] == 1 and clips == 1:
        kept, sent = leave(windows, plan, kind)
        return joined(kept, swap_cores(sent))
    rows = windows.reshape(count, WH * WW, WT, width).transpose(0, 2, 1, 3)
    return roll_behind(rows.reshape(clips, wins, toks, width), plan["local"], plan["bits"]).astype(kind)


def pack_kernel(core_ref, qkv_ref, proj_ref, fc1_ref, fc2_ref, *rest):
    vec_refs, (qkv_out, fc_out) = rest[:-2], rest[-2:]

    def emit(side):
        half = qkv_ref.shape[1] // 2
        qkv_out[:, :half] = qkv_ref[:, side * half : (side + 1) * half]
        at = 0
        for ref in (proj_ref, fc1_ref, fc2_ref):
            half = ref.shape[1] // 2
            fc_out[:, at : at + half] = ref[:, side * half : (side + 1) * half]
            at += half

    half = qkv_ref.shape[1] // 2
    line = jnp.concatenate([ref[...].astype(F32).reshape(1, -1) for ref in vec_refs], axis=1)
    lines = [line[:, at : at + 128] for at in range(0, VECTOR, 128)]
    qkv_out[:, half:] = jnp.concatenate(lines + [jnp.zeros((BLOCK - len(lines), 128), F32)], axis=0).astype(BF)
    for side in range(2):
        @pl.when(core_ref[0] == side)
        def _():
            emit(side)


def pack(core, qkv, proj_t, fc1, fc2_t, vectors):
    columns = (proj_t.shape[1] + fc1.shape[1] + fc2_t.shape[1]) // 2
    vmem = pl.BlockSpec(memory_space=pltpu.VMEM)
    return pl.pallas_call(
        pack_kernel,
        in_specs=[pl.BlockSpec(memory_space=pltpu.SMEM)] + [vmem] * (4 + len(vectors)),
        out_shape=[
            jax.ShapeDtypeStruct((BLOCK, qkv.shape[1] // 2 + 128), BF),
            jax.ShapeDtypeStruct((BLOCK, columns), BF),
        ],
        compiler_params=pltpu.CompilerParams(vmem_limit_bytes=VM),
        name="pack", cost_estimate=cost(2),
    )(core, qkv, proj_t, fc1, fc2_t, *vectors)


def hop(part, flips):
    pairs = [(16 * c + s, 16 * c + (s ^ flips[c])) for c in range(2) for s in range(16)]
    return lax.ppermute(part, ("seq", "shard"), pairs)


def tree_places():
    me = lax.axis_index("shard")
    core = lax.axis_index("seq")
    entry = jnp.arange(16, dtype=jnp.int32)
    v, u, z = entry // 8, entry // 4 % 2, entry % 4
    straight, crossed = me ^ (4 * z + 2 * u + v), me ^ (4 * z + 2 * v + u)
    rel = me ^ entry
    z, y, x = rel // 4, rel // 2 % 2, rel % 2
    place_straight, place_crossed = x * 8 + y * 4 + z, y * 8 + x * 4 + z
    even = core == 0
    pick_core = lambda left, right: jnp.where(even, left, right)
    return jnp.concatenate(
        [
            pick_core(place_straight, place_crossed),
            pick_core(place_crossed, place_straight),
            pick_core(straight, crossed),
            pick_core(crossed, straight),
            jnp.broadcast_to(core, (1,)),
        ]
    ).astype(jnp.int32)


def tree_gather(part):
    arrived = yield [hop(part, (4 * k, 4 * k)) for k in range(1, 4)]
    stack = jnp.stack([part] + arrived)
    arrived = yield hop(stack, (2, 1))
    stack = jnp.concatenate([stack, arrived])
    arrived = yield hop(stack, (1, 2))
    stack = jnp.concatenate([stack, arrived])
    other = yield swap_cores(stack)
    yield stack, other


def tie(*items):
    return lax.optimization_barrier(items)


def add_low(left, right):
    return (left.astype(F32) + right.astype(F32)).astype(BF)


def tree_scatter(own, send):
    arrived = yield swap_cores(send)
    stack = add_low(own, arrived)
    arrived = yield hop(stack[8:], (1, 2))
    stack = add_low(stack[:8], arrived)
    arrived = yield hop(stack[4:], (2, 1))
    stack = add_low(stack[:4], arrived)
    arrived = yield [hop(stack[k], (4 * k, 4 * k)) for k in range(1, 4)]
    arrived = [part.astype(F32) for part in arrived]
    yield (stack[0].astype(F32) + arrived[0]) + (arrived[1] + arrived[2])


def finish(steps, pending):
    while True:
        try:
            pending = steps.send(pending)
        except StopIteration:
            return pending


def table_sum(table):
    for axis, flip in (("seq", 1), ("shard", 1), ("shard", 2)):
        pairs = [(i, i ^ flip) for i in range(2 if axis == "seq" else 16)]
        arrived = yield lax.ppermute(table, axis, pairs)
        table = add_low(table, arrived)
    arrived = yield [hop(table, (4 * k, 4 * k)) for k in range(1, 4)]
    arrived = [part.astype(F32) for part in arrived]
    yield (table.astype(F32) + arrived[0]) + (arrived[1] + arrived[2])


def sides(part, other, core):
    other = other.astype(F32)
    return [jnp.where(core == 0, part, other), jnp.where(core == 0, other, part)]


def body(
    tokens, norm1_gain, norm1_bias, qkv_weight, qv_bias, position_table, proj_weight, proj_bias, norm2_gain,
    norm2_bias, fc1_weight, fc1_bias, fc2_weight, fc2_bias, rel_index, region_ids, cotangent,
):
    levels = lax.axis_size("seq").bit_length() - 1
    clips, wins, toks, width = tokens.shape
    hidden_width = fc1_weight.shape[1]
    plan = {
        "levels": levels,
        "local": [1 if levels > level_pos else 2 for level_pos in range(3)],
        "bits": [levels - 1 - level_pos for level_pos in range(3)],
        "order": jnp.asarray(order_ones(WT // 2), BF),
    }

    def fc_outputs(pair):
        cut = (width // 2, (width + hidden_width) // 2)
        return [jnp.concatenate(two, axis=1) for two in zip(*(jnp.split(part, cut, axis=1) for part in pair))]

    vectors = [fc1_bias, norm1_gain, norm1_bias, qv_bias, proj_bias, norm2_gain, norm2_bias, fc2_bias]
    sizes = [part.shape[0] for part in vectors]
    spread = jnp.asarray(spread_ones(), BF)
    spots = jnp.asarray(spread_spots())
    wide8 = jnp.asarray(lane16(False).T, BF)
    wide16 = jnp.asarray(lane16(True), BF)
    maps = jnp.asarray(np.stack(lane_maps(False) + lane_maps(True)))
    table = prepare(rel_index, maps, position_table.T, region_ids, jnp.asarray(order_ones(0), BF), wide8)
    if clips == 1 and lax.axis_size("shard") == 16 and lax.axis_size("seq") == 2:
        core = lax.axis_index("seq")
        places = tree_places()
        qkv_part, fc_part = pack(
            jnp.reshape(core, (1,)), qkv_weight, proj_weight.T, fc1_weight, fc2_weight.T, vectors
        )
        qkv_steps, fc_steps = tree_gather(qkv_part), tree_gather(fc_part)
        qkv_hop = next(qkv_steps)
        arrived = swap_cores(tokens)
        table, qkv_hop, arrived = tie(table, qkv_hop, arrived)
        labels, narrow, mask_keys, mask_queries = table
        qkv_hop = qkv_steps.send(qkv_hop)
        shifted = enter(tokens, plan, arrived)
        qkv_hop, shifted, narrow, fc_part = tie(qkv_hop, shifted, narrow, fc_part)
        qkv_hop = qkv_steps.send(qkv_hop)
        fc_hop = next(fc_steps)
        bias_low = bias_half(0, narrow, spots)
        arrived = swap_cores(cotangent)
        qkv_hop, bias_low, arrived, narrow = tie(qkv_hop, bias_low, arrived, narrow)
        qkv_hop = qkv_steps.send(qkv_hop)
        out_grad = enter(cotangent, plan, arrived)
        qkv_hop, out_grad, fc_hop = tie(qkv_hop, out_grad, fc_hop)
        qkv_own, qkv_other = qkv_steps.send(qkv_hop)
        fc_hop = fc_steps.send(fc_hop)
        q_t, k_t, v_t, token_k, token_v, vecs = project(places, shifted, qkv_own, qkv_other, hidden_width)
        q_t, fc_hop = tie(q_t, fc_hop)
        fc_hop = fc_steps.send(fc_hop)
        low = attend(0, q_t, token_k, v_t, bias_low, mask_queries, mask_keys)
        narrow, low = tie(narrow, low)
        bias_high = bias_half(1, narrow, spots)
        q_t, low, fc_hop, bias_high = tie(q_t, low, fc_hop, bias_high)
        fc_hop = fc_steps.send(fc_hop)
        high = attend(1, q_t, token_k, v_t, bias_high, mask_queries, mask_keys)
        high, fc_hop = tie(high, fc_hop)
        fc_own, fc_other = fc_steps.send(fc_hop)
        block_out, mid_grad, context_grad_t, fc_keep, fc_send, fc_sums = feed(
            places, shifted, low[1], high[1], out_grad, vecs, fc_own, fc_other
        )
        fc_steps = tree_scatter(fc_keep, fc_send)
        fc_hop = next(fc_steps)
        groups = []
        for side, (context_t, _, expo, inverse_sum) in enumerate((low, high)):
            group = attend_back(
                side, expo, k_t, token_v, q_t, context_grad_t, context_t, inverse_sum, spread, wide16
            )
            group, fc_hop, context_grad_t, block_out = tie(group, fc_hop, context_grad_t, block_out)
            groups.append(group)
            fc_hop = fc_steps.send(fc_hop)
        offsets = jnp.concatenate([group[3] for group in groups]).reshape(HEADS, WIDE)
        table_steps = table_sum(offsets.astype(BF))
        table_hop = next(table_steps)
        input_grad, qkv_keep, qkv_send = input_side(
            places, shifted, groups, mid_grad, vecs, fc_sums, qkv_own, qkv_other
        )
        input_grad, qkv_send, fc_hop, table_hop, block_out = tie(input_grad, qkv_send, fc_hop, table_hop, block_out)
        qkv_steps = tree_scatter(qkv_keep, qkv_send)
        qkv_hop = next(qkv_steps)
        fc_hop = fc_steps.send(fc_hop)
        table_hop = table_steps.send(table_hop)
        kept, sent = leave(input_grad, plan, F32)
        qkv_hop, table_hop, kept, sent, block_out = tie(qkv_hop, table_hop, kept, sent, block_out)
        qkv_hop = qkv_steps.send(qkv_hop)
        table_hop = table_steps.send(table_hop)
        arrived = swap_cores(sent)
        out_kept, out_sent = leave(block_out, plan, BF)
        qkv_hop, table_hop, fc_hop, arrived, out_kept, out_sent = tie(qkv_hop, table_hop, fc_hop, arrived, out_kept, out_sent)
        qkv_hop = qkv_steps.send(qkv_hop)
        table_hop = table_steps.send(table_hop)
        own_fc = finish(fc_steps, fc_hop)
        out_arrived = swap_cores(out_sent)
        fc_swap = swap_cores(own_fc.astype(BF))
        input_grad = joined(kept, arrived)
        qkv_hop, table_hop, input_grad, fc_swap, out_arrived = tie(qkv_hop, table_hop, input_grad, fc_swap, out_arrived)
        qkv_hop = qkv_steps.send(qkv_hop)
        offsets = finish(table_steps, table_hop)
        block_out = joined(out_kept, out_arrived)
        own_fc = fc_outputs(sides(own_fc, fc_swap, core))
        table_grad = spill(labels, offsets, position_table.shape[0])
        qkv_hop, block_out, own_fc, table_grad = tie(qkv_hop, block_out, own_fc, table_grad)
        own_qkv = finish(qkv_steps, qkv_hop)
        small = own_qkv[: VECTOR // 128, width * 3 // 2 :].reshape(-1)
        own_qkv = own_qkv[:, : width * 3 // 2]
        own_qkv = sides(own_qkv, swap_cores(own_qkv.astype(BF)), core)
    else:
        straight = np.arange(16)
        places = jnp.asarray(np.concatenate([straight, straight, straight, straight, np.zeros(1)]), jnp.int32)
        gather = lambda part: lax.all_gather(part, "shard", axis=0, tiled=True)
        halves = lambda part: jnp.split(part, 2, axis=1)
        parts = [halves(gather(part)) for part in (proj_weight.T, fc1_weight, fc2_weight.T)]
        fc_own, fc_other = (jnp.concatenate(pair, axis=1).reshape(16, BLOCK, -1) for pair in zip(*parts))
        rows = lax.all_gather(jnp.concatenate(vectors), "shard", axis=0, tiled=False)
        pieces = [piece.reshape(16, -1) for piece in jnp.split(rows, np.cumsum(sizes)[:-1], axis=1)]
        rows = jnp.pad(jnp.concatenate(pieces, axis=1).reshape(16, -1, 128), ((0, 0), (0, BLOCK - VECTOR // 128), (0, 0)))
        qkv_own, qkv_other = (
            jnp.concatenate([part.reshape(16, BLOCK, -1), rows], axis=2) for part in halves(gather(qkv_weight))
        )
        shifted = enter(tokens, plan, swap_cores(tokens) if levels == 1 else None)
        out_grad = enter(cotangent, plan, swap_cores(cotangent) if levels == 1 else None)
        labels, narrow, mask_keys, mask_queries = table
        bias_low, bias_high = (bias_half(side, narrow, spots) for side in range(2))
        q_t, k_t, v_t, token_k, token_v, vecs = project(places, shifted, qkv_own, qkv_other, hidden_width)
        low = attend(0, q_t, token_k, v_t, bias_low, mask_queries, mask_keys)
        high = attend(1, q_t, token_k, v_t, bias_high, mask_queries, mask_keys)
        block_out, mid_grad, context_grad_t, fc_keep, fc_send, fc_sums = feed(
            places, shifted, low[1], high[1], out_grad, vecs, fc_own, fc_other
        )
        groups = [
            attend_back(side, expo, k_t, token_v, q_t, context_grad_t, context_t, inverse_sum, spread, wide16)
            for side, (context_t, _, expo, inverse_sum) in enumerate((low, high))
        ]
        input_grad, qkv_keep, qkv_send = input_side(
            places, shifted, groups, mid_grad, vecs, fc_sums, qkv_own, qkv_other
        )
        block_out = leave_any(block_out, plan, clips, BF)
        input_grad = leave_any(input_grad, plan, clips, F32)
        offsets = jnp.concatenate([group[3] for group in groups]).reshape(HEADS, WIDE)
        table_grad = spill(labels, lax.psum(offsets, ("seq", "shard")), position_table.shape[0])
        small = qkv_keep[:, : VECTOR // 128, width * 3 // 2 :].reshape(16, VECTOR)
        small = lax.psum(small.astype(F32), ("seq", "shard"))
        pieces = jnp.split(small, np.cumsum([count for _, count in VEC_LANES.values()])[:-1], axis=1)
        shards = lax.axis_size("shard")
        small = jnp.concatenate([piece.reshape(shards, -1) for piece in pieces], axis=1)
        small = lax.dynamic_index_in_dim(small, lax.axis_index("shard"), 0, keepdims=False)

        def owned(grad):
            grad = lax.psum(grad.reshape(16 * BLOCK, -1), "seq")
            return lax.psum_scatter(grad, "shard", scatter_dimension=0, tiled=True).astype(F32)

        own_fc = fc_outputs([owned(fc_keep), owned(fc_send)])
        own_qkv = [owned(qkv_keep[:, :, : width * 3 // 2]), owned(qkv_send[:, :, : width * 3 // 2])]
    own_proj, own_fc1, own_fc2 = own_fc
    own_qkv = jnp.concatenate(own_qkv, axis=1)
    own_f1b, own_g1, own_b1, own_qv, own_pb, own_g2, own_b2, own_f2b = jnp.split(small, np.cumsum(sizes)[:-1])
    return (
        block_out, input_grad, own_g1, own_b1, own_qkv, own_qv, table_grad.T, own_proj.T, own_pb,
        own_g2, own_b2, own_fc1, own_f1b, own_fc2.T, own_f2b,
    )


def solution(mesh):
    return jax.shard_map(
        body,
        mesh=mesh,
        in_specs=(
            P("shard", "seq", None, None),
            P("shard"),
            P("shard"),
            P("shard", None),
            P("shard"),
            P(),
            P(None, "shard"),
            P("shard"),
            P("shard"),
            P("shard"),
            P("shard", None),
            P("shard"),
            P(None, "shard"),
            P("shard"),
            P(),
            P("seq", None),
            P("shard", "seq", None, None),
        ),
        out_specs=(
            P("shard", "seq", None, None),
            P("shard", "seq", None, None),
            P("shard"),
            P("shard"),
            P("shard", None),
            P("shard"),
            P(),
            P(None, "shard"),
            P("shard"),
            P("shard"),
            P("shard"),
            P("shard", None),
            P("shard"),
            P(None, "shard"),
            P("shard"),
        ),
        check_vma=False,
    )
```

```python
import functools

import jax
import jax.numpy as jnp
import numpy as np
from jax import lax
from jax.experimental import pallas as pl
from jax.experimental.pallas import tpu as pltpu
from jax.sharding import PartitionSpec as P

HEADS = 16
HEAD_DIM = 32
WT = 8
WH = 7
WW = 7
WIN_TOK = WT * WH * WW
EPS = 1e-05

BF=jnp.bfloat16; F32=jnp.float32
LOG2E=1.4426950408889634; LN2=0.6931471805599453
SCALE=HEAD_DIM**-0.5
BIG=-(2.0**30)
GROUP=4
VM=54*1024*1024

def cost(micros):
    return pl.CostEstimate(flops=int(micros * 1e9), bytes_accessed=int(micros * 3.6e6), transcendentals=0)


def nt(a,b): return lax.dot_general(a,b,(((1,),(1,)),((),())),preferred_element_type=F32)
def nn(a,b): return jnp.dot(a,b,preferred_element_type=F32)

def placed(block, at, rows):
    parts=[]
    if at: parts.append(jnp.zeros((at,block.shape[1]),block.dtype))
    parts.append(block)
    if rows-at-block.shape[0]: parts.append(jnp.zeros((rows-at-block.shape[0],block.shape[1]),block.dtype))
    return jnp.concatenate(parts,axis=0)

PAIR = 2 * GROUP
SAFE = 2.0**60


def attend_kernel(
    q_ref, k_ref, v_ref, bias_ref, mq_ref, mk_ref, ctx_ref, ctx_tok_ref, e_ref, r_ref, scores
):
    n = q_ref.shape[2]
    ones = jnp.ones((16, n), BF)
    mask_rows = placed(mq_ref[0], 0, 128)
    lhs = [jnp.concatenate([k_ref[0, :, 128 * g : 128 * (g + 1)], mk_ref[0]], axis=1) for g in range(2)]
    rows = lambda h: slice(h * HEAD_DIM, (h + 1) * HEAD_DIM)

    def score(h):
        rhs = jnp.concatenate([placed(q_ref[0, rows(h), :], h % GROUP * HEAD_DIM, 128), mask_rows], axis=0)
        scores[h % 2] = nn(lhs[h // GROUP], rhs)

    def context(h):
        c = nn(jnp.concatenate([v_ref[0, rows(h), :], ones], axis=0), e_ref[0, h])
        total = c[HEAD_DIM : HEAD_DIM + 1]
        r = 1.0 / total
        ctx_ref[0, rows(h), :] = (c[:HEAD_DIM] * r).astype(BF)
        r_ref[0, h : h + 1, :] = r
        return total

    totals = []
    score(0)
    for h in range(PAIR):
        if h + 1 < PAIR:
            score(h + 1)
        e_ref[0, h] = jnp.exp(scores[h % 2] + bias_ref[h].astype(F32)).astype(BF)
        if h:
            totals.append(context(h - 1))
    totals.append(context(PAIR - 1))
    every = jnp.concatenate(totals, axis=0)
    ordinary = jnp.logical_and(jnp.min(every) > 1.0 / SAFE, jnp.max(every) < SAFE)

    ctx_tok_ref[0] = jnp.transpose(ctx_ref[0])

    @pl.when(jnp.logical_not(ordinary))
    def _():
        spot = lax.broadcasted_iota(jnp.int32, (128, n), 0) // HEAD_DIM

        def again(h, carry):
            at = pl.ds(pl.multiple_of(h * HEAD_DIM, HEAD_DIM), HEAD_DIM)
            group = pl.ds(pl.multiple_of(h // GROUP * 128, 128), 128)
            q = jnp.concatenate([q_ref[0, at, :].astype(F32)] * GROUP, axis=0)
            rhs = jnp.where(spot == h % GROUP, q, 0.0).astype(BF)
            s = nn(jnp.concatenate([k_ref[0, :, group], mk_ref[0]], axis=1), jnp.concatenate([rhs, mask_rows], axis=0))
            s = s + bias_ref[h].astype(F32)
            e = jnp.exp(s - jnp.max(s, axis=0, keepdims=True)).astype(BF)
            e_ref[0, h] = e
            c = nn(jnp.concatenate([v_ref[0, at, :], ones], axis=0), e)
            r = 1.0 / c[HEAD_DIM : HEAD_DIM + 1]
            ctx_ref[0, at, :] = (c[:HEAD_DIM] * r).astype(BF)
            r_ref[0, pl.ds(h, 1), :] = r
            return carry

        lax.fori_loop(0, PAIR, again, 0)
        ctx_tok_ref[0] = jnp.transpose(ctx_ref[0])


def attend(side,qT,k,vT,bias,mq,mk):
    nw,width,n=qT.shape
    half=width//2
    wins=mk.shape[0]
    return pl.pallas_call(
        attend_kernel,
        grid=(nw,),
        in_specs=[
            pl.BlockSpec((1,half,n),lambda w:(w,side,0)),
            pl.BlockSpec((1,n,half),lambda w:(w,0,side)),
            pl.BlockSpec((1,half,n),lambda w:(w,side,0)),
            pl.BlockSpec((PAIR,n,n),lambda w:(0,0,0)),
            pl.BlockSpec((1,32,n),lambda w:(w%wins,0,0)),
            pl.BlockSpec((1,n,128),lambda w:(w%wins,0,0)),
        ],
        out_specs=[
            pl.BlockSpec((1,half,n),lambda w:(w,0,0)),
            pl.BlockSpec((1,n,half),lambda w:(w,0,0)),
            pl.BlockSpec((1,PAIR,n,n),lambda w:(w,0,0,0)),
            pl.BlockSpec((1,PAIR,n),lambda w:(w,0,0)),
        ],
        out_shape=[
            jax.ShapeDtypeStruct((nw,half,n),BF),
            jax.ShapeDtypeStruct((nw,n,half),BF),
            jax.ShapeDtypeStruct((nw,PAIR,n,n),BF),
            jax.ShapeDtypeStruct((nw,PAIR,n),F32),
        ],
        scratch_shapes=[pltpu.VMEM((2,n,n),F32)],
        compiler_params=pltpu.CompilerParams(vmem_limit_bytes=VM),
        name="attend", cost_estimate=cost(10),
    )(qT,k,vT,bias,mq,mk)

SPREAD=768
FLAT=1408
WIDE=2816

def spread_ones():
    n=WT*WH*WW
    tok=np.arange(n); c=tok//(WW*WT); e=tok//WT%WW; a=tok%WT
    out=np.zeros((n,SPREAD),np.float32); out[tok,c*104+e*8+a]=1
    return out

def lane16(mirror):
    out=np.zeros((128,256),np.float32)
    for u in range(16):
        for a in range(8):
            out[u*8+a,u*16+(7-a if mirror else a)]=1
    return out

def back_kernel(
    e_ref, k_ref, v_ref, q_ref, g_ref, ctx_ref, r_ref, sp_ref, l16_ref, dq_ref, dk_ref, dv_ref, tab_ref, tot, acc, prob, low
):
    w = pl.program_id(1)
    nw = pl.num_programs(1)
    first = pl.program_id(0) * GROUP
    n = q_ref.shape[2]
    rows = lambda h: slice(h * HEAD_DIM, (h + 1) * HEAD_DIM)

    @pl.when(w == 0)
    def _():
        tot[...] = jnp.zeros_like(tot)

    grads, inner = [], []
    for h in range(GROUP):
        go = g_ref[0, rows(h), :].astype(F32) * r_ref[0, pl.ds(first + h, 1), :]
        inner.append(jnp.sum(go * ctx_ref[0, rows(h), :].astype(F32), axis=0, keepdims=True))
        grads.append(placed(go.astype(BF), h * HEAD_DIM, 128))

    def prob_grad(h):
        prob[h % 2] = nn(v_ref[0], grads[h])

    dq, dk, dv = [], [], []

    def score_side(h):
        dk.append(nt(low[h % 2], placed(q_ref[0, rows(h), :], h * HEAD_DIM, 128)))
        dq.append(nn(k_ref[0, rows(h), :], low[h % 2]) * SCALE)

    def fold(h):
        x = nn(tot[h].astype(BF), sp_ref[...])
        full = jnp.zeros((8, FLAT), F32)
        for d in range(WH):
            part = jnp.zeros((8, SPREAD), F32)
            for f in range(WW):
                j = (d * WW + f) * 8
                part = part + (pltpu.roll(x[j : j + 8, :], 8 * (WW - 1 - f), 1) if f < WW - 1 else x[j : j + 8, :])
            broad = jnp.concatenate([part, jnp.zeros((8, FLAT - SPREAD), F32)], axis=1)
            full = full + (pltpu.roll(broad, 104 * (WH - 1 - d), 1) if d < WH - 1 else broad)
        acc[h * 8 : (h + 1) * 8, :] = full

    def sweep(last):
        prob_grad(0)
        for h in range(GROUP):
            ds = e_ref[0, h].astype(F32) * (prob[h % 2] - inner[h])
            low[h % 2] = ds.astype(BF)
            tot[h] += ds
            dv.append(nt(e_ref[0, h], grads[h]))
            if h + 1 < GROUP:
                prob_grad(h + 1)
            score_side(h)
            if last:
                fold(h)
        dq_ref[0] = jnp.transpose(jnp.concatenate(dq, axis=0).astype(BF))
        dv_ref[0] = ((dv[0] + dv[1]) + (dv[2] + dv[3])).astype(BF)
        dk_ref[0] = ((dk[0] + dk[1]) + (dk[2] + dk[3])).astype(BF)
        dq.clear()
        dk.clear()
        dv.clear()

    @pl.when(w < nw - 1)
    def _():
        sweep(False)

    @pl.when(w == nw - 1)
    def _():
        sweep(True)
        a = acc[...]
        hi = a.astype(BF)
        rest = (a - hi.astype(F32)).astype(BF)
        wide = []
        for t in range(FLAT // 128):
            c = slice(t * 128, (t + 1) * 128)
            wide.append(nn(hi[:, c], l16_ref[...]) + nn(rest[:, c], l16_ref[...]))
        y = jnp.concatenate(wide, axis=1)
        for h in range(GROUP):
            z = pltpu.roll(y[h * 8 : (h + 1) * 8, :], 0, 1, stride=1, stride_axis=0)
            tab_ref[0, h : h + 1, :] = jnp.sum(z, axis=0, keepdims=True)


def attend_back(side,e,kT,v,qT,gT,ctxT,r,sp,l16):
    nw,width,n=qT.shape
    feat=pl.BlockSpec((1,128,n),lambda g,w:(w,2*side+g,0))
    tok=pl.BlockSpec((1,n,128),lambda g,w:(w,0,2*side+g))
    own=pl.BlockSpec((1,n,128),lambda g,w:(w,0,g))
    return pl.pallas_call(
        back_kernel,
        grid=(2,nw),
        in_specs=[
            pl.BlockSpec((1,GROUP,n,n),lambda g,w:(w,g,0,0)),
            feat,tok,feat,feat,pl.BlockSpec((1,128,n),lambda g,w:(w,g,0)),
            pl.BlockSpec((1,PAIR,n),lambda g,w:(w,0,0)),
            pl.BlockSpec(sp.shape,lambda g,w:(0,0)),
            pl.BlockSpec(l16.shape,lambda g,w:(0,0)),
        ],
        out_specs=[own,own,own,pl.BlockSpec((1,GROUP,WIDE),lambda g,w:(g,0,0))],
        out_shape=[
            jax.ShapeDtypeStruct((nw,n,256),BF),
            jax.ShapeDtypeStruct((nw,n,256),BF),
            jax.ShapeDtypeStruct((nw,n,256),BF),
            jax.ShapeDtypeStruct((2,GROUP,WIDE),F32),
        ],
        scratch_shapes=[
            pltpu.VMEM((GROUP,n,n),F32),pltpu.VMEM((GROUP*8,FLAT),F32),pltpu.VMEM((2,n,n),F32),pltpu.VMEM((2,n,n),BF),
        ],
        compiler_params=pltpu.CompilerParams(vmem_limit_bytes=VM),
        name="attend_back", cost_estimate=cost(20),
    )(e,kT,v,qT,gT,ctxT,r,sp,l16)

def lane_maps(mirror):
    lane=np.arange(WIDE); pq=lane//16; o=lane%16
    p=pq//13; q=pq%13
    ok=(pq<169)&(o<15)
    if mirror: o=14-o
    A=o>=7; b=np.where(A,14-o,7-o); C=p>=6; d=np.where(C,12-p,6-p); E=q>=6; f=np.where(E,12-q,6-q)
    col=(b*WH+d)*WW+f
    corner=A*4+C*2+E*1
    return np.where(ok,col,-1).astype(np.int32), np.where(ok,corner,-1).astype(np.int32)

CORNER_ROWS=[(a*WH+c)*WW+e for a in (0,WT-1) for c in (0,WH-1) for e in (0,WW-1)]

def prepare_kernel(rel_ref,maps_ref,table_ref,region_ref,order_ref,l8_ref,lab_ref,narrow_ref,mk_ref,mq_ref):
    values=[]
    n=rel_ref.shape[1]
    rel=jnp.concatenate([rel_ref[row:row+1,:] for row in CORNER_ROWS],axis=0)
    hi=(rel>>6).astype(F32).astype(BF); lo=(rel&63).astype(F32).astype(BF)
    both=jnp.concatenate([hi,lo],axis=0)
    corners=lax.broadcasted_iota(jnp.int32,(8,256),0)
    rows=lax.broadcasted_iota(jnp.int32,(n,256),0)
    trow=lax.broadcasted_iota(jnp.int32,(table_ref.shape[1],256),0)
    for t in range(WIDE//256):
        c=slice(t*256,(t+1)*256)
        for version in range(2):
            col=maps_ref[2*version:2*version+1,c]; cor=maps_ref[2*version+1:2*version+2,c]
            m=jnp.where(rows==col,1.0,0.0).astype(BF)
            y=nn(both,m)
            full=y[:8]*64.0+y[8:]
            lab=jnp.sum(jnp.where(corners==cor,full,0.0),axis=0,keepdims=True)
            lab=jnp.where(cor>=0,lab,-1.0).astype(jnp.int32)
            lab_ref[version:version+1,c]=lab
            if version==0:
                hot=jnp.where(trow==lab,1.0,0.0).astype(BF)
                values.append(nn(table_ref[...],hot))
    values=jnp.concatenate(values,axis=1)
    rolled=[]
    for h in range(HEADS):
        line=jnp.broadcast_to(values[h:h+1],(8,WIDE))
        rolled.append(pltpu.roll(line,WIDE-7,1,stride=1,stride_axis=0))
    rolled=jnp.concatenate(rolled,axis=0).astype(BF)
    for t in range(FLAT//128):
        narrow_ref[:,t*128:(t+1)*128]=nn(rolled[:,t*256:(t+1)*256],l8_ref[...])
    wins=region_ref.shape[0]
    region=jnp.concatenate([region_ref[...].astype(F32),jnp.zeros((16-wins,n),F32)],axis=0).astype(BF)
    across=nt(region,order_ref[...])
    down=nt(order_ref[...],region)
    lanes=lax.broadcasted_iota(jnp.int32,(n,128),1).astype(F32)
    subs=lax.broadcasted_iota(jnp.int32,(32,n),0).astype(F32)
    for w in range(wins):
        mk_ref[w]=jnp.where(down[:,w:w+1]==lanes,1.0,0.0).astype(BF)
        mq_ref[w]=jnp.where(across[w:w+1,:]==subs,0.0,BIG).astype(BF)

def prepare(rel_index,maps,table_t,region_ids,order,l8):
    wins,n=region_ids.shape
    return pl.pallas_call(
        prepare_kernel,
        out_shape=[
            jax.ShapeDtypeStruct((2,WIDE),jnp.int32),
            jax.ShapeDtypeStruct((HEADS*8,FLAT),F32),
            jax.ShapeDtypeStruct((wins,n,128),BF),
            jax.ShapeDtypeStruct((wins,32,n),BF),
        ],
        compiler_params=pltpu.CompilerParams(vmem_limit_bytes=VM),
        name="prepare", cost_estimate=cost(6),
    )(rel_index,maps,table_t,region_ids,order,l8)

def spread_spots():
    place = np.arange(WIN_TOK)
    lane = place // (WW * WT) * 104 + place // WT % WW * 8 + place % WT + 8 * (WW - 1)
    return np.broadcast_to(lane[:, None], (WIN_TOK, 128)).astype(np.int32)


def bias_kernel(narrow_ref, spot_ref, bias_ref, held):
    heads, n, _ = bias_ref.shape
    rows = []
    for h in range(heads):
        line = narrow_ref[8 * h : 8 * h + 8, :]
        for d in range(WH):
            rows.append((pltpu.roll(line, FLAT - 104 * (WH - 1 - d), 1) if d < WH - 1 else line)[:, :SPREAD])
    rows = jnp.concatenate(rows, axis=0).astype(BF)
    spots = jnp.concatenate([spot_ref[...]] * (SPREAD // 128), axis=1)
    lanes = lax.broadcasted_iota(jnp.int32, (n, SPREAD), 1)
    for f in range(WW):
        hot = jnp.where(lanes == spots - 8 * f, 1.0, 0.0).astype(BF)
        y = nt(rows, hot)
        for h in range(heads):
            for d in range(WH):
                at = (h * WH + d) * 8
                held[h, (d * WW + f) * 8 : (d * WW + f + 1) * 8, :] = y[at : at + 8, :]
    for h in range(heads):
        bias_ref[h] = held[h].astype(BF)


def bias_half(side, narrow, spots):
    n = spots.shape[0]
    heads = HEADS // 2
    return pl.pallas_call(
        bias_kernel,
        grid=(1,),
        in_specs=[pl.BlockSpec((8 * heads, FLAT), lambda i: (side, 0)), pl.BlockSpec(spots.shape, lambda i: (0, 0))],
        out_specs=pl.BlockSpec((heads, n, n), lambda i: (0, 0, 0)),
        out_shape=jax.ShapeDtypeStruct((heads, n, n), BF),
        scratch_shapes=[pltpu.VMEM((heads, n, n), F32)],
        compiler_params=pltpu.CompilerParams(vmem_limit_bytes=VM),
        name="position_bias", cost_estimate=cost(5),
    )(narrow, spots)


def spill_kernel(lab_ref,g_ref,out_ref):
    g=g_ref[...]
    hi=g.astype(BF); r1=g-hi.astype(F32); mid=r1.astype(BF); lo=(r1-mid.astype(F32)).astype(BF)
    three=jnp.concatenate([hi,mid,lo],axis=0)
    rows=out_ref.shape[1]
    trow=lax.broadcasted_iota(jnp.int32,(rows,256),0)
    tot=jnp.zeros((48,rows),F32)
    for t in range(WIDE//256):
        c=slice(t*256,(t+1)*256)
        hot=jnp.where(trow==lab_ref[1:2,c],1.0,0.0).astype(BF)
        tot=tot+nt(three[:,c],hot)
    out_ref[...]=tot[:16]+tot[16:32]+tot[32:]

def spill(lab,g,rows):
    return pl.pallas_call(
        spill_kernel,
        out_shape=jax.ShapeDtypeStruct((HEADS,rows),F32),
        compiler_params=pltpu.CompilerParams(vmem_limit_bytes=VM),
        name="table_rows", cost_estimate=cost(5),
    )(lab,g)


BLOCK = 32
B_FC1, B_PROJ, GAIN2, BIAS2, B_FC2, GAIN1, BIAS1, B_QV = range(8)
VEC_LANES = {B_FC1: (0, 128), GAIN1: (128, 32), BIAS1: (160, 32), B_QV: (192, 64), B_PROJ: (256, 32), GAIN2: (288, 32), BIAS2: (320, 32), B_FC2: (352, 32)}
VECTOR = 384


def load_weight(own_ref, other_ref, places_ref, held, sem, vecs=None, start=True):
    core = places_ref[64]
    lanes = slice(0, held.shape[2])
    copies = []
    for i in range(16):
        rows = pl.ds(i * BLOCK, BLOCK)
        own = own_ref.at[places_ref[i]]
        copies.append(pltpu.make_async_copy(own.at[:, lanes], held.at[core, rows, :], sem.at[2 * i]))
        copies.append(
            pltpu.make_async_copy(other_ref.at[places_ref[16 + i]].at[:, lanes], held.at[1 - core, rows, :], sem.at[2 * i + 1])
        )
        if vecs is not None:
            copies.append(pltpu.make_async_copy(own.at[0:16, held.shape[2] :], vecs.at[i], sem.at[32 + i]))
    if start:
        for copy in copies:
            copy.start()
    return copies


def await_all(copies):
    for copy in copies:
        copy.wait()


def store_grad(total, places_ref, own_ref, send_ref):
    core = places_ref[64]

    def block(i, carry):
        own_ref[i, :, : total.shape[2]] = total[core, pl.ds(pl.multiple_of(places_ref[32 + i] * BLOCK, BLOCK), BLOCK), :].astype(BF)
        send_ref[i, :, : total.shape[2]] = total[1 - core, pl.ds(pl.multiple_of(places_ref[48 + i] * BLOCK, BLOCK), BLOCK), :].astype(BF)
        return carry

    lax.fori_loop(0, 16, block, 0)


def normalise(values):
    mean = jnp.mean(values, axis=-1, keepdims=True)
    centred = values - mean
    inverse = lax.rsqrt(jnp.mean(centred * centred, axis=-1, keepdims=True) + EPS)
    return centred * inverse, inverse


def project_kernel(
    places_ref, x_ref, own_ref, other_ref, q_ref, kt_ref, vt_ref, k_ref, v_ref, vec_ref, held, loose, sem
):
    @pl.when(pl.program_id(0) == 0)
    def _():
        await_all(load_weight(own_ref, other_ref, places_ref, held, sem, loose))
        rows = [loose[i].astype(F32) for i in range(16)]
        for name, (at, count) in VEC_LANES.items():
            parts = [row[at // 128 : at // 128 + 1, at % 128 : at % 128 + count] for row in rows]
            vec_ref[name : name + 1, : 16 * count] = jnp.concatenate(parts, axis=1)

    width = x_ref.shape[2]
    normed, _ = normalise(x_ref[0].astype(F32))
    first = (normed * vec_ref[GAIN1 : GAIN1 + 1, :width] + vec_ref[BIAS1 : BIAS1 + 1, :width]).astype(BF)
    left, right = nn(first, held[0]), nn(first, held[1])
    half = width // 2
    q = (left[:, :width] + vec_ref[B_QV : B_QV + 1, :width]) * SCALE
    k = jnp.concatenate([left[:, width:], right[:, :half]], axis=1)
    v = right[:, half:] + vec_ref[B_QV : B_QV + 1, width : 2 * width]
    q_ref[0] = jnp.transpose(q.astype(BF))
    kt_ref[0] = jnp.transpose(k.astype(BF))
    vt_ref[0] = jnp.transpose(v.astype(BF))
    k_ref[0] = k.astype(BF)
    v_ref[0] = v.astype(BF)


def project(places, x, own, other, hidden_width):
    nw, n, width = x.shape
    tok = pl.BlockSpec((1, n, width), lambda w, s: (w, 0, 0))
    feat = pl.BlockSpec((1, width, n), lambda w, s: (w, 0, 0))
    anywhere = pl.BlockSpec(memory_space=pl.ANY)
    vecs = (8, hidden_width)
    return pl.pallas_call(
        project_kernel,
        grid_spec=pltpu.PrefetchScalarGridSpec(
            num_scalar_prefetch=1,
            grid=(nw,),
            in_specs=[tok, anywhere, anywhere],
            out_specs=[feat, feat, feat, tok, tok, pl.BlockSpec(vecs, lambda w, s: (0, 0))],
            scratch_shapes=[
                pltpu.VMEM((2, 16 * BLOCK, own.shape[2] - 128), BF),
                pltpu.VMEM((16, 16, 128), BF),
                pltpu.SemaphoreType.DMA((48,)),
            ],
        ),
        out_shape=[jax.ShapeDtypeStruct((nw, width, n), BF)] * 3
        + [jax.ShapeDtypeStruct((nw, n, width), BF)] * 2
        + [jax.ShapeDtypeStruct(vecs, F32)],
        compiler_params=pltpu.CompilerParams(vmem_limit_bytes=VM),
        name="project", cost_estimate=cost(9),
    )(places, x, own, other)


TAIL = (0.254829592, -0.284496736, 1.421413741, -1.453152027, 1.061405429)


def normal_parts(values):
    t = pl.reciprocal(1.0 + (0.3275911 * 0.7071067811865476) * jnp.abs(values), approx=False)
    series = TAIL[4]
    for factor in TAIL[3::-1]:
        series = series * t + factor
    bell = jnp.exp2(values * values * (-0.5 * LOG2E))
    upper = (0.5 * t) * series * bell
    return jnp.where(values >= 0, 1.0 - upper, upper), bell * 0.3989422804014327


def column_sums(values):
    return jnp.sum(values, axis=0, keepdims=True)


def feed_kernel(
    places_ref, x_ref, ctx0_ref, ctx1_ref, og_ref, vec_ref, own_ref, other_ref, out_ref, mid_grad_ref, gt_ref, own_grad_ref,
    send_grad_ref, sums_ref, held, total, wide, thin, projt, sem,
):
    step = pl.program_id(0)

    @pl.when(step == 0)
    def _():
        total[...] = jnp.zeros_like(total)
        sums_ref[...] = jnp.zeros_like(sums_ref)
        await_all(load_weight(own_ref, other_ref, places_ref, held, sem))

    width = x_ref.shape[2]
    half = width // 2

    @pl.when(step == 0)
    def _():
        for j in range(2):
            projt[j] = jnp.transpose(held[j, :, :half].astype(F32)).astype(BF)

    chunk = (held.shape[2] - half) // 2
    vec = lambda row: vec_ref[row : row + 1, :width]
    ctx = (ctx0_ref[0], ctx1_ref[0])
    branch = nt(ctx[0], held[0, :, :half]) + nt(ctx[1], held[1, :, :half])
    mid = x_ref[0].astype(F32) + (branch + vec(B_PROJ))
    normed, inverse = normalise(mid)
    second = normed * vec(GAIN2) + vec(BIAS2)
    second = second.astype(BF)
    second_t = jnp.transpose(second)
    og = og_ref[0]
    og_t = jnp.transpose(og)
    mlp = jnp.zeros(mid.shape, F32)
    second_grad = jnp.zeros(mid.shape, F32)
    piece = chunk // 2
    cuts = []
    for j in range(2):
        for part in range(2):
            at = half + part * piece
            cuts.append((j, slice(at, at + piece), slice(at + chunk, at + chunk + piece), slice(j * chunk + part * piece, j * chunk + (part + 1) * piece)))

    def widen(i):
        j, c1, c2, cols = cuts[i]
        wide[0, i % 2] = nn(second, held[j, :, c1]) + vec_ref[B_FC1 : B_FC1 + 1, cols]
        wide[1, i % 2] = nn(og, held[j, :, c2])

    widen(0)
    for i, (j, c1, c2, cols) in enumerate(cuts):
        hidden = wide[0, i % 2]
        phi_sum, density = normal_parts(hidden)
        thin[0, i % 2] = (hidden * phi_sum).astype(BF)
        hidden_grad = wide[1, i % 2] * (phi_sum + hidden * density)
        sums_ref[0:1, cols] += column_sums(hidden_grad)
        thin[1, i % 2] = hidden_grad.astype(BF)
        if i + 1 < len(cuts):
            widen(i + 1)
        mlp += nt(thin[0, i % 2], held[j, :, c2])
        second_grad += nt(thin[1, i % 2], held[j, :, c1])
        total[j, :, c1] += nn(second_t, thin[1, i % 2])
        total[j, :, c2] += nn(og_t, thin[0, i % 2])
    out_ref[0] = (mid + (mlp + vec(B_FC2))).astype(BF)
    scaled = second_grad * vec(GAIN2)
    inner = jnp.mean(scaled, axis=-1, keepdims=True)
    along = jnp.mean(scaled * normed, axis=-1, keepdims=True)
    og = og.astype(F32)
    mid_grad = og + inverse * (scaled - inner - normed * along)
    mid_grad_ref[0] = mid_grad
    low = mid_grad.astype(BF)
    sums_ref[1:2, :width] += column_sums(mid_grad)
    sums_ref[2:3, :width] += column_sums(second_grad * normed)
    sums_ref[3:4, :width] += column_sums(second_grad)
    sums_ref[4:5, :width] += column_sums(og)
    low_t = jnp.transpose(low)
    for j in range(2):
        total[j, :, :half] += nn(low_t, ctx[j])
        proj = projt[j]
        gt_ref[0, j * half : (j + 1) * half, :] = nn(proj, low_t).astype(BF)

    @pl.when(step == pl.num_programs(0) - 1)
    def _():
        store_grad(total, places_ref, own_grad_ref, send_grad_ref)


def feed(places, x, ctx0, ctx1, og, vecs, own, other):
    nw, n, width = x.shape
    tok = pl.BlockSpec((1, n, width), lambda w, s: (w, 0, 0))
    feat = pl.BlockSpec((1, width, n), lambda w, s: (w, 0, 0))
    whole = pl.BlockSpec(own.shape, lambda w, s: (0, 0, 0))
    anywhere = pl.BlockSpec(memory_space=pl.ANY)
    side = pl.BlockSpec((1, n, width // 2), lambda w, s: (w, 0, 0))
    hidden_width = own.shape[2] - width // 2
    return pl.pallas_call(
        feed_kernel,
        grid_spec=pltpu.PrefetchScalarGridSpec(
            num_scalar_prefetch=1,
            grid=(nw,),
            in_specs=[tok, side, side, tok, pl.BlockSpec(vecs.shape, lambda w, s: (0, 0)), anywhere, anywhere],
            out_specs=[tok, tok, feat, whole, whole, pl.BlockSpec((8, hidden_width), lambda w, s: (0, 0))],
            scratch_shapes=[
                pltpu.VMEM((2, 16 * BLOCK, own.shape[2]), BF),
                pltpu.VMEM((2, 16 * BLOCK, own.shape[2]), F32),
                pltpu.VMEM((2, 2, n, hidden_width // 4), F32),
                pltpu.VMEM((2, 2, n, hidden_width // 4), BF),
                pltpu.VMEM((2, width // 2, 16 * BLOCK), BF),
                pltpu.SemaphoreType.DMA((32,)),
            ],
        ),
        out_shape=[
            jax.ShapeDtypeStruct((nw, n, width), BF),
            jax.ShapeDtypeStruct((nw, n, width), F32),
            jax.ShapeDtypeStruct((nw, width, n), BF),
            jax.ShapeDtypeStruct(own.shape, BF),
            jax.ShapeDtypeStruct(own.shape, BF),
            jax.ShapeDtypeStruct((8, hidden_width), F32),
        ],
        compiler_params=pltpu.CompilerParams(vmem_limit_bytes=VM),
        name="feed_forward", cost_estimate=cost(44),
    )(places, x, ctx0, ctx1, og, vecs, own, other)


def input_kernel(
    places_ref, x_ref, dq0, dk0, dv0, dq1, dk1, dv1, mid_grad_ref, vec_ref, fc_sums_ref,
    own_ref, other_ref, out_ref, own_grad_ref, send_grad_ref, held, total, sums, small, sem,
):
    step = pl.program_id(0)

    @pl.when(step == 0)
    def _():
        total[...] = jnp.zeros_like(total)
        sums[...] = jnp.zeros_like(sums)
        load_weight(own_ref, other_ref, places_ref, held, sem)

    width = x_ref.shape[2]
    half = width // 2
    vec = lambda row: vec_ref[row : row + 1, :width]
    normed, inverse = normalise(x_ref[0].astype(F32))
    first_t = jnp.transpose((normed * vec(GAIN1) + vec(BIAS1)).astype(BF))
    left = jnp.concatenate([dq0[0], dq1[0], dk0[0]], axis=1)
    right = jnp.concatenate([dk1[0], dv0[0], dv1[0]], axis=1)
    total[0] += nn(first_t, left)
    total[1] += nn(first_t, right)

    @pl.when(step == 0)
    def _():
        await_all(load_weight(own_ref, other_ref, places_ref, held, sem, start=False))

    first_grad = (nt(left, held[0]) + nt(right, held[1])).astype(BF).astype(F32)
    scaled = first_grad * vec(GAIN1)
    inner = jnp.mean(scaled, axis=-1, keepdims=True)
    along = jnp.mean(scaled * normed, axis=-1, keepdims=True)
    out_ref[0] = (mid_grad_ref[0] + inverse * (scaled - inner - normed * along)).astype(BF)
    sums[0:1, :width] += column_sums(first_grad * normed)
    sums[1:2, :width] += column_sums(first_grad)
    sums[2:3, :width] += column_sums(left[:, :width].astype(F32))
    sums[2:3, width:] += column_sums(right[:, half:].astype(F32))

    @pl.when(step == pl.num_programs(0) - 1)
    def _():
        columns = total.shape[2]
        store_grad(total, places_ref, own_grad_ref, send_grad_ref)
        rows = {
            B_FC1: fc_sums_ref[0:1, :], B_PROJ: fc_sums_ref[1:2, :], GAIN2: fc_sums_ref[2:3, :], BIAS2: fc_sums_ref[3:4, :],
            B_FC2: fc_sums_ref[4:5, :], GAIN1: sums[0:1, :], BIAS1: sums[1:2, :], B_QV: sums[2:3, :],
        }
        for i in range(16):
            parts = [rows[name][:, i * count : (i + 1) * count] for name, (_, count) in VEC_LANES.items()]
            line = jnp.concatenate(parts, axis=1)
            small[i] = jnp.concatenate([line[:, :128], line[:, 128:256], line[:, 256:], jnp.zeros((BLOCK - 3, 128), F32)], axis=0)

        def block(i, carry):
            own_grad_ref[i, :, columns:] = small[places_ref[32 + i]].astype(BF)
            send_grad_ref[i, :, columns:] = small[places_ref[48 + i]].astype(BF)
            return carry

        lax.fori_loop(0, 16, block, 0)


def input_side(places, x, groups, mid_grad, vecs, fc_sums, own, other):
    nw, n, width = x.shape
    tok = pl.BlockSpec((1, n, width), lambda w, s: (w, 0, 0))
    part = pl.BlockSpec((1, n, width // 2), lambda w, s: (w, 0, 0))
    flat = lambda shape: pl.BlockSpec(shape, lambda w, s: (0,) * len(shape))
    anywhere = pl.BlockSpec(memory_space=pl.ANY)
    columns = own.shape[2] - 128
    grad = own.shape
    return pl.pallas_call(
        input_kernel,
        grid_spec=pltpu.PrefetchScalarGridSpec(
            num_scalar_prefetch=1,
            grid=(nw,),
            in_specs=[tok] + [part] * 6 + [tok, flat(vecs.shape), flat(fc_sums.shape), anywhere, anywhere],
            out_specs=[tok, flat(grad), flat(grad)],
            scratch_shapes=[
                pltpu.VMEM((2, 16 * BLOCK, columns), BF),
                pltpu.VMEM((2, 16 * BLOCK, columns), F32),
                pltpu.VMEM((8, 2 * width), F32),
                pltpu.VMEM((16, BLOCK, 128), F32),
                pltpu.SemaphoreType.DMA((32,)),
            ],
        ),
        out_shape=[
            jax.ShapeDtypeStruct((nw, n, width), BF),
            jax.ShapeDtypeStruct(grad, BF),
            jax.ShapeDtypeStruct(grad, BF),
        ],
        compiler_params=pltpu.CompilerParams(vmem_limit_bytes=VM),
        name="input_side", cost_estimate=cost(15),
    )(places, x, *[part for group in groups for part in group[:3]], mid_grad, vecs, fc_sums, own, other)


def from_partner(shard, axis, stride):
    return lax.ppermute(shard, axis, [(i, i ^ 1 << stride) for i in range(lax.axis_size(axis))])


def to_block(windows, local_count):
    clip_count, chans = (windows.shape[0], windows.shape[-1])
    parted = windows.reshape(
        clip_count, local_count[0], local_count[1], local_count[2], WT, WH, WW, chans
    )
    parted = parted.transpose(0, 1, 4, 2, 5, 3, 6, 7)
    return parted.reshape(
        clip_count, local_count[0] * WT, local_count[1] * WH, local_count[2] * WW, chans
    )


def from_block(block, local_count):
    clip_count, chans = (block.shape[0], block.shape[-1])
    parted = block.reshape(
        clip_count, local_count[0], WT, local_count[1], WH, local_count[2], WW, chans
    )
    parted = parted.transpose(0, 1, 3, 5, 2, 4, 6, 7)
    return parted.reshape(clip_count, -1, WT * WH * WW, chans)


def roll_ahead(windows, local_count, bit_list):
    block = to_block(windows, local_count)
    for grid_dim, amount, bit_pos in (
        (1, WT // 2, bit_list[0]),
        (2, WH // 2, bit_list[1]),
        (3, WW // 2, bit_list[2]),
    ):
        if bit_pos < 0:
            block = jnp.roll(block, -amount, axis=grid_dim)
        else:
            front = lax.slice_in_dim(block, 0, amount, axis=grid_dim)
            arrived = from_partner(front, "seq", bit_pos)
            rest = lax.slice_in_dim(block, amount, block.shape[grid_dim], axis=grid_dim)
            block = jnp.concatenate([rest, arrived], axis=grid_dim)
    return from_block(block, local_count)


def roll_behind(windows, local_count, bit_list):
    block = to_block(windows, local_count)
    for grid_dim, amount, bit_pos in (
        (1, WT // 2, bit_list[0]),
        (2, WH // 2, bit_list[1]),
        (3, WW // 2, bit_list[2]),
    ):
        if bit_pos < 0:
            block = jnp.roll(block, amount, axis=grid_dim)
        else:
            extent = block.shape[grid_dim]
            trailing = lax.slice_in_dim(block, extent - amount, extent, axis=grid_dim)
            arrived = from_partner(trailing, "seq", bit_pos)
            rest = lax.slice_in_dim(block, 0, extent - amount, axis=grid_dim)
            block = jnp.concatenate([arrived, rest], axis=grid_dim)
    return from_block(block, local_count)


KEEP = WT // 2 * WH * WW


def hwt_order():
    place = np.arange(WIN_TOK)
    return (place % WT * WH + place // (WW * WT)) * WW + place // WT % WW


def order_ones(shift):
    place = np.arange(WIN_TOK)
    out = np.zeros((WIN_TOK, WIN_TOK), np.float32)
    out[place, ((place + shift) % WT * WH + place // (WW * WT)) * WW + place // WT % WW] = 1
    return out


def tile_runs(win):
    runs = []
    for c in range(WH):
        h = (win // 2 * WH + c + WH // 2) % (2 * WH)
        for e, count in ((0, WW - WW // 2), (WW - WW // 2, WW // 2)):
            w = (win % 2 * WW + e + WW // 2) % (2 * WW)
            runs.append((h // WH * 2 + w // WW, h % WH * WW + w % WW, count))
    return runs


def swap_cores(part):
    return lax.ppermute(part, "seq", [(0, 1), (1, 0)])


def enter_kernel(own_ref, arrived_ref, order_ref, out_ref, held):
    _, n, width = own_ref.shape
    rows = lax.broadcasted_iota(jnp.int32, (n, width), 0)
    for source in range(4):
        values = jnp.where(rows >= KEEP, own_ref[source].astype(F32), arrived_ref[source].astype(F32)).astype(BF)
        held[source] = nn(order_ref[...], values)
    for win in range(4):
        parts = [held[source, 8 * at : 8 * (at + count), :] for source, at, count in tile_runs(win)]
        out_ref[win] = jnp.concatenate(parts, axis=0).astype(BF)


def leave_kernel(rows_ref, order_ref, out_ref, send_ref, held):
    for win in range(4):
        values = rows_ref[win].astype(F32)
        start = 0
        for source, at, count in tile_runs(win):
            held[source, 8 * at : 8 * (at + count), :] = values[8 * start : 8 * (start + count), :]
            start += count
    for source in range(4):
        values = nn(order_ref[...], held[source].astype(BF)).astype(out_ref.dtype)
        out_ref[source] = values
        send_ref[source] = values[: send_ref.shape[1]].astype(BF)


SENT = 208


def enter(windows, plan, arrived=None):
    clips, wins, toks, width = windows.shape
    if plan["levels"] == 1 and clips == 1:
        own = windows.reshape(wins, toks, width)
        block = (wins, toks, width // 2)
        part = pl.BlockSpec(block, lambda i: (0, 0, i))
        return pl.pallas_call(
            enter_kernel,
            grid=(2,),
            in_specs=[part, part, pl.BlockSpec((toks, toks), lambda i: (0, 0))],
            out_specs=part,
            out_shape=jax.ShapeDtypeStruct(own.shape, BF),
            scratch_shapes=[pltpu.VMEM(block, F32)],
            compiler_params=pltpu.CompilerParams(vmem_limit_bytes=VM),
            name="enter", cost_estimate=cost(4),
        )(own, arrived.reshape(own.shape), plan["order"])
    rolled = roll_ahead(windows, plan["local"], plan["bits"])
    rolled = rolled.reshape(clips * wins, WT, WH * WW, width).transpose(0, 2, 1, 3)
    return rolled.reshape(clips * wins, toks, width)


def leave(windows, plan, kind):
    wins, toks, width = windows.shape
    block = (wins, toks, width // 2)
    part = pl.BlockSpec(block, lambda i: (0, 0, i))
    return pl.pallas_call(
        leave_kernel,
        grid=(2,),
        in_specs=[part, pl.BlockSpec((toks, toks), lambda i: (0, 0))],
        out_specs=[part, pl.BlockSpec((wins, SENT, width // 2), lambda i: (0, 0, i))],
        out_shape=[jax.ShapeDtypeStruct(windows.shape, kind), jax.ShapeDtypeStruct((wins, SENT, width), BF)],
        scratch_shapes=[pltpu.VMEM(block, F32)],
        compiler_params=pltpu.CompilerParams(vmem_limit_bytes=VM),
        name="leave", cost_estimate=cost(4),
    )(windows, plan["order"].T)


def joined(kept, arrived):
    arrived = jnp.pad(arrived.astype(kept.dtype), ((0, 0), (0, kept.shape[1] - SENT), (0, 0)))
    rows = lax.broadcasted_iota(jnp.int32, kept.shape, 1)
    return jnp.where(rows < KEEP, arrived, kept)[None]


def leave_any(windows, plan, clips, kind):
    count, toks, width = windows.shape
    wins = count // clips
    if plan["levels"] == 1 and clips == 1:
        kept, sent = leave(windows, plan, kind)
        return joined(kept, swap_cores(sent))
    rows = windows.reshape(count, WH * WW, WT, width).transpose(0, 2, 1, 3)
    return roll_behind(rows.reshape(clips, wins, toks, width), plan["local"], plan["bits"]).astype(kind)


def pack_kernel(core_ref, qkv_ref, proj_ref, fc1_ref, fc2_ref, *rest):
    vec_refs, (qkv_out, fc_out) = rest[:-2], rest[-2:]

    def emit(side):
        half = qkv_ref.shape[1] // 2
        qkv_out[:, :half] = qkv_ref[:, side * half : (side + 1) * half]
        at = 0
        for ref in (proj_ref, fc1_ref, fc2_ref):
            half = ref.shape[1] // 2
            fc_out[:, at : at + half] = ref[:, side * half : (side + 1) * half]
            at += half

    half = qkv_ref.shape[1] // 2
    line = jnp.concatenate([ref[...].astype(F32).reshape(1, -1) for ref in vec_refs], axis=1)
    lines = [line[:, at : at + 128] for at in range(0, VECTOR, 128)]
    qkv_out[:, half:] = jnp.concatenate(lines + [jnp.zeros((BLOCK - len(lines), 128), F32)], axis=0).astype(BF)
    for side in range(2):
        @pl.when(core_ref[0] == side)
        def _():
            emit(side)


def pack(core, qkv, proj_t, fc1, fc2_t, vectors):
    columns = (proj_t.shape[1] + fc1.shape[1] + fc2_t.shape[1]) // 2
    vmem = pl.BlockSpec(memory_space=pltpu.VMEM)
    return pl.pallas_call(
        pack_kernel,
        in_specs=[pl.BlockSpec(memory_space=pltpu.SMEM)] + [vmem] * (4 + len(vectors)),
        out_shape=[
            jax.ShapeDtypeStruct((BLOCK, qkv.shape[1] // 2 + 128), BF),
            jax.ShapeDtypeStruct((BLOCK, columns), BF),
        ],
        compiler_params=pltpu.CompilerParams(vmem_limit_bytes=VM),
        name="pack", cost_estimate=cost(2),
    )(core, qkv, proj_t, fc1, fc2_t, *vectors)


def hop(part, flips):
    pairs = [(16 * c + s, 16 * c + (s ^ flips[c])) for c in range(2) for s in range(16)]
    return lax.ppermute(part, ("seq", "shard"), pairs)


def tree_places():
    me = lax.axis_index("shard")
    core = lax.axis_index("seq")
    entry = jnp.arange(16, dtype=jnp.int32)
    v, u, z = entry // 8, entry // 4 % 2, entry % 4
    straight, crossed = me ^ (4 * z + 2 * u + v), me ^ (4 * z + 2 * v + u)
    rel = me ^ entry
    z, y, x = rel // 4, rel // 2 % 2, rel % 2
    place_straight, place_crossed = x * 8 + y * 4 + z, y * 8 + x * 4 + z
    even = core == 0
    pick_core = lambda left, right: jnp.where(even, left, right)
    return jnp.concatenate(
        [
            pick_core(place_straight, place_crossed),
            pick_core(place_crossed, place_straight),
            pick_core(straight, crossed),
            pick_core(crossed, straight),
            jnp.broadcast_to(core, (1,)),
        ]
    ).astype(jnp.int32)


def tree_gather(part):
    arrived = yield [hop(part, (4 * k, 4 * k)) for k in range(1, 4)]
    stack = jnp.stack([part] + arrived)
    arrived = yield hop(stack, (2, 1))
    stack = jnp.concatenate([stack, arrived])
    arrived = yield hop(stack, (1, 2))
    stack = jnp.concatenate([stack, arrived])
    other = yield swap_cores(stack)
    yield stack, other


def tie(*items):
    return lax.optimization_barrier(items)


def add_low(left, right):
    return (left.astype(F32) + right.astype(F32)).astype(BF)


def tree_scatter(own, send):
    arrived = yield swap_cores(send)
    stack = add_low(own, arrived)
    arrived = yield hop(stack[8:], (1, 2))
    stack = add_low(stack[:8], arrived)
    arrived = yield hop(stack[4:], (2, 1))
    stack = add_low(stack[:4], arrived)
    arrived = yield [hop(stack[k], (4 * k, 4 * k)) for k in range(1, 4)]
    arrived = [part.astype(F32) for part in arrived]
    yield (stack[0].astype(F32) + arrived[0]) + (arrived[1] + arrived[2])


def finish(steps, pending):
    while True:
        try:
            pending = steps.send(pending)
        except StopIteration:
            return pending


def table_sum(table):
    for axis, flip in (("seq", 1), ("shard", 1), ("shard", 2)):
        pairs = [(i, i ^ flip) for i in range(2 if axis == "seq" else 16)]
        arrived = yield lax.ppermute(table, axis, pairs)
        table = add_low(table, arrived)
    arrived = yield [hop(table, (4 * k, 4 * k)) for k in range(1, 4)]
    arrived = [part.astype(F32) for part in arrived]
    yield (table.astype(F32) + arrived[0]) + (arrived[1] + arrived[2])


def sides(part, other, core):
    other = other.astype(F32)
    return [jnp.where(core == 0, part, other), jnp.where(core == 0, other, part)]


def body(
    tokens, norm1_gain, norm1_bias, qkv_weight, qv_bias, position_table, proj_weight, proj_bias, norm2_gain,
    norm2_bias, fc1_weight, fc1_bias, fc2_weight, fc2_bias, rel_index, region_ids, cotangent,
):
    levels = lax.axis_size("seq").bit_length() - 1
    clips, wins, toks, width = tokens.shape
    hidden_width = fc1_weight.shape[1]
    plan = {
        "levels": levels,
        "local": [1 if levels > level_pos else 2 for level_pos in range(3)],
        "bits": [levels - 1 - level_pos for level_pos in range(3)],
        "order": jnp.asarray(order_ones(WT // 2), BF),
    }

    def fc_outputs(pair):
        cut = (width // 2, (width + hidden_width) // 2)
        return [jnp.concatenate(two, axis=1) for two in zip(*(jnp.split(part, cut, axis=1) for part in pair))]

    vectors = [fc1_bias, norm1_gain, norm1_bias, qv_bias, proj_bias, norm2_gain, norm2_bias, fc2_bias]
    sizes = [part.shape[0] for part in vectors]
    spread = jnp.asarray(spread_ones(), BF)
    spots = jnp.asarray(spread_spots())
    wide8 = jnp.asarray(lane16(False).T, BF)
    wide16 = jnp.asarray(lane16(True), BF)
    maps = jnp.asarray(np.stack(lane_maps(False) + lane_maps(True)))
    table = prepare(rel_index, maps, position_table.T, region_ids, jnp.asarray(order_ones(0), BF), wide8)
    if clips == 1 and lax.axis_size("shard") == 16 and lax.axis_size("seq") == 2:
        core = lax.axis_index("seq")
        places = tree_places()
        qkv_part, fc_part = pack(
            jnp.reshape(core, (1,)), qkv_weight, proj_weight.T, fc1_weight, fc2_weight.T, vectors
        )
        qkv_steps, fc_steps = tree_gather(qkv_part), tree_gather(fc_part)
        qkv_hop = next(qkv_steps)
        arrived = swap_cores(tokens)
        table, qkv_hop, arrived = tie(table, qkv_hop, arrived)
        labels, narrow, mask_keys, mask_queries = table
        qkv_hop = qkv_steps.send(qkv_hop)
        shifted = enter(tokens, plan, arrived)
        qkv_hop, shifted, narrow, fc_part = tie(qkv_hop, shifted, narrow, fc_part)
        qkv_hop = qkv_steps.send(qkv_hop)
        fc_hop = next(fc_steps)
        bias_low = bias_half(0, narrow, spots)
        arrived = swap_cores(cotangent)
        qkv_hop, bias_low, arrived, narrow = tie(qkv_hop, bias_low, arrived, narrow)
        qkv_hop = qkv_steps.send(qkv_hop)
        out_grad = enter(cotangent, plan, arrived)
        qkv_hop, out_grad, fc_hop = tie(qkv_hop, out_grad, fc_hop)
        qkv_own, qkv_other = qkv_steps.send(qkv_hop)
        fc_hop = fc_steps.send(fc_hop)
        q_t, k_t, v_t, token_k, token_v, vecs = project(places, shifted, qkv_own, qkv_other, hidden_width)
        q_t, fc_hop = tie(q_t, fc_hop)
        fc_hop = fc_steps.send(fc_hop)
        low = attend(0, q_t, token_k, v_t, bias_low, mask_queries, mask_keys)
        narrow, low = tie(narrow, low)
        bias_high = bias_half(1, narrow, spots)
        q_t, low, fc_hop, bias_high = tie(q_t, low, fc_hop, bias_high)
        fc_hop = fc_steps.send(fc_hop)
        high = attend(1, q_t, token_k, v_t, bias_high, mask_queries, mask_keys)
        high, fc_hop = tie(high, fc_hop)
        fc_own, fc_other = fc_steps.send(fc_hop)
        block_out, mid_grad, context_grad_t, fc_keep, fc_send, fc_sums = feed(
            places, shifted, low[1], high[1], out_grad, vecs, fc_own, fc_other
        )
        fc_steps = tree_scatter(fc_keep, fc_send)
        fc_hop = next(fc_steps)
        groups = []
        for side, (context_t, _, expo, inverse_sum) in enumerate((low, high)):
            group = attend_back(
                side, expo, k_t, token_v, q_t, context_grad_t, context_t, inverse_sum, spread, wide16
            )
            group, fc_hop, context_grad_t, block_out = tie(group, fc_hop, context_grad_t, block_out)
            groups.append(group)
            fc_hop = fc_steps.send(fc_hop)
        offsets = jnp.concatenate([group[3] for group in groups]).reshape(HEADS, WIDE)
        table_steps = table_sum(offsets.astype(BF))
        table_hop = next(table_steps)
        input_grad, qkv_keep, qkv_send = input_side(
            places, shifted, groups, mid_grad, vecs, fc_sums, qkv_own, qkv_other
        )
        input_grad, qkv_send, fc_hop, table_hop, block_out = tie(input_grad, qkv_send, fc_hop, table_hop, block_out)
        qkv_steps = tree_scatter(qkv_keep, qkv_send)
        qkv_hop = next(qkv_steps)
        fc_hop = fc_steps.send(fc_hop)
        table_hop = table_steps.send(table_hop)
        kept, sent = leave(input_grad, plan, F32)
        qkv_hop, table_hop, kept, sent, block_out = tie(qkv_hop, table_hop, kept, sent, block_out)
        qkv_hop = qkv_steps.send(qkv_hop)
        table_hop = table_steps.send(table_hop)
        arrived = swap_cores(sent)
        out_kept, out_sent = leave(block_out, plan, BF)
        qkv_hop, table_hop, fc_hop, arrived, out_kept, out_sent = tie(qkv_hop, table_hop, fc_hop, arrived, out_kept, out_sent)
        qkv_hop = qkv_steps.send(qkv_hop)
        table_hop = table_steps.send(table_hop)
        own_fc = finish(fc_steps, fc_hop)
        out_arrived = swap_cores(out_sent)
        fc_swap = swap_cores(own_fc.astype(BF))
        input_grad = joined(kept, arrived)
        qkv_hop, table_hop, input_grad, fc_swap, out_arrived = tie(qkv_hop, table_hop, input_grad, fc_swap, out_arrived)
        qkv_hop = qkv_steps.send(qkv_hop)
        offsets = finish(table_steps, table_hop)
        block_out = joined(out_kept, out_arrived)
        own_fc = fc_outputs(sides(own_fc, fc_swap, core))
        table_grad = spill(labels, offsets, position_table.shape[0])
        qkv_hop, block_out, own_fc, table_grad = tie(qkv_hop, block_out, own_fc, table_grad)
        own_qkv = finish(qkv_steps, qkv_hop)
        small = own_qkv[: VECTOR // 128, width * 3 // 2 :].reshape(-1)
        own_qkv = own_qkv[:, : width * 3 // 2]
        own_qkv = sides(own_qkv, swap_cores(own_qkv.astype(BF)), core)
    else:
        straight = np.arange(16)
        places = jnp.asarray(np.concatenate([straight, straight, straight, straight, np.zeros(1)]), jnp.int32)
        gather = lambda part: lax.all_gather(part, "shard", axis=0, tiled=True)
        halves = lambda part: jnp.split(part, 2, axis=1)
        parts = [halves(gather(part)) for part in (proj_weight.T, fc1_weight, fc2_weight.T)]
        fc_own, fc_other = (jnp.concatenate(pair, axis=1).reshape(16, BLOCK, -1) for pair in zip(*parts))
        rows = lax.all_gather(jnp.concatenate(vectors), "shard", axis=0, tiled=False)
        pieces = [piece.reshape(16, -1) for piece in jnp.split(rows, np.cumsum(sizes)[:-1], axis=1)]
        rows = jnp.pad(jnp.concatenate(pieces, axis=1).reshape(16, -1, 128), ((0, 0), (0, BLOCK - VECTOR // 128), (0, 0)))
        qkv_own, qkv_other = (
            jnp.concatenate([part.reshape(16, BLOCK, -1), rows], axis=2) for part in halves(gather(qkv_weight))
        )
        shifted = enter(tokens, plan, swap_cores(tokens) if levels == 1 else None)
        out_grad = enter(cotangent, plan, swap_cores(cotangent) if levels == 1 else None)
        labels, narrow, mask_keys, mask_queries = table
        bias_low, bias_high = (bias_half(side, narrow, spots) for side in range(2))
        q_t, k_t, v_t, token_k, token_v, vecs = project(places, shifted, qkv_own, qkv_other, hidden_width)
        low = attend(0, q_t, token_k, v_t, bias_low, mask_queries, mask_keys)
        high = attend(1, q_t, token_k, v_t, bias_high, mask_queries, mask_keys)
        block_out, mid_grad, context_grad_t, fc_keep, fc_send, fc_sums = feed(
            places, shifted, low[1], high[1], out_grad, vecs, fc_own, fc_other
        )
        groups = [
            attend_back(side, expo, k_t, token_v, q_t, context_grad_t, context_t, inverse_sum, spread, wide16)
            for side, (context_t, _, expo, inverse_sum) in enumerate((low, high))
        ]
        input_grad, qkv_keep, qkv_send = input_side(
            places, shifted, groups, mid_grad, vecs, fc_sums, qkv_own, qkv_other
        )
        block_out = leave_any(block_out, plan, clips, BF)
        input_grad = leave_any(input_grad, plan, clips, F32)
        offsets = jnp.concatenate([group[3] for group in groups]).reshape(HEADS, WIDE)
        table_grad = spill(labels, lax.psum(offsets, ("seq", "shard")), position_table.shape[0])
        small = qkv_keep[:, : VECTOR // 128, width * 3 // 2 :].reshape(16, VECTOR)
        small = lax.psum(small.astype(F32), ("seq", "shard"))
        pieces = jnp.split(small, np.cumsum([count for _, count in VEC_LANES.values()])[:-1], axis=1)
        shards = lax.axis_size("shard")
        small = jnp.concatenate([piece.reshape(shards, -1) for piece in pieces], axis=1)
        small = lax.dynamic_index_in_dim(small, lax.axis_index("shard"), 0, keepdims=False)

        def owned(grad):
            grad = lax.psum(grad.reshape(16 * BLOCK, -1), "seq")
            return lax.psum_scatter(grad, "shard", scatter_dimension=0, tiled=True).astype(F32)

        own_fc = fc_outputs([owned(fc_keep), owned(fc_send)])
        own_qkv = [owned(qkv_keep[:, :, : width * 3 // 2]), owned(qkv_send[:, :, : width * 3 // 2])]
    own_proj, own_fc1, own_fc2 = own_fc
    own_qkv = jnp.concatenate(own_qkv, axis=1)
    own_f1b, own_g1, own_b1, own_qv, own_pb, own_g2, own_b2, own_f2b = jnp.split(small, np.cumsum(sizes)[:-1])
    return (
        block_out, input_grad, own_g1, own_b1, own_qkv, own_qv, table_grad.T, own_proj.T, own_pb,
        own_g2, own_b2, own_fc1, own_f1b, own_fc2.T, own_f2b,
    )


def solution(mesh):
    return jax.shard_map(
        body,
        mesh=mesh,
        in_specs=(
            P("shard", "seq", None, None),
            P("shard"),
            P("shard"),
            P("shard", None),
            P("shard"),
            P(),
            P(None, "shard"),
            P("shard"),
            P("shard"),
            P("shard"),
            P("shard", None),
            P("shard"),
            P(None, "shard"),
            P("shard"),
            P(),
            P("seq", None),
            P("shard", "seq", None, None),
        ),
        out_specs=(
            P("shard", "seq", None, None),
            P("shard", "seq", None, None),
            P("shard"),
            P("shard"),
            P("shard", None),
            P("shard"),
            P(),
            P(None, "shard"),
            P("shard"),
            P("shard"),
            P("shard"),
            P("shard", None),
            P("shard"),
            P(None, "shard"),
            P("shard"),
        ),
        check_vma=False,
    )
```
